128 devices in a mesh: lat: 8 (over x, z_lo), lon: 16 (over z_hi, y, core).
Axes of the slice: x: 4, y: 4, z: 4 (z_hi: 2, z_lo: 2; z = z_hi * 2 + z_lo), core: 2. Of those that a mesh axis runs over, the one named last changes fastest.
Arguments:
- tokens: bfloat16 [192, 384, 2, 512], P('lat', 'lon'), may hold values from -6 to 6
- cotangent: bfloat16 [192, 384, 2, 512], P('lat', 'lon'), may hold values from -6 to 6
- norm_gain: float32 [512], replicated, may hold values from 0.5 to 1.5
- w_qkv: bfloat16 [512, 1536], replicated, may hold values from -0.25 to 0.25
- w_out: bfloat16 [512, 512], replicated, may hold values from -0.25 to 0.25
- mlp_gain: float32 [512], replicated, may hold values from 0.5 to 1.5
- w_up: bfloat16 [512, 2048], replicated, may hold values from -0.25 to 0.25
- w_down: bfloat16 [2048, 512], replicated, may hold values from -0.125 to 0.125
Outputs:
- output: bfloat16 [192, 384, 2, 512], P('lat', 'lon')
- grad_tokens: bfloat16 [192, 384, 2, 512], P('lat', 'lon')
- grad_norm_gain: float32 [512], replicated
- grad_qkv: float32 [512, 1536], replicated
- grad_out: float32 [512, 512], replicated
- grad_mlp_gain: float32 [512], replicated
- grad_up: float32 [512, 2048], replicated
- grad_down: float32 [2048, 512], replicated
The draws below stay inside these ranges and needn't reach their ends.
All inputs are finite; a program needn't handle non-finite values.
Results may differ from the reference program's by a relative error of at most 0.02.
Values may be sent and summed in bfloat16 or wider, within the bound.
No kernel may reach another device: no remote copies, remote signals or barrier semaphores. Data moves between devices by JAX's collectives and lax.ppermute only.
A program may use at most 192 MiB of HBM per device.

```python
import jax
import jax.numpy as jnp
from jax import lax

D = 512
FF = 2048
HD = 64
WLAT = 6
WLON = 12
LEV = 2
LAT_DEV = 24
LON_DEV = 24
NLAT = 192
NLON = 384
N_LAT = 8
N_LON = 16


def shard_levels(stream_key, dims, cuts, least, largest):
    factor_of, own = 1.0, jax.random.fold_in(stream_key, 6)
    for position, blocks in cuts:
        draws = jnp.exp(jax.random.uniform(jax.random.fold_in(own, position), (blocks,), jnp.float32, least / len(cuts), largest / len(cuts)))
        factor_of = factor_of * jnp.repeat(draws, dims[position] // blocks).reshape([-1 if axis == position else 1 for axis in range(len(dims))])
    return factor_of


def noise(key, extent, deviation, most, pieces=(), dtype=jnp.bfloat16):
    factor_of = shard_levels(key, extent, pieces, -0.22, 0.18) if pieces else 1.0
    entries = jax.random.normal(key, extent, jnp.float32) * deviation * factor_of
    return jnp.minimum(jnp.maximum(entries, -most), most).astype(dtype)


def setup_inputs(seed: int = 0) -> dict:
    arg_keys = jax.random.split(jax.random.key(seed), 9)
    return {
        "tokens": noise(arg_keys[0], (NLAT, NLON, LEV, D), 1.0, 6.0, ((0, 8), (1, 16))),
        "cotangent": noise(arg_keys[1], (NLAT, NLON, LEV, D), 1.0, 6.0, ((0, 8), (1, 16))),
        "norm_gain": jnp.clip(1.0 + 0.1 * jax.random.normal(arg_keys[2], (D,), jnp.float32), 0.5, 1.5),
        "w_qkv": noise(arg_keys[3], (D, 3 * D), D ** -0.5, 0.25),
        "w_out": noise(arg_keys[4], (D, D), D ** -0.5, 0.25),
        "mlp_gain": jnp.clip(1.0 + 0.1 * jax.random.normal(arg_keys[5], (D,), jnp.float32), 0.5, 1.5),
        "w_up": noise(arg_keys[6], (D, FF), D ** -0.5, 0.25),
        "w_down": noise(arg_keys[7], (FF, D), FF ** -0.5, 0.125),
    }


def layer_norm(values, gain):
    mean = lax.optimization_barrier(jnp.mean(values, axis=-1, keepdims=True))
    centred = values - mean
    var = lax.optimization_barrier(jnp.mean(centred * centred, axis=-1, keepdims=True))
    return centred * lax.rsqrt(var + 1e-05) * gain

def windows(array):
    rows, cols, levels, width = array.shape
    split = array.reshape(rows // WLAT, WLAT, cols // WLON, WLON, levels, width)
    return split.transpose(0, 2, 1, 3, 4, 5).reshape(-1, WLAT * WLON * levels, width)

def unwindows(array, rows, cols, levels):
    width = array.shape[-1]
    split = array.reshape(rows // WLAT, cols // WLON, WLAT, WLON, levels, width)
    return split.transpose(0, 2, 1, 3, 4, 5).reshape(rows, cols, levels, width)

def block(shifted, norm_gain, w_qkv, w_out, mlp_gain, w_up, w_down, last_band):
    rows, cols, levels, width = shifted.shape
    heads = width // HD
    base = windows(shifted).astype(jnp.float32)
    count, size, _ = base.shape
    normed = layer_norm(base, norm_gain).astype(jnp.bfloat16)
    qkv = jnp.dot(normed.reshape(count * size, width), w_qkv, preferred_element_type=jnp.float32)
    qkv = qkv.astype(jnp.bfloat16).reshape(count, size, 3, heads, HD)
    query = qkv[:, :, 0].astype(jnp.float32)
    keys = qkv[:, :, 1].astype(jnp.float32)
    values = qkv[:, :, 2].astype(jnp.float32)
    scores = jnp.einsum('wqhd,wkhd->whqk', query, keys) * HD ** (-0.5)
    row_ids = lax.broadcasted_iota(jnp.int32, (rows, cols, levels, 1), 0)
    groups = jnp.where(last_band & (row_ids >= rows - WLAT // 2), 1, 0).astype(jnp.int32)
    group_w = windows(groups)[:, :, 0]
    allowed = group_w[:, None, :, None] == group_w[:, None, None, :]
    scores = jnp.where(allowed, scores, -1000000000.0)
    weights = jax.nn.softmax(scores, axis=-1).astype(jnp.bfloat16)
    attended = jnp.einsum('whqk,wkhd->wqhd', weights.astype(jnp.float32), values)
    attended = attended.astype(jnp.bfloat16).reshape(count * size, width)
    projected = jnp.dot(attended, w_out, preferred_element_type=jnp.float32)
    mid = (base + projected.reshape(count, size, width)).astype(jnp.bfloat16)
    mid_f = mid.astype(jnp.float32)
    normed2 = layer_norm(mid_f, mlp_gain).astype(jnp.bfloat16).reshape(count * size, width)
    hidden = jax.nn.gelu(jnp.dot(normed2, w_up, preferred_element_type=jnp.float32), approximate=False)
    down = jnp.dot(hidden.astype(jnp.bfloat16), w_down, preferred_element_type=jnp.float32)
    result = (mid_f + down.reshape(count, size, width)).astype(jnp.bfloat16)
    return unwindows(result, rows, cols, levels)

def to_tiles(array):
    split = array.reshape(N_LAT, LAT_DEV, N_LON, LON_DEV, LEV, D)
    return split.transpose(0, 2, 1, 3, 4, 5).reshape(N_LAT * N_LON, LAT_DEV, LON_DEV, LEV, D)

def from_tiles(array):
    split = array.reshape(N_LAT, N_LON, LAT_DEV, LON_DEV, LEV, D)
    return split.transpose(0, 2, 1, 3, 4, 5).reshape(NLAT, NLON, LEV, D)

def reference(tokens, cotangent, norm_gain, w_qkv, w_out, mlp_gain, w_up, w_down):
    half_lat = WLAT // 2
    half_lon = WLON // 2
    shifted = jnp.roll(tokens, (-half_lat, -half_lon), axis=(0, 1))
    pulled = jnp.roll(cotangent, (-half_lat, -half_lon), axis=(0, 1))
    flags = jnp.arange(N_LAT * N_LON) // N_LON == N_LAT - 1
    params = (norm_gain, w_qkv, w_out, mlp_gain, w_up, w_down)

    def step(carry, item):
        tile, tile_cot, flag = item

        def forward(tile_in, gain1, wqkv, wout, gain2, wup, wdown):
            return block(tile_in, gain1, wqkv, wout, gain2, wup, wdown, flag)
        result, pullback = jax.vjp(forward, tile, *params)
        grads = pullback(tile_cot)
        carry = tuple((total + part.astype(jnp.float32) for total, part in zip(carry, grads[1:])))
        return (carry, (result, grads[0]))
    zeros = tuple((jnp.zeros(p.shape, jnp.float32) for p in params))
    sums, (results, grad_tiles) = lax.scan(step, zeros, (to_tiles(shifted), to_tiles(pulled), flags))
    output = jnp.roll(from_tiles(results), (half_lat, half_lon), axis=(0, 1))
    grad_tokens = jnp.roll(from_tiles(grad_tiles), (half_lat, half_lon), axis=(0, 1))
    return (output, grad_tokens, sums[0], sums[1], sums[2], sums[3], sums[4], sums[5])
```

```python
import functools

import jax
import jax.numpy as jnp
from jax import lax
from jax.experimental import pallas as pl
from jax.experimental.pallas import tpu as pltpu
from jax.sharding import PartitionSpec as P

HD = 64
WLAT = 6
WLON = 12
LEV = 2
WIN = WLAT * WLON * LEV
D = 512
FF = 2048
HALF_LAT = WLAT // 2
HALF_LON = WLON // 2
EPS = 1e-05
F32 = jnp.float32
BF16 = jnp.bfloat16
PAIR = 2 * HD
LIMIT = 56 * 1024 * 1024


def mm(a, b):
    return lax.dot_general(a, b, (((1,), (0,)), ((), ())), preferred_element_type=F32)


def mm_t(a, b):
    return lax.dot_general(a, b, (((1,), (1,)), ((), ())), preferred_element_type=F32)


def t_mm(a, b):
    return lax.dot_general(a, b, (((0,), (0,)), ((), ())), preferred_element_type=F32)


def normalised(values):
    mean = jnp.mean(values, axis=-1, keepdims=True)
    centred = values - mean
    var = jnp.mean(centred * centred, axis=-1, keepdims=True)
    scale = lax.rsqrt(var + EPS)
    return centred * scale, scale


def norm_pullback(xhat, scale, gain, grad):
    dxhat = grad * gain
    m1 = jnp.mean(dxhat, axis=-1, keepdims=True)
    m2 = jnp.mean(dxhat * xhat, axis=-1, keepdims=True)
    return scale * (dxhat - m1 - xhat * m2)


def gelu_parts(x):
    a = jnp.abs(x)
    t = 1.0 / (1.0 + (0.3275911 * 0.7071067811865476) * a)
    e = jnp.exp(-0.5 * x * x)
    poly = t * (0.127414796 + t * (-0.142248368 + t * (0.7107068705 + t * (-0.7265760135 + t * 0.5307027145))))
    tail = poly * e
    cdf = jnp.where(x >= 0.0, 1.0 - tail, tail)
    return cdf, 0.3989422804014327 * e


def front_kernel(flag_ref, x_ref, g1_ref, wqkv_ref, wout_ref, g2_ref,
                 n1_ref, qkv_ref, p_ref, att_ref, mid_ref, n2_ref):
    tokens = x_ref.shape[0]
    count = tokens // WIN
    per_row = count // 4
    gain1 = g1_ref[...]
    gain2 = g2_ref[...]

    @pl.loop(0, count)
    def _(w):
        rows = pl.ds(pl.multiple_of(w * WIN, WIN), WIN)
        xhat, _ = normalised(x_ref[rows, :].astype(F32))
        n1_ref[rows, :] = (xhat * gain1).astype(BF16)

    big = 2 * WIN

    @pl.loop(0, tokens // big)
    def _(b):
        rows = pl.ds(pl.multiple_of(b * big, big), big)
        n1 = n1_ref[rows, :]
        qkv_ref[rows, 0:D] = (mm(n1, wqkv_ref[:, 0:D]).astype(BF16) * 0.125).astype(BF16)
        qkv_ref[rows, D:2 * D] = mm(n1, wqkv_ref[:, D:2 * D]).astype(BF16)
        qkv_ref[rows, 2 * D:3 * D] = mm(n1, wqkv_ref[:, 2 * D:3 * D]).astype(BF16)

    key_group = lax.broadcasted_iota(jnp.int32, (WIN, WIN), 0) >= WIN // 2
    query_group = lax.broadcasted_iota(jnp.int32, (WIN, WIN), 1) >= WIN // 2
    split = key_group != query_group
    low = lax.broadcasted_iota(jnp.int32, (WIN, PAIR), 1) < HD

    @pl.loop(0, count)
    def _(w):
        rows = pl.ds(pl.multiple_of(w * WIN, WIN), WIN)
        cut = jnp.logical_and(flag_ref[0] == 1, w >= count - per_row)
        masked = jnp.logical_and(split, cut)
        for pair in range(D // PAIR):
            lanes = slice(pair * PAIR, (pair + 1) * PAIR)
            q = qkv_ref[rows, pair * PAIR:(pair + 1) * PAIR]
            k = qkv_ref[rows, D + pair * PAIR:D + (pair + 1) * PAIR]
            v = qkv_ref[rows, 2 * D + pair * PAIR:2 * D + (pair + 1) * PAIR]
            outs = []
            for h in range(2):
                mine = low if h == 0 else jnp.logical_not(low)
                kh = jnp.where(mine, k, jnp.zeros_like(k))
                s = mm_t(kh, q)
                s = jnp.where(masked, -1000000000.0, s)
                e = jnp.exp(s - jnp.max(s, axis=0, keepdims=True))
                p = (e * (1.0 / jnp.sum(e, axis=0, keepdims=True))).astype(BF16)
                p_ref[w, 2 * pair + h] = p
                outs.append(t_mm(p, v))
            att_ref[rows, lanes] = jnp.where(low, outs[0], outs[1]).astype(BF16)

    @pl.loop(0, tokens // big)
    def _(b):
        rows = pl.ds(pl.multiple_of(b * big, big), big)
        mid = (x_ref[rows, :].astype(F32) + mm(att_ref[rows, :], wout_ref[...])).astype(BF16)
        mid_ref[rows, :] = mid
        xhat, _ = normalised(mid.astype(F32))
        n2_ref[rows, :] = (xhat * gain2).astype(BF16)


def mlp_kernel(n2_ref, cot_ref, mid_ref, g2_ref, wup_ref, wdown_ref,
               res_ref, dmid_ref, dg2_ref, gup_ref, gdown_ref,
               down_acc, dn2_acc, hid_ref, du_ref):
    step = pl.program_id(0)
    tokens = n2_ref.shape[0]
    big = 2 * WIN

    @pl.when(step == 0)
    def _():
        down_acc[...] = jnp.zeros_like(down_acc)
        dn2_acc[...] = jnp.zeros_like(dn2_acc)

    @pl.loop(0, tokens // big)
    def _(b):
        rows = pl.ds(pl.multiple_of(b * big, big), big)
        up = mm(n2_ref[rows, :], wup_ref[...])
        cdf, pdf = gelu_parts(up)
        hid = (up * cdf).astype(BF16)
        hid_ref[rows, :] = hid
        dhid = mm_t(cot_ref[rows, :], wdown_ref[...]).astype(BF16).astype(F32)
        du = (dhid * (cdf + up * pdf)).astype(BF16)
        du_ref[rows, :] = du
        down_acc[rows, :] += mm(hid, wdown_ref[...])
        dn2_acc[rows, :] += mm_t(du, wup_ref[...])

    gdown_ref[...] = t_mm(hid_ref[...], cot_ref[...]).astype(BF16)
    gup_ref[...] = t_mm(n2_ref[...], du_ref[...]).astype(BF16)

    @pl.when(step == pl.num_programs(0) - 1)
    def _():
        gain2 = g2_ref[...]
        dg2_ref[...] = jnp.zeros_like(dg2_ref)

        @pl.loop(0, tokens // big)
        def _(b):
            rows = pl.ds(pl.multiple_of(b * big, big), big)
            mid = mid_ref[rows, :].astype(F32)
            res_ref[rows, :] = (mid + down_acc[rows, :]).astype(BF16)
            xhat, scale = normalised(mid)
            dn2 = dn2_acc[rows, :].astype(BF16).astype(F32)
            dg2_ref[...] += jnp.sum(dn2 * xhat, axis=0, keepdims=True)
            dmid = cot_ref[rows, :].astype(F32) + norm_pullback(xhat, scale, gain2, dn2)
            dmid_ref[rows, :] = dmid.astype(BF16)


def back_kernel(x_ref, dmid_ref, n1_ref, qkv_ref, p_ref, att_ref, g1_ref, wqkv_ref, wout_ref,
                dx_ref, dg1_ref, gqkv_ref, gout_ref, datt_ref, dqkv_ref):
    tokens = x_ref.shape[0]
    count = tokens // WIN
    gain1 = g1_ref[...]
    big = 2 * WIN

    gout_ref[...] = t_mm(att_ref[...], dmid_ref[...]).astype(BF16)

    @pl.loop(0, tokens // big)
    def _(b):
        rows = pl.ds(pl.multiple_of(b * big, big), big)
        datt_ref[rows, :] = mm_t(dmid_ref[rows, :], wout_ref[...]).astype(BF16)

    low = lax.broadcasted_iota(jnp.int32, (WIN, PAIR), 1) < HD

    @pl.loop(0, count)
    def _(w):
        rows = pl.ds(pl.multiple_of(w * WIN, WIN), WIN)
        for pair in range(D // PAIR):
            lanes = slice(pair * PAIR, (pair + 1) * PAIR)
            q = qkv_ref[rows, pair * PAIR:(pair + 1) * PAIR]
            k = qkv_ref[rows, D + pair * PAIR:D + (pair + 1) * PAIR]
            v = qkv_ref[rows, 2 * D + pair * PAIR:2 * D + (pair + 1) * PAIR]
            da = datt_ref[rows, lanes]
            dqs, dks, dvs = [], [], []
            for h in range(2):
                mine = low if h == 0 else jnp.logical_not(low)
                vh = jnp.where(mine, v, jnp.zeros_like(v))
                p = p_ref[w, 2 * pair + h]
                pf = p.astype(F32)
                dp = mm_t(vh, da).astype(BF16).astype(F32)
                ds = (pf * (dp - jnp.sum(dp * pf, axis=0, keepdims=True))).astype(BF16)
                dvs.append(mm(p, da))
                dks.append(mm(ds, q))
                dqs.append(t_mm(ds, k))
            dqkv_ref[rows, pair * PAIR:(pair + 1) * PAIR] = (jnp.where(low, dqs[0], dqs[1]) * 0.125).astype(BF16)
            dqkv_ref[rows, D + pair * PAIR:D + (pair + 1) * PAIR] = jnp.where(low, dks[0], dks[1]).astype(BF16)
            dqkv_ref[rows, 2 * D + pair * PAIR:2 * D + (pair + 1) * PAIR] = jnp.where(low, dvs[0], dvs[1]).astype(BF16)

    for part in range(3):
        gqkv_ref[:, part * D:(part + 1) * D] = t_mm(n1_ref[...], dqkv_ref[:, part * D:(part + 1) * D]).astype(BF16)

    dg1_ref[...] = jnp.zeros_like(dg1_ref)

    @pl.loop(0, tokens // big)
    def _(b):
        rows = pl.ds(pl.multiple_of(b * big, big), big)
        dn1 = mm_t(dqkv_ref[rows, :], wqkv_ref[...]).astype(BF16).astype(F32)
        xhat, scale = normalised(x_ref[rows, :].astype(F32))
        dg1_ref[...] += jnp.sum(dn1 * xhat, axis=0, keepdims=True)
        dx = dmid_ref[rows, :].astype(F32) + norm_pullback(xhat, scale, gain1, dn1)
        dx_ref[rows, :] = dx.astype(BF16)


def params():
    return pltpu.CompilerParams(vmem_limit_bytes=LIMIT)


def shape(dims, dtype=BF16):
    return jax.ShapeDtypeStruct(dims, dtype)


def front(flag, x, g1, wqkv, wout, g2):
    tokens = x.shape[0]
    count = tokens // WIN
    vm = pl.BlockSpec(memory_space=pltpu.VMEM)
    return pl.pallas_call(
        front_kernel,
        name="front",
        in_specs=[pl.BlockSpec(memory_space=pltpu.SMEM)] + [vm] * 5,
        out_specs=[vm] * 6,
        out_shape=[
            shape((tokens, D)),
            shape((tokens, 3 * D)),
            shape((count, D // HD, WIN, WIN)),
            shape((tokens, D)),
            shape((tokens, D)),
            shape((tokens, D)),
        ],
        compiler_params=params(),
    )(flag, x, g1, wqkv, wout, g2)


def mlp(n2, cot, mid, g2, wup, wdown, chunk=512):
    tokens = n2.shape[0]
    whole = pl.BlockSpec((tokens, D), lambda i: (0, 0))
    gain = pl.BlockSpec((1, D), lambda i: (0, 0))
    cols = pl.BlockSpec((D, chunk), lambda i: (0, i))
    rows = pl.BlockSpec((chunk, D), lambda i: (i, 0))
    return pl.pallas_call(
        mlp_kernel,
        name="mlp",
        grid=(FF // chunk,),
        in_specs=[whole, whole, whole, gain, cols, rows],
        out_specs=[whole, whole, gain, cols, rows],
        out_shape=[
            shape((tokens, D)),
            shape((tokens, D)),
            shape((1, D), F32),
            shape((D, FF)),
            shape((FF, D)),
        ],
        scratch_shapes=[
            pltpu.VMEM((tokens, D), F32),
            pltpu.VMEM((tokens, D), F32),
            pltpu.VMEM((tokens, chunk), BF16),
            pltpu.VMEM((tokens, chunk), BF16),
        ],
        compiler_params=params(),
    )(n2, cot, mid, g2, wup, wdown)


def back(x, dmid, n1, qkv, p, att, g1, wqkv, wout):
    tokens = x.shape[0]
    vm = pl.BlockSpec(memory_space=pltpu.VMEM)
    return pl.pallas_call(
        back_kernel,
        name="back",
        in_specs=[vm] * 9,
        out_specs=[vm] * 4,
        out_shape=[
            shape((tokens, D)),
            shape((1, D), F32),
            shape((D, 3 * D)),
            shape((D, D)),
        ],
        scratch_shapes=[
            pltpu.VMEM((tokens, D), BF16),
            pltpu.VMEM((tokens, 3 * D), BF16),
        ],
        compiler_params=params(),
    )(x, dmid, n1, qkv, p, att, g1, wqkv, wout)


def shifted_2(block, axis, distance):
    devices = range(lax.axis_size(axis))
    route = [((i - distance) % len(devices), i) for i in devices]
    return lax.ppermute(block, axis, route)


def windows(array):
    rows, cols, levels, width = array.shape
    split = array.reshape(rows // WLAT, WLAT, cols // WLON, WLON, levels, width)
    return split.transpose(0, 2, 1, 3, 4, 5).reshape(-1, width)


def unwindows(array, rows, cols, levels):
    width = array.shape[-1]
    split = array.reshape(rows // WLAT, cols // WLON, WLAT, WLON, levels, width)
    return split.transpose(0, 2, 1, 3, 4, 5).reshape(rows, cols, levels, width)


def pull_rims(block):
    rim = shifted_2(block[:HALF_LAT], "lat", -1)
    block = jnp.concatenate([block[HALF_LAT:], rim], axis=0)
    rim = shifted_2(block[:, :HALF_LON], "lon", -1)
    return jnp.concatenate([block[:, HALF_LON:], rim], axis=1)


def push_rims(block):
    tail = shifted_2(block[-HALF_LAT:], "lat", 1)
    moved = jnp.concatenate([tail, block[:-HALF_LAT]], axis=0)
    tail = shifted_2(moved[:, -HALF_LON:], "lon", 1)
    return jnp.concatenate([tail, moved[:, :-HALF_LON]], axis=1)


def shards(tokens, cotangent, norm_gain, w_qkv, w_out, mlp_gain, w_up, w_down):
    rows, cols, levels, _ = tokens.shape
    g1 = norm_gain.reshape(1, D)
    g2 = mlp_gain.reshape(1, D)
    x = windows(pull_rims(tokens))
    cot = windows(pull_rims(cotangent))
    last_band = lax.axis_index("lat") == lax.axis_size("lat") - 1
    flag = last_band.astype(jnp.int32).reshape(1)

    n1, qkv, p, att, mid, n2 = front(flag, x, g1, w_qkv, w_out, g2)
    res, dmid, dg2, gup, gdown = mlp(n2, cot, mid, g2, w_up, w_down)
    dx, dg1, gqkv, gout = back(x, dmid, n1, qkv, p, att, g1, w_qkv, w_out)

    output = push_rims(unwindows(res, rows, cols, levels))
    grad_tokens = push_rims(unwindows(dx, rows, cols, levels))
    sums = lax.psum((gup, gdown, gqkv, gout), ("lat", "lon"))
    gains = lax.psum(jnp.concatenate([dg1, dg2]), ("lat", "lon"))
    gup, gdown, gqkv, gout = (part.astype(F32) for part in sums)
    return (output, grad_tokens, gains[0], gqkv, gout, gains[1], gup, gdown)


def solution(mesh):
    field = P("lat", "lon", None, None)
    return jax.shard_map(
        shards,
        mesh=mesh,
        in_specs=(field, field, P(), P(), P(), P(), P(), P()),
        out_specs=(field, field, P(), P(), P(), P(), P(), P()),
        check_vma=False,
    )
```

```python
import functools

import jax
import jax.numpy as jnp
from jax import lax
from jax.experimental import pallas as pl
from jax.experimental.pallas import tpu as pltpu
from jax.sharding import PartitionSpec as P

HD = 64
WLAT = 6
WLON = 12
LEV = 2
WIN = WLAT * WLON * LEV
D = 512
FF = 2048
HALF_LAT = WLAT // 2
HALF_LON = WLON // 2
EPS = 1e-05
F32 = jnp.float32
BF16 = jnp.bfloat16
PAIR = 2 * HD
LIMIT = 56 * 1024 * 1024


def mm(a, b):
    return lax.dot_general(a, b, (((1,), (0,)), ((), ())), preferred_element_type=F32)


def mm_t(a, b):
    return lax.dot_general(a, b, (((1,), (1,)), ((), ())), preferred_element_type=F32)


def t_mm(a, b):
    return lax.dot_general(a, b, (((0,), (0,)), ((), ())), preferred_element_type=F32)


def normalised(values):
    mean = jnp.mean(values, axis=-1, keepdims=True)
    centred = values - mean
    var = jnp.mean(centred * centred, axis=-1, keepdims=True)
    scale = lax.rsqrt(var + EPS)
    return centred * scale, scale


def norm_pullback(xhat, scale, gain, grad):
    dxhat = grad * gain
    m1 = jnp.mean(dxhat, axis=-1, keepdims=True)
    m2 = jnp.mean(dxhat * xhat, axis=-1, keepdims=True)
    return scale * (dxhat - m1 - xhat * m2)


def gelu_parts(x):
    a = jnp.abs(x)
    t = 1.0 / (1.0 + (0.3275911 * 0.7071067811865476) * a)
    e = jnp.exp(-0.5 * x * x)
    poly = t * (0.127414796 + t * (-0.142248368 + t * (0.7107068705 + t * (-0.7265760135 + t * 0.5307027145))))
    tail = poly * e
    cdf = jnp.where(x >= 0.0, 1.0 - tail, tail)
    return cdf, 0.3989422804014327 * e


BANDS = 4
SIDES = 2


def strips():
    for band in range(BANDS):
        first = HALF_LAT + band * WLAT
        last = band == BANDS - 1
        across = [(0, WLAT, first, False)]
        if last:
            across = [(0, HALF_LAT, first, False), (HALF_LAT, HALF_LAT, 0, True)]
        for side in range(SIDES):
            left = HALF_LON + side * WLON
            along = [(0, WLON, left, False)]
            if side == SIDES - 1:
                along = [(0, HALF_LON, left, False), (HALF_LON, HALF_LON, 0, True)]
            for at_row, rows, row, far_row in across:
                for at_col, cols, col, far_col in along:
                    piece = 2 * far_row + far_col
                    if far_row and not far_col:
                        col -= HALF_LON
                    if far_col and not far_row:
                        row -= HALF_LAT
                    yield (
                        band, side, pl.ds(at_row, rows), pl.ds(at_col, cols),
                        piece, pl.ds(row, rows), pl.ds(col, cols),
                    )


STRIPS = len(list(strips()))


def gather_windows(which, field, rim_lon, rim_lat, corner, buffer, sems):
    copies = []
    for i, (band, side, to_rows, to_cols, piece, rows, cols) in enumerate(strips()):
        source = field if piece == 0 else (None, rim_lon, rim_lat, corner)[piece].at[which]
        copies.append(pltpu.make_async_copy(
            source.at[rows, cols], buffer.at[band, side, to_rows, to_cols], sems.at[i]))
    return copies


def scatter_windows(which, buffer, field, rim_lon, rim_lat, corner, sems):
    copies = []
    for i, (band, side, to_rows, to_cols, piece, rows, cols) in enumerate(strips()):
        target = field if piece == 0 else (None, rim_lon, rim_lat, corner)[piece].at[which]
        copies.append(pltpu.make_async_copy(
            buffer.at[band, side, to_rows, to_cols], target.at[rows, cols], sems.at[i]))
    return copies


def front_kernel(flag_ref, tok_ref, cot_ref, lon_ref, lat_ref, corner_ref, g1_ref, wqkv_ref, wout_ref, g2_ref,
                 x_ref, cotw_ref, n1_ref, qkv_ref, p_ref, att_ref, mid_ref, n2_ref, tok_buf, cot_buf, sems):
    tok_copies = gather_windows(0, tok_ref, lon_ref, lat_ref, corner_ref, tok_buf, sems.at[0])
    cot_copies = gather_windows(1, cot_ref, lon_ref, lat_ref, corner_ref, cot_buf, sems.at[1])
    for copy in tok_copies + cot_copies:
        copy.start()
    for copy in tok_copies:
        copy.wait()
    for band in range(BANDS):
        for side in range(SIDES):
            w = band * SIDES + side
            x_ref[w * WIN:(w + 1) * WIN, :] = tok_buf[band, side].reshape(WIN, D)
    tokens = x_ref.shape[0]
    count = tokens // WIN
    per_row = count // 4
    gain1 = g1_ref[...]
    gain2 = g2_ref[...]

    @pl.loop(0, count)
    def _(w):
        rows = pl.ds(pl.multiple_of(w * WIN, WIN), WIN)
        xhat, _ = normalised(x_ref[rows, :].astype(F32))
        n1_ref[rows, :] = (xhat * gain1).astype(BF16)

    big = 2 * WIN

    @pl.loop(0, tokens // big)
    def _(b):
        rows = pl.ds(pl.multiple_of(b * big, big), big)
        n1 = n1_ref[rows, :]
        qkv_ref[rows, 0:D] = (mm(n1, wqkv_ref[:, 0:D]).astype(BF16) * 0.125).astype(BF16)
        qkv_ref[rows, D:2 * D] = mm(n1, wqkv_ref[:, D:2 * D]).astype(BF16)
        qkv_ref[rows, 2 * D:3 * D] = mm(n1, wqkv_ref[:, 2 * D:3 * D]).astype(BF16)

    key_group = lax.broadcasted_iota(jnp.int32, (WIN, WIN), 0) >= WIN // 2
    query_group = lax.broadcasted_iota(jnp.int32, (WIN, WIN), 1) >= WIN // 2
    split = key_group != query_group
    low = lax.broadcasted_iota(jnp.int32, (WIN, PAIR), 1) < HD

    @pl.loop(0, count)
    def _(w):
        rows = pl.ds(pl.multiple_of(w * WIN, WIN), WIN)
        cut = jnp.logical_and(flag_ref[0] == 1, w >= count - per_row)
        masked = jnp.logical_and(split, cut)
        for pair in range(D // PAIR):
            lanes = slice(pair * PAIR, (pair + 1) * PAIR)
            q = qkv_ref[rows, pair * PAIR:(pair + 1) * PAIR]
            k = qkv_ref[rows, D + pair * PAIR:D + (pair + 1) * PAIR]
            v = qkv_ref[rows, 2 * D + pair * PAIR:2 * D + (pair + 1) * PAIR]
            outs = []
            for h in range(2):
                mine = low if h == 0 else jnp.logical_not(low)
                kh = jnp.where(mine, k, jnp.zeros_like(k))
                s = mm_t(kh, q)
                s = jnp.where(masked, -1000000000.0, s)
                e = jnp.exp(s - jnp.max(s, axis=0, keepdims=True))
                p = (e * (1.0 / jnp.sum(e, axis=0, keepdims=True))).astype(BF16)
                p_ref[w, 2 * pair + h] = p
                outs.append(t_mm(p, v))
            att_ref[rows, lanes] = jnp.where(low, outs[0], outs[1]).astype(BF16)

    @pl.loop(0, tokens // big)
    def _(b):
        rows = pl.ds(pl.multiple_of(b * big, big), big)
        mid = (x_ref[rows, :].astype(F32) + mm(att_ref[rows, :], wout_ref[...])).astype(BF16)
        mid_ref[rows, :] = mid
        xhat, _ = normalised(mid.astype(F32))
        n2_ref[rows, :] = (xhat * gain2).astype(BF16)

    for copy in cot_copies:
        copy.wait()
    for band in range(BANDS):
        for side in range(SIDES):
            w = band * SIDES + side
            cotw_ref[w * WIN:(w + 1) * WIN, :] = cot_buf[band, side].reshape(WIN, D)


def mlp_chunk(n2_ref, cot_ref, wup_ref, wdown_ref, gup_ref, gdown_ref, down_acc, dn2_acc, hid_ref, du_ref):
    tokens = n2_ref.shape[0]
    big = 2 * WIN

    @pl.loop(0, tokens // big)
    def _(b):
        rows = pl.ds(pl.multiple_of(b * big, big), big)
        up = mm(n2_ref[rows, :], wup_ref[...])
        cdf, pdf = gelu_parts(up)
        hid = (up * cdf).astype(BF16)
        hid_ref[rows, :] = hid
        dhid = mm_t(cot_ref[rows, :], wdown_ref[...]).astype(BF16).astype(F32)
        du = (dhid * (cdf + up * pdf)).astype(BF16)
        du_ref[rows, :] = du
        down_acc[rows, :] += mm(hid, wdown_ref[...])
        dn2_acc[rows, :] += mm_t(du, wup_ref[...])

    gdown_ref[...] = t_mm(hid_ref[...], cot_ref[...]).astype(BF16)
    gup_ref[...] = t_mm(n2_ref[...], du_ref[...]).astype(BF16)


def mlp_send_kernel(me_ref, n2_ref, cot_ref, wup_ref, wdown_ref,
                    down_acc, dn2_acc, gup_ref, gdown_ref, hid_ref, du_ref):
    del me_ref

    @pl.when(pl.program_id(0) == 0)
    def _():
        down_acc[...] = jnp.zeros_like(down_acc)
        dn2_acc[...] = jnp.zeros_like(dn2_acc)

    mlp_chunk(n2_ref, cot_ref, wup_ref, wdown_ref, gup_ref, gdown_ref, down_acc, dn2_acc, hid_ref, du_ref)


def mlp_keep_kernel(me_ref, n2_ref, cot_ref, wup_ref, wdown_ref, mid_ref, g2_ref, down_in, dn2_in,
                    res_ref, dmid_ref, dg2_ref, gup_ref, gdown_ref,
                    down_acc, dn2_acc, hid_ref, du_ref):
    del me_ref
    tokens = n2_ref.shape[0]
    big = 2 * WIN

    @pl.when(pl.program_id(0) == 0)
    def _():
        down_acc[...] = down_in[...]
        dn2_acc[...] = dn2_in[...]

    mlp_chunk(n2_ref, cot_ref, wup_ref, wdown_ref, gup_ref, gdown_ref, down_acc, dn2_acc, hid_ref, du_ref)

    @pl.when(pl.program_id(0) == pl.num_programs(0) - 1)
    def _():
        gain2 = g2_ref[...]
        dg2_ref[...] = jnp.zeros_like(dg2_ref)

        @pl.loop(0, tokens // big)
        def _(b):
            rows = pl.ds(pl.multiple_of(b * big, big), big)
            mid = mid_ref[rows, :].astype(F32)
            res_ref[rows, :] = (mid + down_acc[rows, :]).astype(BF16)
            xhat, scale = normalised(mid)
            dn2 = dn2_acc[rows, :].astype(BF16).astype(F32)
            dg2_ref[...] += jnp.sum(dn2 * xhat, axis=0, keepdims=True)
            dmid = cot_ref[rows, :].astype(F32) + norm_pullback(xhat, scale, gain2, dn2)
            dmid_ref[rows, :] = dmid.astype(BF16)


HALF = D // 2
SLOTS = 72
CHIPS_N = 64


def att_grads(half, n1_ref, dqkv_ref, att_ref, dmid_ref, dg1, dg2, out_ref):
    per = D // (CHIPS_N // 4)
    lanes = pl.ds(pl.multiple_of(half * HALF, HALF), HALF)
    for part in range(4):
        if part < 3:
            part_lanes = pl.ds(pl.multiple_of(part * D + half * HALF, HALF), HALF)
            grad = t_mm(n1_ref[...], dqkv_ref[:, part_lanes])
        else:
            grad = t_mm(att_ref[...], dmid_ref[:, lanes])
        grad = grad.astype(BF16)
        first = part * (CHIPS_N // 4)
        for block in range(2):
            piece = grad[:, block * 128:(block + 1) * 128].reshape(CHIPS_N // 4, per, 128)
            out_ref[first:first + CHIPS_N // 4, block * per:(block + 1) * per, :] = piece
    out_ref[:, 2 * per:, :] = jnp.zeros((CHIPS_N, SLOTS - 2 * per, 128), BF16)
    gain = jnp.where(half == 0, dg1, dg2)
    for block in range(D // 128):
        row = jnp.broadcast_to(gain[:, block * 128:(block + 1) * 128], (SLOTS - 2 * per, 128))
        out_ref[block, 2 * per:, :] = row.astype(BF16)


def back_kernel(me_ref, dmid_ref, n1_ref, qkv_ref, p_ref, att_ref, x_ref, g1_ref, wqkv_ref, wout_ref, dg2_ref, res_ref,
                out_ref, grad_ref, lon_ref, lat_ref, corner_ref, dqkv_ref, dg1_ref, send_ref,
                datt_ref, dx_ref, res_buf, dx_buf, sems):
    for band in range(BANDS):
        for side in range(SIDES):
            w = band * SIDES + side
            res_buf[band, side] = res_ref[w * WIN:(w + 1) * WIN, :].reshape(WLAT, WLON, LEV, D)
    res_copies = scatter_windows(0, res_buf, out_ref, lon_ref, lat_ref, corner_ref, sems.at[0])
    for copy in res_copies:
        copy.start()
    tokens = dmid_ref.shape[0]
    count = tokens // WIN
    gain1 = g1_ref[...]
    big = 2 * WIN

    @pl.loop(0, tokens // big)
    def _(b):
        rows = pl.ds(pl.multiple_of(b * big, big), big)
        datt_ref[rows, :] = mm_t(dmid_ref[rows, :], wout_ref[...]).astype(BF16)

    low = lax.broadcasted_iota(jnp.int32, (WIN, PAIR), 1) < HD

    @pl.loop(0, count)
    def _(w):
        rows = pl.ds(pl.multiple_of(w * WIN, WIN), WIN)
        for pair in range(D // PAIR):
            lanes = slice(pair * PAIR, (pair + 1) * PAIR)
            q = qkv_ref[rows, pair * PAIR:(pair + 1) * PAIR]
            k = qkv_ref[rows, D + pair * PAIR:D + (pair + 1) * PAIR]
            v = qkv_ref[rows, 2 * D + pair * PAIR:2 * D + (pair + 1) * PAIR]
            da = datt_ref[rows, lanes]
            dqs, dks, dvs = [], [], []
            for h in range(2):
                mine = low if h == 0 else jnp.logical_not(low)
                vh = jnp.where(mine, v, jnp.zeros_like(v))
                p = p_ref[w, 2 * pair + h]
                pf = p.astype(F32)
                dp = mm_t(vh, da).astype(BF16).astype(F32)
                ds = (pf * (dp - jnp.sum(dp * pf, axis=0, keepdims=True))).astype(BF16)
                dvs.append(mm(p, da))
                dks.append(mm(ds, q))
                dqs.append(t_mm(ds, k))
            dqkv_ref[rows, pair * PAIR:(pair + 1) * PAIR] = (jnp.where(low, dqs[0], dqs[1]) * 0.125).astype(BF16)
            dqkv_ref[rows, D + pair * PAIR:D + (pair + 1) * PAIR] = jnp.where(low, dks[0], dks[1]).astype(BF16)
            dqkv_ref[rows, 2 * D + pair * PAIR:2 * D + (pair + 1) * PAIR] = jnp.where(low, dvs[0], dvs[1]).astype(BF16)

    dg1_ref[...] = jnp.zeros_like(dg1_ref)

    @pl.loop(0, tokens // big)
    def _(b):
        rows = pl.ds(pl.multiple_of(b * big, big), big)
        dn1 = mm_t(dqkv_ref[rows, :], wqkv_ref[...]).astype(BF16).astype(F32)
        xhat, scale = normalised(x_ref[rows, :].astype(F32))
        dg1_ref[...] += jnp.sum(dn1 * xhat, axis=0, keepdims=True)
        dx = dmid_ref[rows, :].astype(F32) + norm_pullback(xhat, scale, gain1, dn1)
        dx_ref[rows, :] = dx.astype(BF16)

    for band in range(BANDS):
        for side in range(SIDES):
            w = band * SIDES + side
            dx_buf[band, side] = dx_ref[w * WIN:(w + 1) * WIN, :].reshape(WLAT, WLON, LEV, D)
    dx_copies = scatter_windows(1, dx_buf, grad_ref, lon_ref, lat_ref, corner_ref, sems.at[1])
    for copy in dx_copies:
        copy.start()
    att_grads(1 - me_ref[0], n1_ref, dqkv_ref, att_ref, dmid_ref, dg1_ref[...], dg2_ref[...], send_ref)
    for copy in res_copies + dx_copies:
        copy.wait()


def keep_kernel(me_ref, n1_ref, dqkv_ref, att_ref, dmid_ref, dg1_ref, dg2_ref, keep_ref):
    att_grads(me_ref[0], n1_ref, dqkv_ref, att_ref, dmid_ref, dg1_ref[...], dg2_ref[...], keep_ref)


def share_kernel(in_ref, out_ref):
    total = in_ref[0].astype(F32)
    for chip in range(1, in_ref.shape[0]):
        total += in_ref[chip].astype(F32)
    total = total.astype(BF16)
    for chip in range(in_ref.shape[0]):
        out_ref[chip] = total


def unpack_mlp_kernel(me_ref, mine_ref, theirs_ref, gup_ref, gdown_ref):
    wide = FF // 2
    for ref, half in ((mine_ref, me_ref[0]), (theirs_ref, 1 - me_ref[0])):
        for block in range(2):
            lanes = pl.ds(pl.multiple_of(half * wide + block * D, D), D)
            gup_ref[:, lanes] = ref[block * D:(block + 1) * D, :].astype(F32)
        gdown_ref[pl.ds(pl.multiple_of(half * wide, wide), wide), :] = ref[2 * D:, :].astype(F32)


def unpack_att_kernel(me_ref, mine_ref, theirs_ref, gqkv_ref, gout_ref, gains_ref):
    quarter = CHIPS_N // 4
    per = D // quarter
    for ref, half in ((mine_ref, me_ref[0]), (theirs_ref, 1 - me_ref[0])):
        for part in range(4):
            for block in range(2):
                piece = ref[part * quarter:(part + 1) * quarter, block * per:(block + 1) * per, :]
                piece = piece.reshape(D, 128).astype(F32)
                out, first = (gqkv_ref, part * D) if part < 3 else (gout_ref, 0)
                out[:, pl.ds(pl.multiple_of(half * HALF + (first + block * 128), 128), 128)] = piece
        for block in range(D // 128):
            gains_ref[pl.ds(pl.multiple_of(half * 8, 8), 8), block * 128:(block + 1) * 128] = ref[block, 2 * per:, :].astype(F32)


def pack_kernel(tok_ref, cot_ref, lon_ref, lat_ref, corner_ref, sems):
    copies = []
    for which, ref in enumerate((tok_ref, cot_ref)):
        below, right = pl.ds(HALF_LAT, ref.shape[0] - HALF_LAT), pl.ds(HALF_LON, ref.shape[1] - HALF_LON)
        top, left = pl.ds(0, HALF_LAT), pl.ds(0, HALF_LON)
        for i, (rows, cols, out) in enumerate(((below, left, lon_ref), (top, right, lat_ref), (top, left, corner_ref))):
            copies.append(pltpu.make_async_copy(ref.at[rows, cols], out.at[which], sems.at[which, i]))
    for copy in copies:
        copy.start()
    for copy in copies:
        copy.wait()


def place_kernel(out_in, grad_in, lon_ref, lat_ref, corner_ref, out_ref, grad_ref, sems):
    del out_in, grad_in
    copies = []
    for which, ref in enumerate((out_ref, grad_ref)):
        below, right = pl.ds(HALF_LAT, ref.shape[0] - HALF_LAT), pl.ds(HALF_LON, ref.shape[1] - HALF_LON)
        top, left = pl.ds(0, HALF_LAT), pl.ds(0, HALF_LON)
        for i, (rows, cols, rim) in enumerate(((below, left, lon_ref), (top, right, lat_ref), (top, left, corner_ref))):
            copies.append(pltpu.make_async_copy(rim.at[which], ref.at[rows, cols], sems.at[which, i]))
    for copy in copies:
        copy.start()
    for copy in copies:
        copy.wait()


def params():
    return pltpu.CompilerParams(vmem_limit_bytes=LIMIT)


def cost(flops, moved):
    return pl.CostEstimate(flops=flops, bytes_accessed=moved, transcendentals=0)


def shape(dims, dtype=BF16):
    return jax.ShapeDtypeStruct(dims, dtype)


SM = pl.BlockSpec(memory_space=pltpu.SMEM)
VM = pl.BlockSpec(memory_space=pltpu.VMEM)


ANY = pl.BlockSpec(memory_space=pl.ANY)


def rim_shapes(rows, cols, levels):
    return [
        shape((2, rows - HALF_LAT, HALF_LON, levels, D)),
        shape((2, HALF_LAT, cols - HALF_LON, levels, D)),
        shape((2, HALF_LAT, HALF_LON, levels, D)),
    ]


def pack(tokens, cotangent):
    return pl.pallas_call(
        pack_kernel,
        name="pack",
        in_specs=[ANY] * 2,
        out_specs=[ANY] * 3,
        out_shape=rim_shapes(*tokens.shape[:3]),
        scratch_shapes=[pltpu.SemaphoreType.DMA((2, 3))],
    )(tokens, cotangent)


def place(output, grad, lon, lat, corner):
    return pl.pallas_call(
        place_kernel,
        name="place",
        in_specs=[ANY] * 5,
        out_specs=[ANY] * 2,
        out_shape=[shape(output.shape), shape(grad.shape)],
        input_output_aliases={0: 0, 1: 1},
        scratch_shapes=[pltpu.SemaphoreType.DMA((2, 3))],
        cost_estimate=cost(10**9, 2**21),
    )(output, grad, lon, lat, corner)


WINDOWED = (BANDS, SIDES, WLAT, WLON, LEV, D)


def front(flag, tok, cot, lon, lat, corner, g1, wqkv, wout, g2):
    tokens = tok.size // D
    count = tokens // WIN
    return pl.pallas_call(
        front_kernel,
        name="front",
        in_specs=[SM] + [ANY] * 5 + [VM] * 4,
        out_specs=[VM] * 8,
        out_shape=[
            shape((tokens, D)),
            shape((tokens, D)),
            shape((tokens, D)),
            shape((tokens, 3 * D)),
            shape((count, D // HD, WIN, WIN)),
            shape((tokens, D)),
            shape((tokens, D)),
            shape((tokens, D)),
        ],
        scratch_shapes=[
            pltpu.VMEM(WINDOWED, BF16),
            pltpu.VMEM(WINDOWED, BF16),
            pltpu.SemaphoreType.DMA((2, STRIPS)),
        ],
        compiler_params=params(),
        cost_estimate=cost(20 * 10**9, 10 * 2**20),
    )(flag, tok, cot, lon, lat, corner, g1, wqkv, wout, g2)


def mlp_specs(tokens, chunk):
    steps = FF // chunk // 2
    specs = {
        "whole": pl.BlockSpec((tokens, D), lambda i, me: (0, 0)),
        "gain": pl.BlockSpec((1, D), lambda i, me: (0, 0)),
        "out": pl.BlockSpec((chunk, D), lambda i, me: (i, 0)),
    }
    for name, other in (("send", 1), ("keep", 0)):
        def place(i, me, other=other):
            return (me[0] if other == 0 else 1 - me[0]) * steps + i
        specs[name] = [
            pl.BlockSpec((D, chunk), lambda i, me, place=place: (0, place(i, me))),
            pl.BlockSpec((chunk, D), lambda i, me, place=place: (place(i, me), 0)),
        ]
    return specs, steps


def mlp_send(me, n2, cot, wup, wdown, chunk=512):
    tokens = n2.shape[0]
    specs, steps = mlp_specs(tokens, chunk)
    whole, out = specs["whole"], specs["out"]
    return pl.pallas_call(
        mlp_send_kernel,
        name="mlp_send",
        grid_spec=pltpu.PrefetchScalarGridSpec(
            num_scalar_prefetch=1,
            grid=(steps,),
            in_specs=[whole, whole] + specs["send"],
            out_specs=[whole, whole, out, out],
            scratch_shapes=[pltpu.VMEM((tokens, chunk), BF16), pltpu.VMEM((tokens, chunk), BF16)],
        ),
        out_shape=[shape((tokens, D), F32), shape((tokens, D), F32), shape((FF // 2, D)), shape((FF // 2, D))],
        compiler_params=params(),
        cost_estimate=cost(16 * 10**9, 10 * 2**20),
    )(me, n2, cot, wup, wdown)


def mlp_keep(me, n2, cot, wup, wdown, mid, g2, down, dn2, chunk=512):
    tokens = n2.shape[0]
    specs, steps = mlp_specs(tokens, chunk)
    whole, out, gain = specs["whole"], specs["out"], specs["gain"]
    return pl.pallas_call(
        mlp_keep_kernel,
        name="mlp_keep",
        grid_spec=pltpu.PrefetchScalarGridSpec(
            num_scalar_prefetch=1,
            grid=(steps,),
            in_specs=[whole, whole] + specs["keep"] + [whole, gain, whole, whole],
            out_specs=[whole, whole, gain, out, out],
            scratch_shapes=[
                pltpu.VMEM((tokens, D), F32),
                pltpu.VMEM((tokens, D), F32),
                pltpu.VMEM((tokens, chunk), BF16),
                pltpu.VMEM((tokens, chunk), BF16),
            ],
        ),
        out_shape=[
            shape((tokens, D)),
            shape((tokens, D)),
            shape((1, D), F32),
            shape((FF // 2, D)),
            shape((FF // 2, D)),
        ],
        compiler_params=params(),
        cost_estimate=cost(16 * 10**9, 10 * 2**20),
    )(me, n2, cot, wup, wdown, mid, g2, down, dn2)


def back(me, dmid, n1, qkv, p, att, x, g1, wqkv, wout, dg2, res, field):
    tokens = x.shape[0]
    return pl.pallas_call(
        back_kernel,
        name="back",
        in_specs=[SM] + [VM] * 11,
        out_specs=[ANY] * 5 + [VM] * 3,
        out_shape=[shape(field), shape(field)] + rim_shapes(*field[:3]) + [
            shape((tokens, 3 * D)),
            shape((1, D), F32),
            shape((CHIPS_N, SLOTS, 128)),
        ],
        scratch_shapes=[
            pltpu.VMEM((tokens, D), BF16),
            pltpu.VMEM((tokens, D), BF16),
            pltpu.VMEM(WINDOWED, BF16),
            pltpu.VMEM(WINDOWED, BF16),
            pltpu.SemaphoreType.DMA((2, STRIPS)),
        ],
        compiler_params=params(),
        cost_estimate=cost(30 * 10**9, 10 * 2**20),
    )(me, dmid, n1, qkv, p, att, x, g1, wqkv, wout, dg2, res)


def keep_grads(me, n1, dqkv, att, dmid, dg1, dg2):
    return pl.pallas_call(
        keep_kernel,
        name="keep",
        in_specs=[SM] + [VM] * 6,
        out_specs=VM,
        out_shape=shape((CHIPS_N, SLOTS, 128)),
        compiler_params=params(),
        cost_estimate=cost(4 * 10**9, 4 * 2**20),
    )(me, n1, dqkv, att, dmid, dg1, dg2)


def unpack_mlp(me, mine, theirs):
    return pl.pallas_call(
        unpack_mlp_kernel,
        name="unpack_mlp",
        in_specs=[SM, VM, VM],
        out_specs=[VM, VM],
        out_shape=[shape((D, FF), F32), shape((FF, D), F32)],
        compiler_params=params(),
        cost_estimate=cost(10**9, 12 * 2**20),
    )(me, mine, theirs)


def unpack_att(me, mine, theirs):
    return pl.pallas_call(
        unpack_att_kernel,
        name="unpack_att",
        in_specs=[SM, VM, VM],
        out_specs=[VM] * 3,
        out_shape=[shape((D, 3 * D), F32), shape((D, D), F32), shape((16, D), F32)],
        compiler_params=params(),
        cost_estimate=cost(10**9, 6 * 2**20),
    )(me, mine, theirs)


LAT = ("x", "zl")
LON = ("zh", "y", "c")
CHIPS = ("x", "zl", "zh", "y")


def send_rims(lon, lat, corner, distance):
    lats, lons = lax.axis_size(LAT), lax.axis_size(LON)
    moved = []
    for block, down, across in ((lon, 0, distance), (lat, distance, 0), (corner, distance, distance)):
        route = [
            (i * lons + j, (i + down) % lats * lons + (j + across) % lons)
            for i in range(lats) for j in range(lons)
        ]
        moved.append(lax.ppermute(block, LAT + LON, route))
    return moved


def other_core(block):
    return lax.ppermute(block, "c", [(0, 1), (1, 0)])


def exchange(parts):
    return lax.all_to_all(parts, CHIPS, 0, 0, tiled=True)


def add_cores(keep, got):
    return (keep.astype(F32) + got.astype(F32)).astype(BF16)


def shared(parts):
    return pl.pallas_call(
        share_kernel,
        name="share",
        in_specs=[VM],
        out_specs=VM,
        out_shape=shape(parts.shape),
        compiler_params=params(),
        cost_estimate=cost(10**9, 2 * parts.size * 2),
    )(parts)


def shards(tokens, cotangent, norm_gain, w_qkv, w_out, mlp_gain, w_up, w_down):
    g1 = norm_gain.reshape(1, D)
    g2 = mlp_gain.reshape(1, D)
    last_band = lax.axis_index(LAT) == lax.axis_size(LAT) - 1
    flag = last_band.astype(jnp.int32).reshape(1)
    me = lax.axis_index("c").astype(jnp.int32).reshape(1)

    rims = send_rims(*pack(tokens, cotangent), -1)
    x, cot, n1, qkv, p, att, mid, n2 = front(flag, tokens, cotangent, *rims, g1, w_qkv, w_out, g2)
    down, dn2, gup, gdown = mlp_send(me, n2, cot, w_up, w_down)
    got = other_core(jnp.concatenate([gup, gdown]))
    res, dmid, dg2, gup, gdown = mlp_keep(me, n2, cot, w_up, w_down, mid, g2, down, dn2)
    mlp_part = add_cores(jnp.concatenate([gup, gdown]), got).reshape(CHIPS_N, -1, D)
    mlp_part = exchange(mlp_part)
    output, grad_tokens, lon, lat, corner, dqkv, dg1, send = back(
        me, dmid, n1, qkv, p, att, x, g1, w_qkv, w_out, dg2, res, tokens.shape)
    got = other_core(send)
    rims = send_rims(lon, lat, corner, 1)
    keep = keep_grads(me, n1, dqkv, att, dmid, dg1, dg2)
    att_part = exchange(add_cores(keep, got))
    output, grad_tokens = place(output, grad_tokens, *rims)
    mlp_mine = exchange(shared(mlp_part)).reshape(-1, D)
    att_part, output, grad_tokens = lax.optimization_barrier((att_part, output, grad_tokens))
    att_mine = exchange(shared(att_part))
    gup, gdown = unpack_mlp(me, mlp_mine, other_core(mlp_mine))
    att_mine, gup, gdown = lax.optimization_barrier((att_mine, gup, gdown))
    gqkv, gout, gains = unpack_att(me, att_mine, other_core(att_mine))
    return (output, grad_tokens, gains[0], gqkv, gout, gains[8], gup, gdown)


def solution(mesh):
    field = P(LAT, LON, None, None)
    mesh = jax.sharding.Mesh(mesh.devices.reshape(4, 2, 2, 4, 2), ("x", "zl", "zh", "y", "c"))
    return jax.shard_map(
        shards,
        mesh=mesh,
        in_specs=(field, field, P(), P(), P(), P(), P(), P()),
        out_specs=(field, field, P(), P(), P(), P(), P(), P()),
        check_vma=False,
    )
```

```python
import functools

import jax
import jax.numpy as jnp
from jax import lax
from jax.experimental import pallas as pl
from jax.experimental.pallas import tpu as pltpu
from jax.sharding import PartitionSpec as P

HD = 64
WLAT = 6
WLON = 12
LEV = 2
WIN = WLAT * WLON * LEV
D = 512
FF = 2048
HALF_LAT = WLAT // 2
HALF_LON = WLON // 2
EPS = 1e-05
F32 = jnp.float32
BF16 = jnp.bfloat16
PAIR = 2 * HD


def mm(a, b):
    return lax.dot_general(a, b, (((1,), (0,)), ((), ())), preferred_element_type=F32)


def mm_t(a, b):
    return lax.dot_general(a, b, (((1,), (1,)), ((), ())), preferred_element_type=F32)


def t_mm(a, b):
    return lax.dot_general(a, b, (((0,), (0,)), ((), ())), preferred_element_type=F32)


def normalised(values):
    mean = jnp.mean(values, axis=-1, keepdims=True)
    centred = values - mean
    var = jnp.mean(centred * centred, axis=-1, keepdims=True)
    scale = lax.rsqrt(var + EPS)
    return centred * scale, scale


def norm_pullback(xhat, scale, gain, grad):
    dxhat = grad * gain
    m1 = jnp.mean(dxhat, axis=-1, keepdims=True)
    m2 = jnp.mean(dxhat * xhat, axis=-1, keepdims=True)
    return scale * (dxhat - m1 - xhat * m2)


def gelu_parts(x):
    a = jnp.abs(x)
    t = 1.0 / (1.0 + (0.3275911 * 0.7071067811865476) * a)
    e = jnp.exp(-0.5 * x * x)
    poly = t * (0.127414796 + t * (-0.142248368 + t * (0.7107068705 + t * (-0.7265760135 + t * 0.5307027145))))
    tail = poly * e
    cdf = jnp.where(x >= 0.0, 1.0 - tail, tail)
    return cdf, 0.3989422804014327 * e


BANDS = 4
SIDES = 2


def strips():
    for band in range(BANDS):
        first = HALF_LAT + band * WLAT
        last = band == BANDS - 1
        across = [(0, WLAT, first, False)]
        if last:
            across = [(0, HALF_LAT, first, False), (HALF_LAT, HALF_LAT, 0, True)]
        for side in range(SIDES):
            left = HALF_LON + side * WLON
            along = [(0, WLON, left, False)]
            if side == SIDES - 1:
                along = [(0, HALF_LON, left, False), (HALF_LON, HALF_LON, 0, True)]
            for at_row, rows, row, far_row in across:
                for at_col, cols, col, far_col in along:
                    piece = 2 * far_row + far_col
                    if far_row and not far_col:
                        col -= HALF_LON
                    if far_col and not far_row:
                        row -= HALF_LAT
                    yield (
                        band, side, pl.ds(at_row, rows), pl.ds(at_col, cols),
                        piece, pl.ds(row, rows), pl.ds(col, cols),
                    )


SAVES = 6
STRIPS = len(list(strips()))


def gather_windows(which, field, rim_lon, rim_lat, corner, buffer, sems):
    copies = []
    for i, (band, side, to_rows, to_cols, piece, rows, cols) in enumerate(strips()):
        source = field if piece == 0 else (None, rim_lon, rim_lat, corner)[piece].at[which]
        copies.append(pltpu.make_async_copy(
            source.at[rows, cols], buffer.at[band, side, to_rows, to_cols], sems.at[i]))
    return copies


def scatter_windows(which, buffer, field, rim_lon, rim_lat, corner, sems):
    copies = []
    for i, (band, side, to_rows, to_cols, piece, rows, cols) in enumerate(strips()):
        target = field if piece == 0 else (None, rim_lon, rim_lat, corner)[piece].at[which]
        copies.append(pltpu.make_async_copy(
            buffer.at[band, side, to_rows, to_cols], target.at[rows, cols], sems.at[i]))
    return copies


def front_kernel(flag_ref, tok_ref, cot_ref, lon_ref, lat_ref, corner_ref, g1_ref, wqkv_hbm, wout_hbm, g2_ref,
                 x_out, n1_out, qkv_out, p_out, att_out, mid_out, cot_out, cotw_ref, n2_ref,
                 tok_buf, cot_buf, x_ref, n1_ref, qkv_ref, p_ref, att_ref, mid_ref, wqkv_ref, wout_ref,
                 sems, out_sems, w_sems):
    wqkv_copy = pltpu.make_async_copy(wqkv_hbm, wqkv_ref, w_sems.at[0])
    wout_copy = pltpu.make_async_copy(wout_hbm, wout_ref, w_sems.at[1])
    saves = []

    def save(source, target):
        copy = pltpu.make_async_copy(source, target, out_sems.at[len(saves)])
        copy.start()
        saves.append(copy)

    tok_copies = gather_windows(0, tok_ref, lon_ref, lat_ref, corner_ref, tok_buf, sems.at[0])
    cot_copies = gather_windows(1, cot_ref, lon_ref, lat_ref, corner_ref, cot_buf, sems.at[1])
    for copy in tok_copies + [wqkv_copy, wout_copy] + cot_copies:
        copy.start()
    for copy in tok_copies:
        copy.wait()
    for band in range(BANDS):
        for side in range(SIDES):
            w = band * SIDES + side
            x_ref[w * WIN:(w + 1) * WIN, :] = tok_buf[band, side].reshape(WIN, D)
    save(x_ref, x_out)
    tokens = x_ref.shape[0]
    count = tokens // WIN
    per_row = count // 4
    gain1 = g1_ref[...]
    gain2 = g2_ref[...]

    @pl.loop(0, count)
    def _(w):
        rows = pl.ds(pl.multiple_of(w * WIN, WIN), WIN)
        xhat, _ = normalised(x_ref[rows, :].astype(F32))
        n1_ref[rows, :] = (xhat * gain1).astype(BF16)

    wqkv_copy.wait()

    big = ROWS

    @pl.loop(0, tokens // big)
    def _(b):
        rows = pl.ds(pl.multiple_of(b * big, big), big)
        n1 = n1_ref[rows, :]
        qkv_ref[rows, 0:D] = (mm(n1, wqkv_ref[:, 0:D]).astype(BF16) * 0.125).astype(BF16)
        qkv_ref[rows, D:2 * D] = mm(n1, wqkv_ref[:, D:2 * D]).astype(BF16)
        qkv_ref[rows, 2 * D:3 * D] = mm(n1, wqkv_ref[:, 2 * D:3 * D]).astype(BF16)

    save(n1_ref, n1_out)
    save(qkv_ref, qkv_out)

    key_group = lax.broadcasted_iota(jnp.int32, (WIN, WIN), 0) >= WIN // 2
    query_group = lax.broadcasted_iota(jnp.int32, (WIN, WIN), 1) >= WIN // 2
    split = key_group != query_group
    low = lax.broadcasted_iota(jnp.int32, (WIN, PAIR), 1) < HD

    @pl.loop(0, count)
    def _(w):
        rows = pl.ds(pl.multiple_of(w * WIN, WIN), WIN)
        cut = jnp.logical_and(flag_ref[0] == 1, w >= count - per_row)
        masked = jnp.logical_and(split, cut)
        for pair in range(D // PAIR):
            lanes = slice(pair * PAIR, (pair + 1) * PAIR)
            q = qkv_ref[rows, pair * PAIR:(pair + 1) * PAIR]
            k = qkv_ref[rows, D + pair * PAIR:D + (pair + 1) * PAIR]
            v = qkv_ref[rows, 2 * D + pair * PAIR:2 * D + (pair + 1) * PAIR]
            outs = []
            for h in range(2):
                mine = low if h == 0 else jnp.logical_not(low)
                kh = jnp.where(mine, k, jnp.zeros_like(k))
                s = mm_t(kh, q)
                s = jnp.where(masked, -1000000000.0, s)
                e = jnp.exp(s - jnp.max(s, axis=0, keepdims=True))
                p = (e * (1.0 / jnp.sum(e, axis=0, keepdims=True))).astype(BF16)
                p_ref[w, 2 * pair + h] = p
                outs.append(t_mm(p, v))
            att_ref[rows, lanes] = jnp.where(low, outs[0], outs[1]).astype(BF16)
        pltpu.make_async_copy(p_ref.at[w], p_out.at[w], out_sems.at[SAVES + w]).start()

    save(att_ref, att_out)
    wout_copy.wait()

    @pl.loop(0, tokens // big)
    def _(b):
        rows = pl.ds(pl.multiple_of(b * big, big), big)
        mid = (x_ref[rows, :].astype(F32) + mm(att_ref[rows, :], wout_ref[...])).astype(BF16)
        mid_ref[rows, :] = mid
        xhat, _ = normalised(mid.astype(F32))
        n2_ref[rows, :] = (xhat * gain2).astype(BF16)

    save(mid_ref, mid_out)
    for copy in cot_copies:
        copy.wait()
    for band in range(BANDS):
        for side in range(SIDES):
            w = band * SIDES + side
            cotw_ref[w * WIN:(w + 1) * WIN, :] = cot_buf[band, side].reshape(WIN, D)
    save(cotw_ref, cot_out)
    for copy in saves:
        copy.wait()
    for w in range(count):
        pltpu.make_async_copy(p_ref.at[w], p_out.at[w], out_sems.at[SAVES + w]).wait()


CHUNK = 512
ROWS = 4 * WIN


def mlp_chunk(chunk, n2_ref, cot_ref, wup_ref, wdown_ref, down_in, dn2_in, down_out, dn2_out, hid_ref, du_ref):
    at = pl.ds(pl.multiple_of(chunk * CHUNK, CHUNK), CHUNK)

    @pl.loop(0, n2_ref.shape[0] // ROWS)
    def _(b):
        rows = pl.ds(pl.multiple_of(b * ROWS, ROWS), ROWS)
        up = mm(n2_ref[rows, :], wup_ref[:, at])
        cdf, pdf = gelu_parts(up)
        hid = (up * cdf).astype(BF16)
        hid_ref[rows, :] = hid
        dhid = mm_t(cot_ref[rows, :], wdown_ref[at, :]).astype(BF16).astype(F32)
        du = (dhid * (cdf + up * pdf)).astype(BF16)
        du_ref[rows, :] = du
        down = mm(hid, wdown_ref[at, :])
        dn2 = mm_t(du, wup_ref[:, at])
        if down_in is None:
            down_out[rows, :] = down
            dn2_out[rows, :] = dn2
        else:
            down_out[rows, :] = down_in[rows, :] + down
            dn2_out[rows, :] = dn2_in[rows, :] + dn2

    return t_mm(n2_ref[...], du_ref[...]).astype(BF16), t_mm(hid_ref[...], cot_ref[...]).astype(BF16)


def send_kernel(me_ref, n2_ref, cot_ref, wup_ref, wdown_ref, down_ref, dn2_ref, grads_ref, hid_ref, du_ref):
    for i in range(2):
        carried = (down_ref, dn2_ref) if i else (None, None)
        grads = mlp_chunk((1 - me_ref[0]) * 2 + i, n2_ref, cot_ref, wup_ref, wdown_ref,
                          *carried, down_ref, dn2_ref, hid_ref, du_ref)
        for part, grad in enumerate(grads):
            grads_ref[(2 * part + i) * CHUNK:(2 * part + i + 1) * CHUNK, :] = grad


def keep_first_kernel(me_ref, n2_ref, cot_ref, wup_ref, wdown_ref, down_in, dn2_in,
                      down_ref, dn2_ref, early_ref, hid_ref, du_ref):
    grads = mlp_chunk(me_ref[0] * 2, n2_ref, cot_ref, wup_ref, wdown_ref,
                      down_in, dn2_in, down_ref, dn2_ref, hid_ref, du_ref)
    for part, grad in enumerate(grads):
        early_ref[part * CHUNK:(part + 1) * CHUNK, :] = grad


def keep_second_kernel(me_ref, n2_ref, cot_ref, wup_ref, wdown_ref, down_in, dn2_in, early_ref, got_ref,
                       down_hbm, dn2_hbm, grads_ref, hid_ref, du_ref, down_ref, dn2_ref, sems):
    grads = mlp_chunk(me_ref[0] * 2 + 1, n2_ref, cot_ref, wup_ref, wdown_ref,
                      down_in, dn2_in, down_ref, dn2_ref, hid_ref, du_ref)
    copies = [
        pltpu.make_async_copy(down_ref, down_hbm, sems.at[0]),
        pltpu.make_async_copy(dn2_ref, dn2_hbm, sems.at[1]),
    ]
    for copy in copies:
        copy.start()
    for part, grad in enumerate(grads):
        for i in range(2):
            rows = slice((2 * part + i) * CHUNK, (2 * part + i + 1) * CHUNK)
            mine = grad if i else early_ref[part * CHUNK:(part + 1) * CHUNK, :]
            grads_ref[rows, :] = (mine.astype(F32) + got_ref[rows, :].astype(F32)).astype(BF16)
    for copy in copies:
        copy.wait()


HALF = D // 2
SLOTS = 72
CHIPS_N = 64


def att_grads(half, n1_ref, dqkv_ref, att_ref, dmid_ref, dg1, dg2, out_ref):
    per = D // (CHIPS_N // 4)
    lanes = pl.ds(pl.multiple_of(half * HALF, HALF), HALF)
    for part in range(4):
        if part < 3:
            part_lanes = pl.ds(pl.multiple_of(part * D + half * HALF, HALF), HALF)
            grad = t_mm(n1_ref[...], dqkv_ref[:, part_lanes])
        else:
            grad = t_mm(att_ref[...], dmid_ref[:, lanes])
        grad = grad.astype(BF16)
        first = part * (CHIPS_N // 4)
        for block in range(2):
            piece = grad[:, block * 128:(block + 1) * 128].reshape(CHIPS_N // 4, per, 128)
            out_ref[first:first + CHIPS_N // 4, block * per:(block + 1) * per, :] = piece
    out_ref[:, 2 * per:, :] = jnp.zeros((CHIPS_N, SLOTS - 2 * per, 128), BF16)
    gain = jnp.where(half == 0, dg1, dg2)
    for block in range(D // 128):
        row = jnp.broadcast_to(gain[:, block * 128:(block + 1) * 128], (SLOTS - 2 * per, 128))
        out_ref[block, 2 * per:, :] = row.astype(BF16)


def att_back(first, last, datt_ref, qkv_ref, p_ref, dqkv_ref):
    low = lax.broadcasted_iota(jnp.int32, (WIN, PAIR), 1) < HD

    @pl.loop(first, last)
    def _(w):
        rows = pl.ds(pl.multiple_of(w * WIN, WIN), WIN)
        for pair in range(D // PAIR):
            lanes = slice(pair * PAIR, (pair + 1) * PAIR)
            q = qkv_ref[rows, pair * PAIR:(pair + 1) * PAIR]
            k = qkv_ref[rows, D + pair * PAIR:D + (pair + 1) * PAIR]
            v = qkv_ref[rows, 2 * D + pair * PAIR:2 * D + (pair + 1) * PAIR]
            da = datt_ref[rows, lanes]
            dqs, dks, dvs = [], [], []
            for h in range(2):
                mine = low if h == 0 else jnp.logical_not(low)
                vh = jnp.where(mine, v, jnp.zeros_like(v))
                p = p_ref[w, 2 * pair + h]
                pf = p.astype(F32)
                dp = mm_t(vh, da).astype(BF16).astype(F32)
                ds = (pf * (dp - jnp.sum(dp * pf, axis=0, keepdims=True))).astype(BF16)
                dvs.append(mm(p, da))
                dks.append(mm(ds, q))
                dqs.append(t_mm(ds, k))
            dqkv_ref[rows, pair * PAIR:(pair + 1) * PAIR] = (jnp.where(low, dqs[0], dqs[1]) * 0.125).astype(BF16)
            dqkv_ref[rows, D + pair * PAIR:D + (pair + 1) * PAIR] = jnp.where(low, dks[0], dks[1]).astype(BF16)
            dqkv_ref[rows, 2 * D + pair * PAIR:2 * D + (pair + 1) * PAIR] = jnp.where(low, dvs[0], dvs[1]).astype(BF16)


def back_kernel(me_ref, cot_hbm, mid_hbm, down_hbm, dn2_hbm, wout_hbm, qkv_hbm, p_hbm, wqkv_hbm, x_hbm, att_hbm, n1_hbm,
                g1_ref, g2_ref,
                out_ref, grad_ref, lon_ref, lat_ref, corner_ref,
                att_ref, n1_ref, dmid_ref, dqkv_ref, dg1_ref, dg2_ref, send_ref,
                cot_ref, mid_ref, down_ref, dn2_ref, wout_ref, qkv_ref, p_ref, wqkv_ref, x_ref,
                datt_ref, dx_ref, res_ref, res_buf, dx_buf, in_sems, sems):
    loads = {}
    for i, (name, source, target) in enumerate((
        ("cot", cot_hbm, cot_ref), ("mid", mid_hbm, mid_ref), ("down", down_hbm, down_ref), ("dn2", dn2_hbm, dn2_ref),
        ("wout", wout_hbm, wout_ref), ("qkv", qkv_hbm, qkv_ref), ("p", p_hbm, p_ref), ("wqkv", wqkv_hbm, wqkv_ref),
        ("x", x_hbm, x_ref), ("att", att_hbm, att_ref), ("n1", n1_hbm, n1_ref),
    )):
        loads[name] = pltpu.make_async_copy(source, target, in_sems.at[i])
        loads[name].start()

    gain1 = g1_ref[...]
    gain2 = g2_ref[...]
    dg2_ref[...] = jnp.zeros_like(dg2_ref)
    tokens = cot_ref.shape[0]
    for name in ("cot", "mid", "down", "dn2"):
        loads[name].wait()

    @pl.loop(0, tokens // WIN)
    def _(b):
        rows = pl.ds(pl.multiple_of(b * WIN, WIN), WIN)
        mid = mid_ref[rows, :].astype(F32)
        res_ref[rows, :] = (mid + down_ref[rows, :]).astype(BF16)
        xhat, scale = normalised(mid)
        dn2 = dn2_ref[rows, :].astype(BF16).astype(F32)
        dg2_ref[...] += jnp.sum(dn2 * xhat, axis=0, keepdims=True)
        dmid = cot_ref[rows, :].astype(F32) + norm_pullback(xhat, scale, gain2, dn2)
        dmid_ref[rows, :] = dmid.astype(BF16)

    for band in range(BANDS):
        for side in range(SIDES):
            w = band * SIDES + side
            res_buf[band, side] = res_ref[w * WIN:(w + 1) * WIN, :].reshape(WLAT, WLON, LEV, D)
    res_copies = scatter_windows(0, res_buf, out_ref, lon_ref, lat_ref, corner_ref, sems.at[0])
    for copy in res_copies:
        copy.start()

    loads["wout"].wait()

    @pl.loop(0, tokens // ROWS)
    def _(b):
        rows = pl.ds(pl.multiple_of(b * ROWS, ROWS), ROWS)
        datt_ref[rows, :] = mm_t(dmid_ref[rows, :], wout_ref[...]).astype(BF16)

    loads["qkv"].wait()
    loads["p"].wait()
    att_back(0, tokens // WIN, datt_ref, qkv_ref, p_ref, dqkv_ref)

    dg1_ref[...] = jnp.zeros_like(dg1_ref)
    loads["wqkv"].wait()
    loads["x"].wait()

    @pl.loop(0, tokens // ROWS)
    def _(b):
        rows = pl.ds(pl.multiple_of(b * ROWS, ROWS), ROWS)
        dn1 = mm_t(dqkv_ref[rows, :], wqkv_ref[...]).astype(BF16).astype(F32)
        xhat, scale = normalised(x_ref[rows, :].astype(F32))
        dg1_ref[...] += jnp.sum(dn1 * xhat, axis=0, keepdims=True)
        dx = dmid_ref[rows, :].astype(F32) + norm_pullback(xhat, scale, gain1, dn1)
        dx_ref[rows, :] = dx.astype(BF16)

    for band in range(BANDS):
        for side in range(SIDES):
            w = band * SIDES + side
            dx_buf[band, side] = dx_ref[w * WIN:(w + 1) * WIN, :].reshape(WLAT, WLON, LEV, D)
    dx_copies = scatter_windows(1, dx_buf, grad_ref, lon_ref, lat_ref, corner_ref, sems.at[1])
    for copy in dx_copies:
        copy.start()
    loads["att"].wait()
    loads["n1"].wait()
    att_grads(1 - me_ref[0], n1_ref, dqkv_ref, att_ref, dmid_ref, dg1_ref[...], dg2_ref[...], send_ref)
    for copy in res_copies + dx_copies:
        copy.wait()


def keep_kernel(me_ref, n1_ref, dqkv_ref, att_ref, dmid_ref, dg1_ref, dg2_ref, keep_ref):
    att_grads(me_ref[0], n1_ref, dqkv_ref, att_ref, dmid_ref, dg1_ref[...], dg2_ref[...], keep_ref)


def total_of(parts_ref, rows):
    total = parts_ref[0, rows, :].astype(F32)
    for chip in range(1, CHIPS_N):
        total += parts_ref[chip, rows, :].astype(F32)
    return total.astype(BF16)


SHARE = FF // CHIPS_N
MIXED = SLOTS + SHARE * D // 128


def lane_blocks():
    return [(slice(SLOTS + i * SHARE, SLOTS + (i + 1) * SHARE), slice(i * 128, (i + 1) * 128)) for i in range(D // 128)]


def merge_kernel(parts_ref, keep_ref, got_ref, out_ref):
    total = total_of(parts_ref, slice(0, SHARE))
    for chip in range(CHIPS_N):
        both = keep_ref[chip].astype(F32) + got_ref[chip].astype(F32)
        out_ref[chip, 0:SLOTS, :] = both.astype(BF16)
        for rows, lanes in lane_blocks():
            out_ref[chip, rows, :] = total[:, lanes]


def share_kernel(parts_ref, out_ref):
    total = total_of(parts_ref, slice(0, SLOTS))
    for chip in range(CHIPS_N):
        out_ref[chip] = total


def compact_kernel(parts_ref, after_ref, done_ref):
    del after_ref
    for chip in range(CHIPS_N):
        for rows, lanes in lane_blocks():
            done_ref[chip * SHARE:(chip + 1) * SHARE, lanes] = parts_ref[chip, rows, :]


def unpack_mlp_kernel(me_ref, mine_ref, theirs_ref, gup_ref, gdown_ref):
    wide = FF // 2
    for ref, half in ((mine_ref, me_ref[0]), (theirs_ref, 1 - me_ref[0])):
        for block in range(2):
            lanes = pl.ds(pl.multiple_of(half * wide + block * D, D), D)
            gup_ref[:, lanes] = ref[block * D:(block + 1) * D, :].astype(F32)
        gdown_ref[pl.ds(pl.multiple_of(half * wide, wide), wide), :] = ref[2 * D:, :].astype(F32)


def unpack_att_kernel(me_ref, mine_ref, theirs_ref, gqkv_ref, gout_ref, gains_ref):
    quarter = CHIPS_N // 4
    per = D // quarter
    for ref, half in ((mine_ref, me_ref[0]), (theirs_ref, 1 - me_ref[0])):
        for part in range(4):
            for block in range(2):
                piece = ref[part * quarter:(part + 1) * quarter, block * per:(block + 1) * per, :]
                piece = piece.reshape(D, 128).astype(F32)
                out, first = (gqkv_ref, part * D) if part < 3 else (gout_ref, 0)
                out[:, pl.ds(pl.multiple_of(half * HALF + (first + block * 128), 128), 128)] = piece
        for block in range(D // 128):
            gains_ref[pl.ds(pl.multiple_of(half * 8, 8), 8), block * 128:(block + 1) * 128] = ref[block, 2 * per:, :].astype(F32)


def pack_kernel(tok_ref, cot_ref, lon_ref, lat_ref, corner_ref, sems):
    copies = []
    for which, ref in enumerate((tok_ref, cot_ref)):
        below, right = pl.ds(HALF_LAT, ref.shape[0] - HALF_LAT), pl.ds(HALF_LON, ref.shape[1] - HALF_LON)
        top, left = pl.ds(0, HALF_LAT), pl.ds(0, HALF_LON)
        for i, (rows, cols, out) in enumerate(((below, left, lon_ref), (top, right, lat_ref), (top, left, corner_ref))):
            copies.append(pltpu.make_async_copy(ref.at[rows, cols], out.at[which], sems.at[which, i]))
    for copy in copies:
        copy.start()
    for copy in copies:
        copy.wait()


def place_kernel(out_in, grad_in, lon_ref, lat_ref, corner_ref, out_ref, grad_ref, sems):
    del out_in, grad_in
    copies = []
    for which, ref in enumerate((out_ref, grad_ref)):
        below, right = pl.ds(HALF_LAT, ref.shape[0] - HALF_LAT), pl.ds(HALF_LON, ref.shape[1] - HALF_LON)
        top, left = pl.ds(0, HALF_LAT), pl.ds(0, HALF_LON)
        for i, (rows, cols, rim) in enumerate(((below, left, lon_ref), (top, right, lat_ref), (top, left, corner_ref))):
            copies.append(pltpu.make_async_copy(rim.at[which], ref.at[rows, cols], sems.at[which, i]))
    for copy in copies:
        copy.start()
    for copy in copies:
        copy.wait()


def params(mib=32):
    return pltpu.CompilerParams(vmem_limit_bytes=mib * 2**20)


def cost(flops, moved):
    return pl.CostEstimate(flops=flops, bytes_accessed=moved, transcendentals=0)


def shape(dims, dtype=BF16):
    return jax.ShapeDtypeStruct(dims, dtype)


SM = pl.BlockSpec(memory_space=pltpu.SMEM)
VM = pl.BlockSpec(memory_space=pltpu.VMEM)


ANY = pl.BlockSpec(memory_space=pl.ANY)
HB = pl.BlockSpec(memory_space=pltpu.HBM)


def rim_shapes(rows, cols, levels):
    return [
        shape((2, rows - HALF_LAT, HALF_LON, levels, D)),
        shape((2, HALF_LAT, cols - HALF_LON, levels, D)),
        shape((2, HALF_LAT, HALF_LON, levels, D)),
    ]


def pack(tokens, cotangent):
    return pl.pallas_call(
        pack_kernel,
        name="pack",
        in_specs=[ANY] * 2,
        out_specs=[VM] * 3,
        out_shape=rim_shapes(*tokens.shape[:3]),
        scratch_shapes=[pltpu.SemaphoreType.DMA((2, 3))],
    )(tokens, cotangent)


def place(output, grad, lon, lat, corner):
    return pl.pallas_call(
        place_kernel,
        name="place",
        in_specs=[ANY] * 2 + [VM] * 3,
        out_specs=[ANY] * 2,
        out_shape=[shape(output.shape), shape(grad.shape)],
        input_output_aliases={0: 0, 1: 1},
        scratch_shapes=[pltpu.SemaphoreType.DMA((2, 3))],
        cost_estimate=cost(10**9, 2**21),
    )(output, grad, lon, lat, corner)


WINDOWED = (BANDS, SIDES, WLAT, WLON, LEV, D)


def local(dims, dtype=BF16):
    return pltpu.VMEM(dims, dtype)


def held(*arrays):
    return [pltpu.with_memory_space_constraint(array, pltpu.VMEM) for array in arrays]


def far(*arrays):
    return [pltpu.with_memory_space_constraint(array, pltpu.HBM) for array in arrays]


def front(flag, tok, cot, lon, lat, corner, g1, wqkv, wout, g2):
    tokens = tok.size // D
    count = tokens // WIN
    saved = [(tokens, D), (tokens, D), (tokens, 3 * D), (count, D // HD, WIN, WIN), (tokens, D), (tokens, D)]
    return pl.pallas_call(
        front_kernel,
        name="front",
        in_specs=[SM] + [ANY] * 5 + [VM, HB, HB, VM],
        out_specs=[HB] * 7 + [VM] * 2,
        out_shape=[pltpu.HBM(dims, BF16) for dims in saved + [(tokens, D)]] + [local((tokens, D)), local((tokens, D))],
        scratch_shapes=[
            pltpu.VMEM(WINDOWED, BF16),
            pltpu.VMEM(WINDOWED, BF16),
        ] + [pltpu.VMEM(dims, BF16) for dims in saved] + [
            pltpu.VMEM((D, 3 * D), BF16),
            pltpu.VMEM((D, D), BF16),
            pltpu.SemaphoreType.DMA((2, STRIPS)),
            pltpu.SemaphoreType.DMA((SAVES + count,)),
            pltpu.SemaphoreType.DMA((2,)),
        ],
        compiler_params=params(),
        cost_estimate=cost(15 * 10**9, 10 * 2**20),
    )(flag, tok, cot, lon, lat, corner, g1, *far(wqkv, wout), g2)


def mlp(kind, me, n2, cot, wup, wdown, *carried):
    tokens = n2.shape[0]
    sums = [local((tokens, D), F32)] * 2
    scratch = [pltpu.VMEM((tokens, CHUNK), BF16)] * 2
    out_specs, aliases = [VM] * 3, {}
    if kind == "send":
        kernel, out_shape = send_kernel, sums + [shape((FF, D))]
    elif kind == "first":
        kernel, out_shape = keep_first_kernel, sums + [local((2 * CHUNK, D))]
        aliases = {5: 0, 6: 1}
    else:
        kernel, out_shape = keep_second_kernel, [pltpu.HBM((tokens, D), F32)] * 2 + [pltpu.HBM((FF, D), BF16)]
        out_specs = [HB, HB, VM]
        scratch = scratch + [pltpu.VMEM((tokens, D), F32)] * 2 + [pltpu.SemaphoreType.DMA((2,))]
    return pl.pallas_call(
        kernel,
        name="mlp_" + kind,
        in_specs=[SM, VM, VM, VM, VM] + [VM] * len(carried),
        out_specs=out_specs,
        out_shape=out_shape,
        scratch_shapes=scratch,
        input_output_aliases=aliases,
        compiler_params=params(),
        cost_estimate=cost((16 if kind == "send" else 8) * 10**9, 10 * 2**20),
    )(me, *held(n2, cot, wup, wdown, *carried))


def back(me, cot, mid, down, dn2, wout, qkv, p, wqkv, x, att, n1, g1, g2, field):
    tokens = x.shape[0]
    count = tokens // WIN
    return pl.pallas_call(
        back_kernel,
        name="back",
        in_specs=[SM] + [HB] * 11 + [VM] * 2,
        out_specs=[ANY] * 5 + [VM] * 7,
        out_shape=[shape(field), shape(field)] + rim_shapes(*field[:3]) + [
            local((tokens, D)),
            local((tokens, D)),
            local((tokens, D)),
            local((tokens, 3 * D)),
            local((1, D), F32),
            local((1, D), F32),
            shape((CHIPS_N, SLOTS, 128)),
        ],
        scratch_shapes=[
            pltpu.VMEM((tokens, D), BF16),
            pltpu.VMEM((tokens, D), BF16),
            pltpu.VMEM((tokens, D), F32),
            pltpu.VMEM((tokens, D), F32),
            pltpu.VMEM((D, D), BF16),
            pltpu.VMEM((tokens, 3 * D), BF16),
            pltpu.VMEM((count, D // HD, WIN, WIN), BF16),
            pltpu.VMEM((D, 3 * D), BF16),
            pltpu.VMEM((tokens, D), BF16),
            pltpu.VMEM((tokens, D), BF16),
            pltpu.VMEM((tokens, D), BF16),
            pltpu.VMEM((tokens, D), BF16),
            pltpu.VMEM(WINDOWED, BF16),
            pltpu.VMEM(WINDOWED, BF16),
            pltpu.SemaphoreType.DMA((11,)),
            pltpu.SemaphoreType.DMA((2, STRIPS)),
        ],
        compiler_params=params(40),
        cost_estimate=cost(30 * 10**9, 10 * 2**20),
    )(me, *far(cot, mid, down, dn2, wout, qkv, p, wqkv, x, att, n1), g1, g2)


def keep_grads(me, n1, dqkv, att, dmid, dg1, dg2):
    return pl.pallas_call(
        keep_kernel,
        name="keep",
        in_specs=[SM] + [VM] * 6,
        out_specs=VM,
        out_shape=shape((CHIPS_N, SLOTS, 128)),
        compiler_params=params(),
        cost_estimate=cost(4 * 10**9, 4 * 2**20),
    )(me, *held(n1, dqkv, att, dmid, dg1, dg2))


def simple(kernel, name, out_shape, *operands, moved=4 * 2**20, mib=56):
    return pl.pallas_call(
        kernel,
        name=name,
        in_specs=[VM] * len(operands),
        out_specs=VM,
        out_shape=out_shape,
        compiler_params=params(mib),
        cost_estimate=cost(10**9, moved),
    )(*operands)


def unpack_mlp(me, mine, theirs):
    return pl.pallas_call(
        unpack_mlp_kernel,
        name="unpack_mlp",
        in_specs=[SM] + [VM] * 2,
        out_specs=[VM, VM],
        out_shape=[shape((D, FF), F32), shape((FF, D), F32)],
        compiler_params=params(56),
        cost_estimate=cost(10**9, 12 * 2**20),
    )(me, mine, theirs)


def unpack_att(me, mine, theirs):
    return pl.pallas_call(
        unpack_att_kernel,
        name="unpack_att",
        in_specs=[SM, VM, VM],
        out_specs=[VM] * 3,
        out_shape=[shape((D, 3 * D), F32), shape((D, D), F32), shape((16, D), F32)],
        compiler_params=params(),
        cost_estimate=cost(10**9, 6 * 2**20),
    )(me, mine, theirs)


LAT = ("x", "zl")
LON = ("zh", "y", "c")
CHIPS = ("x", "zl", "zh", "y")


def send_rims(lon, lat, corner, distance):
    lats, lons = lax.axis_size(LAT), lax.axis_size(LON)
    moved = []
    for block, down, across in ((lon, 0, distance), (lat, distance, 0), (corner, distance, distance)):
        route = [
            (i * lons + j, (i + down) % lats * lons + (j + across) % lons)
            for i in range(lats) for j in range(lons)
        ]
        moved.append(lax.ppermute(block, LAT + LON, route))
    return moved


def other_core(block):
    return lax.ppermute(block, "c", [(0, 1), (1, 0)])


def exchange(parts):
    return lax.all_to_all(parts, CHIPS, 0, 0, tiled=True)


def shards(tokens, cotangent, norm_gain, w_qkv, w_out, mlp_gain, w_up, w_down):
    g1 = norm_gain.reshape(1, D)
    g2 = mlp_gain.reshape(1, D)
    last_band = lax.axis_index(LAT) == lax.axis_size(LAT) - 1
    flag = last_band.astype(jnp.int32).reshape(1)
    me = lax.axis_index("c").astype(jnp.int32).reshape(1)

    rims = send_rims(*pack(tokens, cotangent), -1)
    x, n1, qkv, p, att, mid, cot_far, cot, n2 = front(flag, tokens, cotangent, *rims, g1, w_qkv, w_out, g2)
    fixed = (me, n2, cot, w_up, w_down)
    down, dn2, grads = mlp("send", *fixed)
    got = other_core(grads)
    down, dn2, early = mlp("first", *fixed, down, dn2)
    down, dn2, grads = mlp("second", *fixed, down, dn2, early, got)
    sums = exchange(grads.reshape(CHIPS_N, SHARE, D))
    output, grad_tokens, lon, lat, corner, att, n1, dmid, dqkv, dg1, dg2, send = back(
        me, cot_far, mid, down, dn2, w_out, qkv, p, w_qkv, x, att, n1, g1, g2, tokens.shape)
    got = other_core(send)
    rims = send_rims(lon, lat, corner, 1)
    keep = keep_grads(me, n1, dqkv, att, dmid, dg1, dg2)
    output, grad_tokens = place(output, grad_tokens, *rims)
    mixed = exchange(simple(merge_kernel, "merge", pltpu.HBM((CHIPS_N, MIXED, 128), BF16), sums, keep, got))
    mixed, output, grad_tokens = lax.optimization_barrier((mixed, output, grad_tokens))
    share = simple(share_kernel, "share", pltpu.HBM((CHIPS_N, SLOTS, 128), BF16), mixed)
    att_mine = exchange(share)
    mlp_mine = simple(compact_kernel, "compact", shape((FF, D)), mixed, share)
    gup, gdown = unpack_mlp(me, mlp_mine, other_core(mlp_mine))
    att_mine, gup, gdown = lax.optimization_barrier((att_mine, gup, gdown))
    gqkv, gout, gains = unpack_att(me, att_mine, other_core(att_mine))
    return (output, grad_tokens, gains[0], gqkv, gout, gains[8], gup, gdown)


def solution(mesh):
    field = P(LAT, LON, None, None)
    mesh = jax.sharding.Mesh(mesh.devices.reshape(4, 2, 2, 4, 2), ("x", "zl", "zh", "y", "c"))
    return jax.shard_map(
        shards,
        mesh=mesh,
        in_specs=(field, field, P(), P(), P(), P(), P(), P()),
        out_specs=(field, field, P(), P(), P(), P(), P(), P()),
        check_vma=False,
    )
```

```python
import functools

import jax
import jax.numpy as jnp
from jax import lax
from jax.experimental import pallas as pl
from jax.experimental.pallas import tpu as pltpu
from jax.sharding import PartitionSpec as P

HD = 64
WLAT = 6
WLON = 12
LEV = 2
WIN = WLAT * WLON * LEV
D = 512
FF = 2048
HALF_LAT = WLAT // 2
HALF_LON = WLON // 2
EPS = 1e-05
F32 = jnp.float32
BF16 = jnp.bfloat16
PAIR = 2 * HD


def mm(a, b):
    return lax.dot_general(a, b, (((1,), (0,)), ((), ())), preferred_element_type=F32)


def mm_t(a, b):
    return lax.dot_general(a, b, (((1,), (1,)), ((), ())), preferred_element_type=F32)


def t_mm(a, b):
    return lax.dot_general(a, b, (((0,), (0,)), ((), ())), preferred_element_type=F32)


def normalised(values):
    mean = jnp.mean(values, axis=-1, keepdims=True)
    centred = values - mean
    var = jnp.mean(centred * centred, axis=-1, keepdims=True)
    scale = lax.rsqrt(var + EPS)
    return centred * scale, scale


def norm_pullback(xhat, scale, gain, grad):
    dxhat = grad * gain
    m1 = jnp.mean(dxhat, axis=-1, keepdims=True)
    m2 = jnp.mean(dxhat * xhat, axis=-1, keepdims=True)
    return scale * (dxhat - m1 - xhat * m2)


def gelu_parts(x):
    a = jnp.abs(x)
    t = 1.0 / (1.0 + (0.3275911 * 0.7071067811865476) * a)
    e = jnp.exp(-0.5 * x * x)
    poly = t * (0.127414796 + t * (-0.142248368 + t * (0.7107068705 + t * (-0.7265760135 + t * 0.5307027145))))
    tail = poly * e
    cdf = jnp.where(x >= 0.0, 1.0 - tail, tail)
    return cdf, 0.3989422804014327 * e


BANDS = 4
SIDES = 2


def strips():
    for band in range(BANDS):
        first = HALF_LAT + band * WLAT
        last = band == BANDS - 1
        across = [(0, WLAT, first, False)]
        if last:
            across = [(0, HALF_LAT, first, False), (HALF_LAT, HALF_LAT, 0, True)]
        for side in range(SIDES):
            left = HALF_LON + side * WLON
            along = [(0, WLON, left, False)]
            if side == SIDES - 1:
                along = [(0, HALF_LON, left, False), (HALF_LON, HALF_LON, 0, True)]
            for at_row, rows, row, far_row in across:
                for at_col, cols, col, far_col in along:
                    piece = 2 * far_row + far_col
                    if far_row and not far_col:
                        col -= HALF_LON
                    if far_col and not far_row:
                        row -= HALF_LAT
                    yield (
                        band, side, pl.ds(at_row, rows), pl.ds(at_col, cols),
                        piece, pl.ds(row, rows), pl.ds(col, cols),
                    )


SAVES = 6
STRIPS = len(list(strips()))


def gather_windows(which, field, rim_lon, rim_lat, corner, buffer, sems):
    copies = []
    for i, (band, side, to_rows, to_cols, piece, rows, cols) in enumerate(strips()):
        source = field if piece == 0 else (None, rim_lon, rim_lat, corner)[piece].at[which]
        copies.append(pltpu.make_async_copy(
            source.at[rows, cols], buffer.at[band, side, to_rows, to_cols], sems.at[i]))
    return copies


def scatter_windows(which, buffer, field, rim_lon, rim_lat, corner, sems):
    copies = []
    for i, (band, side, to_rows, to_cols, piece, rows, cols) in enumerate(strips()):
        target = field if piece == 0 else (None, rim_lon, rim_lat, corner)[piece].at[which]
        copies.append(pltpu.make_async_copy(
            buffer.at[band, side, to_rows, to_cols], target.at[rows, cols], sems.at[i]))
    return copies


def front_kernel(flag_ref, tok_ref, cot_ref, lon_ref, lat_ref, corner_ref, g1_ref, wqkv_hbm, wout_hbm, g2_ref,
                 x_out, n1_out, qkv_out, p_out, att_out, mid_out, cot_out, cotw_ref, n2_ref,
                 tok_buf, cot_buf, x_ref, n1_ref, qkv_ref, p_ref, att_ref, mid_ref, wqkv_ref, wout_ref,
                 sems, out_sems, w_sems):
    wqkv_copy = pltpu.make_async_copy(wqkv_hbm, wqkv_ref, w_sems.at[0])
    wout_copy = pltpu.make_async_copy(wout_hbm, wout_ref, w_sems.at[1])
    saves = []

    def save(source, target):
        copy = pltpu.make_async_copy(source, target, out_sems.at[len(saves)])
        copy.start()
        saves.append(copy)

    tok_copies = gather_windows(0, tok_ref, lon_ref, lat_ref, corner_ref, tok_buf, sems.at[0])
    cot_copies = gather_windows(1, cot_ref, lon_ref, lat_ref, corner_ref, cot_buf, sems.at[1])
    for copy in tok_copies + [wqkv_copy, wout_copy] + cot_copies:
        copy.start()
    for copy in tok_copies:
        copy.wait()
    for band in range(BANDS):
        for side in range(SIDES):
            w = band * SIDES + side
            x_ref[w * WIN:(w + 1) * WIN, :] = tok_buf[band, side].reshape(WIN, D)
    save(x_ref, x_out)
    tokens = x_ref.shape[0]
    count = tokens // WIN
    per_row = count // 4
    gain1 = g1_ref[...]
    gain2 = g2_ref[...]

    @pl.loop(0, count, unroll=2)
    def _(w):
        rows = pl.ds(pl.multiple_of(w * WIN, WIN), WIN)
        xhat, _ = normalised(x_ref[rows, :].astype(F32))
        n1_ref[rows, :] = (xhat * gain1).astype(BF16)

    wqkv_copy.wait()

    big = ROWS

    @pl.loop(0, tokens // big)
    def _(b):
        rows = pl.ds(pl.multiple_of(b * big, big), big)
        n1 = n1_ref[rows, :]
        qkv_ref[rows, 0:D] = (mm(n1, wqkv_ref[:, 0:D]).astype(BF16) * 0.125).astype(BF16)
        qkv_ref[rows, D:2 * D] = mm(n1, wqkv_ref[:, D:2 * D]).astype(BF16)
        qkv_ref[rows, 2 * D:3 * D] = mm(n1, wqkv_ref[:, 2 * D:3 * D]).astype(BF16)

    save(n1_ref, n1_out)
    save(qkv_ref, qkv_out)

    key_group = lax.broadcasted_iota(jnp.int32, (WIN, WIN), 0) >= WIN // 2
    query_group = lax.broadcasted_iota(jnp.int32, (WIN, WIN), 1) >= WIN // 2
    split = key_group != query_group
    low = lax.broadcasted_iota(jnp.int32, (WIN, PAIR), 1) < HD

    @pl.loop(0, count, unroll=4)
    def _(w):
        rows = pl.ds(pl.multiple_of(w * WIN, WIN), WIN)
        cut = jnp.logical_and(flag_ref[0] == 1, w >= count - per_row)
        masked = jnp.logical_and(split, cut)
        for pair in range(D // PAIR):
            lanes = slice(pair * PAIR, (pair + 1) * PAIR)
            q = qkv_ref[rows, pair * PAIR:(pair + 1) * PAIR]
            k = qkv_ref[rows, D + pair * PAIR:D + (pair + 1) * PAIR]
            v = qkv_ref[rows, 2 * D + pair * PAIR:2 * D + (pair + 1) * PAIR]
            outs = []
            for h in range(2):
                mine = low if h == 0 else jnp.logical_not(low)
                kh = jnp.where(mine, k, jnp.zeros_like(k))
                s = mm_t(kh, q)
                s = jnp.where(masked, -1000000000.0, s)
                e = jnp.exp(s - jnp.max(s, axis=0, keepdims=True))
                p = (e * (1.0 / jnp.sum(e, axis=0, keepdims=True))).astype(BF16)
                p_ref[w, 2 * pair + h] = p
                outs.append(t_mm(p, v))
            att_ref[rows, lanes] = jnp.where(low, outs[0], outs[1]).astype(BF16)
        pltpu.make_async_copy(p_ref.at[w], p_out.at[w], out_sems.at[SAVES + w]).start()

    save(att_ref, att_out)
    wout_copy.wait()

    @pl.loop(0, tokens // big)
    def _(b):
        rows = pl.ds(pl.multiple_of(b * big, big), big)
        mid = (x_ref[rows, :].astype(F32) + mm(att_ref[rows, :], wout_ref[...])).astype(BF16)
        mid_ref[rows, :] = mid
        xhat, _ = normalised(mid.astype(F32))
        n2_ref[rows, :] = (xhat * gain2).astype(BF16)

    save(mid_ref, mid_out)
    for copy in cot_copies:
        copy.wait()
    for band in range(BANDS):
        for side in range(SIDES):
            w = band * SIDES + side
            cotw_ref[w * WIN:(w + 1) * WIN, :] = cot_buf[band, side].reshape(WIN, D)
    save(cotw_ref, cot_out)
    for copy in saves:
        copy.wait()
    for w in range(count):
        pltpu.make_async_copy(p_ref.at[w], p_out.at[w], out_sems.at[SAVES + w]).wait()


CHUNK = 512
ROWS = 4 * WIN


def mlp_chunk(chunk, n2_ref, cot_ref, wup_ref, wdown_ref, down_in, dn2_in, down_out, dn2_out, hid_ref, du_ref):
    at = pl.ds(pl.multiple_of(chunk * CHUNK, CHUNK), CHUNK)

    @pl.loop(0, n2_ref.shape[0] // ROWS)
    def _(b):
        rows = pl.ds(pl.multiple_of(b * ROWS, ROWS), ROWS)
        up = mm(n2_ref[rows, :], wup_ref[:, at])
        cdf, pdf = gelu_parts(up)
        hid = (up * cdf).astype(BF16)
        hid_ref[rows, :] = hid
        dhid = mm_t(cot_ref[rows, :], wdown_ref[at, :]).astype(BF16).astype(F32)
        du = (dhid * (cdf + up * pdf)).astype(BF16)
        du_ref[rows, :] = du
        down = mm(hid, wdown_ref[at, :])
        dn2 = mm_t(du, wup_ref[:, at])
        if down_in is None:
            down_out[rows, :] = down
            dn2_out[rows, :] = dn2
        else:
            down_out[rows, :] = down_in[rows, :] + down
            dn2_out[rows, :] = dn2_in[rows, :] + dn2

    return t_mm(n2_ref[...], du_ref[...]).astype(BF16), t_mm(hid_ref[...], cot_ref[...]).astype(BF16)


def send_kernel(me_ref, n2_ref, cot_ref, wup_ref, wdown_ref, down_ref, dn2_ref, grads_ref, hid_ref, du_ref):
    for i in range(2):
        carried = (down_ref, dn2_ref) if i else (None, None)
        grads = mlp_chunk((1 - me_ref[0]) * 2 + i, n2_ref, cot_ref, wup_ref, wdown_ref,
                          *carried, down_ref, dn2_ref, hid_ref, du_ref)
        for part, grad in enumerate(grads):
            grads_ref[(2 * part + i) * CHUNK:(2 * part + i + 1) * CHUNK, :] = grad


def keep_first_kernel(me_ref, n2_ref, cot_ref, wup_ref, wdown_ref, down_in, dn2_in,
                      down_ref, dn2_ref, early_ref, hid_ref, du_ref):
    grads = mlp_chunk(me_ref[0] * 2, n2_ref, cot_ref, wup_ref, wdown_ref,
                      down_in, dn2_in, down_ref, dn2_ref, hid_ref, du_ref)
    for part, grad in enumerate(grads):
        early_ref[part * CHUNK:(part + 1) * CHUNK, :] = grad


def keep_second_kernel(me_ref, n2_ref, cot_ref, wup_ref, wdown_ref, down_in, dn2_in, early_ref, got_ref,
                       down_hbm, dn2_hbm, grads_ref, hid_ref, du_ref, down_ref, dn2_ref, sems):
    grads = mlp_chunk(me_ref[0] * 2 + 1, n2_ref, cot_ref, wup_ref, wdown_ref,
                      down_in, dn2_in, down_ref, dn2_ref, hid_ref, du_ref)
    copies = [
        pltpu.make_async_copy(down_ref, down_hbm, sems.at[0]),
        pltpu.make_async_copy(dn2_ref, dn2_hbm, sems.at[1]),
    ]
    for copy in copies:
        copy.start()
    for part, grad in enumerate(grads):
        for i in range(2):
            rows = slice((2 * part + i) * CHUNK, (2 * part + i + 1) * CHUNK)
            mine = grad if i else early_ref[part * CHUNK:(part + 1) * CHUNK, :]
            grads_ref[rows, :] = (mine.astype(F32) + got_ref[rows, :].astype(F32)).astype(BF16)
    for copy in copies:
        copy.wait()


HALF = D // 2
CHIPS_N = 64
GRADS = 64
GAINS = 8


def att_grads(half, n1_ref, dqkv_ref, att_ref, dmid_ref, out_ref):
    per = D // (CHIPS_N // 4)
    lanes = pl.ds(pl.multiple_of(half * HALF, HALF), HALF)
    for part in range(4):
        if part < 3:
            part_lanes = pl.ds(pl.multiple_of(part * D + half * HALF, HALF), HALF)
            grad = t_mm(n1_ref[...], dqkv_ref[:, part_lanes])
        else:
            grad = t_mm(att_ref[...], dmid_ref[:, lanes])
        grad = grad.astype(BF16)
        first = part * (CHIPS_N // 4)
        for block in range(2):
            piece = grad[:, block * 128:(block + 1) * 128].reshape(CHIPS_N // 4, per, 128)
            out_ref[first:first + CHIPS_N // 4, block * per:(block + 1) * per, :] = piece


def att_back(first, last, datt_ref, qkv_ref, p_ref, dqkv_ref):
    low = lax.broadcasted_iota(jnp.int32, (WIN, PAIR), 1) < HD

    @pl.loop(first, last, unroll=4)
    def _(w):
        rows = pl.ds(pl.multiple_of(w * WIN, WIN), WIN)
        for pair in range(D // PAIR):
            lanes = slice(pair * PAIR, (pair + 1) * PAIR)
            q = qkv_ref[rows, pair * PAIR:(pair + 1) * PAIR]
            k = qkv_ref[rows, D + pair * PAIR:D + (pair + 1) * PAIR]
            v = qkv_ref[rows, 2 * D + pair * PAIR:2 * D + (pair + 1) * PAIR]
            da = datt_ref[rows, lanes]
            dqs, dks, dvs = [], [], []
            for h in range(2):
                mine = low if h == 0 else jnp.logical_not(low)
                vh = jnp.where(mine, v, jnp.zeros_like(v))
                p = p_ref[w, 2 * pair + h]
                pf = p.astype(F32)
                dp = mm_t(vh, da).astype(BF16).astype(F32)
                ds = (pf * (dp - jnp.sum(dp * pf, axis=0, keepdims=True))).astype(BF16)
                dvs.append(mm(p, da))
                dks.append(mm(ds, q))
                dqs.append(t_mm(ds, k))
            dqkv_ref[rows, pair * PAIR:(pair + 1) * PAIR] = (jnp.where(low, dqs[0], dqs[1]) * 0.125).astype(BF16)
            dqkv_ref[rows, D + pair * PAIR:D + (pair + 1) * PAIR] = jnp.where(low, dks[0], dks[1]).astype(BF16)
            dqkv_ref[rows, 2 * D + pair * PAIR:2 * D + (pair + 1) * PAIR] = jnp.where(low, dvs[0], dvs[1]).astype(BF16)


def start_loads(pairs, sems):
    loads = []
    for i, (source, target) in enumerate(pairs):
        loads.append(pltpu.make_async_copy(source, target, sems.at[i]))
        loads[-1].start()
    return loads


def back_kernel(cot_hbm, mid_hbm, down_hbm, dn2_hbm, wout_hbm, qkv_hbm, p_hbm, att_hbm, n1_hbm, g2_ref,
                res_out, dmid_out, dqkv_out, dg2_ref, att_ref, n1_ref, dmid_ref, dqkv_ref,
                cot_ref, mid_ref, down_ref, dn2_ref, wout_ref, qkv_ref, p_ref, datt_ref, res_ref, in_sems, sems):
    loads = start_loads((
        (cot_hbm, cot_ref), (mid_hbm, mid_ref), (down_hbm, down_ref), (dn2_hbm, dn2_ref),
        (wout_hbm, wout_ref), (qkv_hbm, qkv_ref), (p_hbm, p_ref), (att_hbm, att_ref), (n1_hbm, n1_ref),
    ), in_sems)
    gain2 = g2_ref[...]
    dg2_ref[...] = jnp.zeros_like(dg2_ref)
    tokens = cot_ref.shape[0]
    for load in loads[:4]:
        load.wait()

    @pl.loop(0, tokens // WIN, unroll=2)
    def _(b):
        rows = pl.ds(pl.multiple_of(b * WIN, WIN), WIN)
        mid = mid_ref[rows, :].astype(F32)
        res_ref[rows, :] = (mid + down_ref[rows, :]).astype(BF16)
        xhat, scale = normalised(mid)
        dn2 = dn2_ref[rows, :].astype(BF16).astype(F32)
        dg2_ref[...] += jnp.sum(dn2 * xhat, axis=0, keepdims=True)
        dmid = cot_ref[rows, :].astype(F32) + norm_pullback(xhat, scale, gain2, dn2)
        dmid_ref[rows, :] = dmid.astype(BF16)

    saves = [
        pltpu.make_async_copy(res_ref, res_out, sems.at[0]),
        pltpu.make_async_copy(dmid_ref, dmid_out, sems.at[1]),
    ]
    for copy in saves:
        copy.start()
    loads[4].wait()

    @pl.loop(0, tokens // ROWS)
    def _(b):
        rows = pl.ds(pl.multiple_of(b * ROWS, ROWS), ROWS)
        datt_ref[rows, :] = mm_t(dmid_ref[rows, :], wout_ref[...]).astype(BF16)

    loads[5].wait()
    loads[6].wait()
    att_back(0, tokens // WIN, datt_ref, qkv_ref, p_ref, dqkv_ref)
    saves.append(pltpu.make_async_copy(dqkv_ref, dqkv_out, sems.at[2]))
    saves[-1].start()
    for copy in loads[7:] + saves:
        copy.wait()


def tokens_kernel(dqkv_hbm, wqkv_hbm, x_hbm, dmid_hbm, res_hbm, g1_ref, after_ref,
                  out_ref, grad_ref, lon_ref, lat_ref, corner_ref, dg1_ref,
                  dqkv_ref, wqkv_ref, x_ref, dmid_ref, res_ref, dx_ref, res_buf, dx_buf, in_sems, sems):
    loads = start_loads((
        (res_hbm, res_ref), (dqkv_hbm, dqkv_ref), (wqkv_hbm, wqkv_ref), (x_hbm, x_ref), (dmid_hbm, dmid_ref),
    ), in_sems)
    gain1 = g1_ref[...]
    tokens = x_ref.shape[0]
    dg1_ref[...] = jnp.zeros_like(dg1_ref)
    loads[0].wait()
    for band in range(BANDS):
        for side in range(SIDES):
            w = band * SIDES + side
            res_buf[band, side] = res_ref[w * WIN:(w + 1) * WIN, :].reshape(WLAT, WLON, LEV, D)
    res_copies = scatter_windows(0, res_buf, out_ref, lon_ref, lat_ref, corner_ref, sems.at[0])
    for copy in res_copies:
        copy.start()
    for load in loads[1:]:
        load.wait()

    @pl.loop(0, tokens // ROWS)
    def _(b):
        rows = pl.ds(pl.multiple_of(b * ROWS, ROWS), ROWS)
        dn1 = mm_t(dqkv_ref[rows, :], wqkv_ref[...]).astype(BF16).astype(F32)
        xhat, scale = normalised(x_ref[rows, :].astype(F32))
        dg1_ref[...] += jnp.sum(dn1 * xhat, axis=0, keepdims=True)
        dx = dmid_ref[rows, :].astype(F32) + norm_pullback(xhat, scale, gain1, dn1)
        dx_ref[rows, :] = dx.astype(BF16)

    for band in range(BANDS):
        for side in range(SIDES):
            w = band * SIDES + side
            dx_buf[band, side] = dx_ref[w * WIN:(w + 1) * WIN, :].reshape(WLAT, WLON, LEV, D)
    dx_copies = scatter_windows(1, dx_buf, grad_ref, lon_ref, lat_ref, corner_ref, sems.at[1])
    for copy in dx_copies:
        copy.start()
    for copy in res_copies + dx_copies:
        copy.wait()


SHARE = FF // CHIPS_N
MLP = SHARE * D // 128
ALL = GRADS + GAINS + MLP


def total_of(parts_ref, rows):
    total = parts_ref[0, rows, :].astype(F32)
    for chip in range(1, CHIPS_N):
        total += parts_ref[chip, rows, :].astype(F32)
    return total.astype(BF16)


def half_kernel(half_ref, n1_ref, dqkv_ref, att_ref, dmid_ref, out_ref):
    att_grads(half_ref[0], n1_ref, dqkv_ref, att_ref, dmid_ref, out_ref)


def add_kernel(keep_ref, got_ref, out_ref):
    for chip in range(CHIPS_N):
        out_ref[chip] = (keep_ref[chip].astype(F32) + got_ref[chip].astype(F32)).astype(BF16)


def share_mlp_kernel(sums_ref, after_ref, tile_ref):
    del after_ref
    total = total_of(sums_ref, slice(0, SHARE))
    for block in range(D // 128):
        tile_ref[block * SHARE:(block + 1) * SHARE, :] = total[:, block * 128:(block + 1) * 128]


def share_kernel(parts_hbm, tile_ref, dg1_ref, dg2_ref, out_ref, parts_ref, share_ref, sem, sems):
    load = pltpu.make_async_copy(parts_hbm, parts_ref, sem)
    load.start()
    share_ref[GRADS + GAINS:, :] = tile_ref[...]
    share_ref[GRADS:GRADS + GAINS, :] = jnp.concatenate(
        [ref[:, block * 128:(block + 1) * 128] for ref in (dg1_ref, dg2_ref) for block in range(D // 128)]).astype(BF16)
    load.wait()
    share_ref[0:GRADS, :] = total_of(parts_ref, slice(0, GRADS))
    copies = [pltpu.make_async_copy(share_ref, out_ref.at[chip], sems.at[chip]) for chip in range(CHIPS_N)]
    for copy in copies:
        copy.start()
    for copy in copies:
        copy.wait()


def unpack_kernel(mine, half_ref, all_ref, gains_in, *refs):
    (gup_hbm, gdown_hbm, gqkv_hbm, gout_hbm, gains_ref, gup_ref, gdown_ref, att_ref, sems) = refs if mine else refs[4:]
    half = half_ref[0]
    wide = FF // 2
    copies = []

    def send(source, target):
        copies.append(pltpu.make_async_copy(source, target, sems.at[len(copies)]))
        copies[-1].start()

    blocks = [(slice(GRADS + GAINS + i * SHARE, GRADS + GAINS + (i + 1) * SHARE), i * 128) for i in range(D // 128)]
    quarter = CHIPS_N // 4
    for rows, lane in blocks:
        gdown_ref[:, lane:lane + 128] = all_ref[2 * quarter:, rows, :].reshape(wide, 128).astype(F32)
    send(gdown_ref, gdown_hbm.at[pl.ds(pl.multiple_of(half * wide, wide), wide), :])
    for j in range(2):
        for rows, lane in blocks:
            piece = all_ref[j * quarter:(j + 1) * quarter, rows, :].reshape(D, 128)
            gup_ref[:, j * D + lane:j * D + lane + 128] = piece.astype(F32)
    send(gup_ref, gup_hbm.at[:, pl.ds(pl.multiple_of(half * wide, wide), wide)])
    per = GRADS // 2
    for part in range(4):
        for block in range(2):
            piece = all_ref[part * quarter:(part + 1) * quarter, block * per:(block + 1) * per, :].reshape(D, 128)
            att_ref[part, :, block * 128:(block + 1) * 128] = piece.astype(F32)
        out, first = (gqkv_hbm, part * D) if part < 3 else (gout_hbm, 0)
        send(att_ref.at[part], out.at[:, pl.ds(pl.multiple_of(half * HALF + first, HALF), HALF)])
    gains = all_ref[0, GRADS:GRADS + GAINS, :].astype(F32)
    for chip in range(1, CHIPS_N):
        gains += all_ref[chip, GRADS:GRADS + GAINS, :].astype(F32)
    gains_ref[...] = gains if mine else gains_in[...] + gains
    for copy in copies:
        copy.wait()


def pack_kernel(tok_ref, cot_ref, lon_ref, lat_ref, corner_ref, sems):
    copies = []
    for which, ref in enumerate((tok_ref, cot_ref)):
        below, right = pl.ds(HALF_LAT, ref.shape[0] - HALF_LAT), pl.ds(HALF_LON, ref.shape[1] - HALF_LON)
        top, left = pl.ds(0, HALF_LAT), pl.ds(0, HALF_LON)
        for i, (rows, cols, out) in enumerate(((below, left, lon_ref), (top, right, lat_ref), (top, left, corner_ref))):
            copies.append(pltpu.make_async_copy(ref.at[rows, cols], out.at[which], sems.at[which, i]))
    for copy in copies:
        copy.start()
    for copy in copies:
        copy.wait()


def place_kernel(out_in, grad_in, lon_ref, lat_ref, corner_ref, after_ref, out_ref, grad_ref, sems):
    del out_in, grad_in, after_ref
    copies = []
    for which, ref in enumerate((out_ref, grad_ref)):
        below, right = pl.ds(HALF_LAT, ref.shape[0] - HALF_LAT), pl.ds(HALF_LON, ref.shape[1] - HALF_LON)
        top, left = pl.ds(0, HALF_LAT), pl.ds(0, HALF_LON)
        for i, (rows, cols, rim) in enumerate(((below, left, lon_ref), (top, right, lat_ref), (top, left, corner_ref))):
            copies.append(pltpu.make_async_copy(rim.at[which], ref.at[rows, cols], sems.at[which, i]))
    for copy in copies:
        copy.start()
    for copy in copies:
        copy.wait()


def params(mib=32):
    return pltpu.CompilerParams(vmem_limit_bytes=mib * 2**20)


def cost(flops, moved):
    return pl.CostEstimate(flops=flops, bytes_accessed=moved, transcendentals=0)


def shape(dims, dtype=BF16):
    return jax.ShapeDtypeStruct(dims, dtype)


SM = pl.BlockSpec(memory_space=pltpu.SMEM)
VM = pl.BlockSpec(memory_space=pltpu.VMEM)


ANY = pl.BlockSpec(memory_space=pl.ANY)
HB = pl.BlockSpec(memory_space=pltpu.HBM)


def rim_shapes(rows, cols, levels):
    return [
        shape((2, rows - HALF_LAT, HALF_LON, levels, D)),
        shape((2, HALF_LAT, cols - HALF_LON, levels, D)),
        shape((2, HALF_LAT, HALF_LON, levels, D)),
    ]


def pack(tokens, cotangent):
    return pl.pallas_call(
        pack_kernel,
        name="pack",
        in_specs=[ANY] * 2,
        out_specs=[VM] * 3,
        out_shape=[local(rim.shape) for rim in rim_shapes(*tokens.shape[:3])],
        scratch_shapes=[pltpu.SemaphoreType.DMA((2, 3))],
    )(tokens, cotangent)


def place(output, grad, lon, lat, corner, after):
    return pl.pallas_call(
        place_kernel,
        name="place",
        in_specs=[ANY] * 2 + [VM] * 3 + [ANY],
        out_specs=[ANY] * 2,
        out_shape=[shape(output.shape), shape(grad.shape)],
        input_output_aliases={0: 0, 1: 1},
        scratch_shapes=[pltpu.SemaphoreType.DMA((2, 3))],
        cost_estimate=cost(10**9, 2**21),
    )(output, grad, lon, lat, corner, after)


WINDOWED = (BANDS, SIDES, WLAT, WLON, LEV, D)


def local(dims, dtype=BF16):
    return pltpu.VMEM(dims, dtype)


def held(*arrays):
    return [pltpu.with_memory_space_constraint(array, pltpu.VMEM) for array in arrays]


def far(*arrays):
    return [pltpu.with_memory_space_constraint(array, pltpu.HBM) for array in arrays]


def front(flag, tok, cot, lon, lat, corner, g1, wqkv, wout, g2):
    tokens = tok.size // D
    count = tokens // WIN
    saved = [(tokens, D), (tokens, D), (tokens, 3 * D), (count, D // HD, WIN, WIN), (tokens, D), (tokens, D)]
    return pl.pallas_call(
        front_kernel,
        name="front",
        in_specs=[SM] + [ANY] * 5 + [VM, HB, HB, VM],
        out_specs=[HB] * 7 + [VM] * 2,
        out_shape=[pltpu.HBM(dims, BF16) for dims in saved + [(tokens, D)]] + [local((tokens, D)), local((tokens, D))],
        scratch_shapes=[
            pltpu.VMEM(WINDOWED, BF16),
            pltpu.VMEM(WINDOWED, BF16),
        ] + [pltpu.VMEM(dims, BF16) for dims in saved] + [
            pltpu.VMEM((D, 3 * D), BF16),
            pltpu.VMEM((D, D), BF16),
            pltpu.SemaphoreType.DMA((2, STRIPS)),
            pltpu.SemaphoreType.DMA((SAVES + count,)),
            pltpu.SemaphoreType.DMA((2,)),
        ],
        compiler_params=params(),
        cost_estimate=cost(15 * 10**9, 10 * 2**20),
    )(flag, tok, cot, lon, lat, corner, g1, *far(wqkv, wout), g2)


def mlp(kind, me, n2, cot, wup, wdown, *carried):
    tokens = n2.shape[0]
    sums = [local((tokens, D), F32)] * 2
    scratch = [pltpu.VMEM((tokens, CHUNK), BF16)] * 2
    out_specs, aliases = [VM] * 3, {}
    if kind == "send":
        kernel, out_shape = send_kernel, sums + [shape((FF, D))]
    elif kind == "first":
        kernel, out_shape = keep_first_kernel, sums + [local((2 * CHUNK, D))]
        aliases = {5: 0, 6: 1}
    else:
        kernel, out_shape = keep_second_kernel, [pltpu.HBM((tokens, D), F32)] * 2 + [pltpu.HBM((FF, D), BF16)]
        out_specs = [HB, HB, VM]
        scratch = scratch + [pltpu.VMEM((tokens, D), F32)] * 2 + [pltpu.SemaphoreType.DMA((2,))]
    return pl.pallas_call(
        kernel,
        name="mlp_" + kind,
        in_specs=[SM, VM, VM, VM, VM] + [VM] * len(carried),
        out_specs=out_specs,
        out_shape=out_shape,
        scratch_shapes=scratch,
        input_output_aliases=aliases,
        compiler_params=params(),
        cost_estimate=cost((16 if kind == "send" else 8) * 10**9, 10 * 2**20),
    )(me, *held(n2, cot, wup, wdown, *carried))


def back(cot, mid, down, dn2, wout, qkv, p, att, n1, g2):
    tokens = cot.shape[0]
    count = tokens // WIN
    halves = pltpu.VMEM((tokens, D), BF16)
    full = pltpu.VMEM((tokens, D), F32)
    return pl.pallas_call(
        back_kernel,
        name="back",
        in_specs=[HB] * 9 + [VM],
        out_specs=[HB] * 3 + [VM] * 5,
        out_shape=[
            pltpu.HBM((tokens, D), BF16),
            pltpu.HBM((tokens, D), BF16),
            pltpu.HBM((tokens, 3 * D), BF16),
            shape((1, D), F32),
            local((tokens, D)),
            local((tokens, D)),
            local((tokens, D)),
            local((tokens, 3 * D)),
        ],
        scratch_shapes=[
            halves,
            halves,
            full,
            full,
            pltpu.VMEM((D, D), BF16),
            pltpu.VMEM((tokens, 3 * D), BF16),
            pltpu.VMEM((count, D // HD, WIN, WIN), BF16),
            halves,
            halves,
            pltpu.SemaphoreType.DMA((9,)),
            pltpu.SemaphoreType.DMA((3,)),
        ],
        compiler_params=params(40),
        cost_estimate=cost(25 * 10**9, 10 * 2**20),
    )(*far(cot, mid, down, dn2, wout, qkv, p, att, n1), g2)


def token_grads(dqkv, wqkv, x, dmid, res, g1, after, field):
    tokens = x.shape[0]
    halves = pltpu.VMEM((tokens, D), BF16)
    return pl.pallas_call(
        tokens_kernel,
        name="tokens",
        in_specs=[HB] * 5 + [VM, ANY],
        out_specs=[ANY] * 5 + [VM],
        out_shape=[shape(field), shape(field)] + rim_shapes(*field[:3]) + [shape((1, D), F32)],
        scratch_shapes=[
            pltpu.VMEM((tokens, 3 * D), BF16),
            pltpu.VMEM((D, 3 * D), BF16),
            halves,
            halves,
            halves,
            halves,
            pltpu.VMEM(WINDOWED, BF16),
            pltpu.VMEM(WINDOWED, BF16),
            pltpu.SemaphoreType.DMA((5,)),
            pltpu.SemaphoreType.DMA((2, STRIPS)),
        ],
        compiler_params=params(),
        cost_estimate=cost(6 * 10**9, 10 * 2**20),
    )(*far(dqkv, wqkv, x, dmid, res), g1, after)


def half_grads(name, half, n1, dqkv, att, dmid):
    return pl.pallas_call(
        half_kernel,
        name=name,
        in_specs=[SM] + [VM] * 4,
        out_specs=VM,
        out_shape=local((CHIPS_N, GRADS, 128)),
        compiler_params=params(),
        cost_estimate=cost(4 * 10**9, 4 * 2**20),
    )(half, *held(n1, dqkv, att, dmid))


def simple(kernel, name, out_shape, *operands, specs=None, scratch=(), mib=56):
    return pl.pallas_call(
        kernel,
        name=name,
        in_specs=specs or [VM] * len(operands),
        out_specs=VM if not scratch else HB,
        out_shape=out_shape,
        scratch_shapes=scratch,
        compiler_params=params(mib),
        cost_estimate=cost(10**9, 4 * 2**20),
    )(*operands)


def unpack(half, gathered, carried=None):
    mine = carried is None
    outs = [pltpu.HBM((D, FF), F32), pltpu.HBM((FF, D), F32), pltpu.HBM((D, 3 * D), F32), pltpu.HBM((D, D), F32)]
    gains = jnp.zeros((GAINS, 128), F32) if mine else carried[4]
    return pl.pallas_call(
        functools.partial(unpack_kernel, mine),
        name="unpack_mine" if mine else "unpack_theirs",
        in_specs=[SM, VM, VM] + ([] if mine else [HB] * 4),
        out_specs=[HB] * 4 + [VM],
        out_shape=outs + [shape((GAINS, 128), F32)],
        scratch_shapes=[
            pltpu.VMEM((D, FF // 2), F32),
            pltpu.VMEM((FF // 2, D), F32),
            pltpu.VMEM((4, D, HALF), F32),
            pltpu.SemaphoreType.DMA((6,)),
        ],
        input_output_aliases={} if mine else {3: 0, 4: 1, 5: 2, 6: 3},
        compiler_params=params(40),
        cost_estimate=cost(10**9, 10 * 2**20),
    )(half, gathered, gains, *([] if mine else far(*carried[:4])))


LAT = ("x", "zl")
LON = ("zh", "y", "c")
CHIPS = ("x", "zl", "zh", "y")


def send_rims(lon, lat, corner, distance):
    lats, lons = lax.axis_size(LAT), lax.axis_size(LON)
    moved = []
    for block, down, across in ((lon, 0, distance), (lat, distance, 0), (corner, distance, distance)):
        route = [
            (i * lons + j, (i + down) % lats * lons + (j + across) % lons)
            for i in range(lats) for j in range(lons)
        ]
        moved.append(lax.ppermute(block, LAT + LON, route))
    return moved


def other_core(block):
    return lax.ppermute(block, "c", [(0, 1), (1, 0)])


def exchange(parts):
    return lax.all_to_all(parts, CHIPS, 0, 0, tiled=True)


def shards(tokens, cotangent, norm_gain, w_qkv, w_out, mlp_gain, w_up, w_down):
    g1 = norm_gain.reshape(1, D)
    g2 = mlp_gain.reshape(1, D)
    last_band = lax.axis_index(LAT) == lax.axis_size(LAT) - 1
    flag = last_band.astype(jnp.int32).reshape(1)
    me = lax.axis_index("c").astype(jnp.int32).reshape(1)

    rims = send_rims(*pack(tokens, cotangent), -1)
    x, n1, qkv, p, att, mid, cot_far, cot, n2 = front(flag, tokens, cotangent, *rims, g1, w_qkv, w_out, g2)
    fixed = (me, n2, cot, w_up, w_down)
    down, dn2, grads = mlp("send", *fixed)
    got = other_core(grads)
    down, dn2, early = mlp("first", *fixed, down, dn2)
    down, dn2, grads = mlp("second", *fixed, down, dn2, early, got)
    sums = exchange(grads.reshape(CHIPS_N, SHARE, D))
    res, dmid_far, dqkv_far, dg2, att, n1, dmid, dqkv = back(cot_far, mid, down, dn2, w_out, qkv, p, att, n1, g2)
    got = other_core(half_grads("send", 1 - me, n1, dqkv, att, dmid))
    keep = half_grads("keep", me, n1, dqkv, att, dmid)
    added = simple(add_kernel, "add", pltpu.HBM((CHIPS_N, GRADS, 128), BF16), *held(keep, got), mib=32)
    att_sums = exchange(added)
    tile = simple(share_mlp_kernel, "share_mlp", shape((MLP, 128)), sums, added, specs=[VM, ANY])
    output, grad_tokens, lon, lat, corner, dg1 = token_grads(
        dqkv_far, w_qkv, x, dmid_far, res, g1, added, tokens.shape)
    att_sums, tile, dg1 = lax.optimization_barrier((att_sums, tile, dg1))
    rims = send_rims(lon, lat, corner, 1)
    shares = simple(
        share_kernel, "share", pltpu.HBM((CHIPS_N, ALL, 128), BF16), *far(att_sums), tile, dg1, dg2,
        specs=[HB, VM, VM, VM],
        scratch=[
            pltpu.VMEM((CHIPS_N, GRADS, 128), BF16),
            pltpu.VMEM((ALL, 128), BF16),
            pltpu.SemaphoreType.DMA,
            pltpu.SemaphoreType.DMA((CHIPS_N,)),
        ])
    gathered = exchange(shares)
    theirs = other_core(gathered)
    grads = unpack(1 - me, theirs, unpack(me, gathered))
    output, grad_tokens = place(output, grad_tokens, *rims, grads[4])
    gup, gdown, gqkv, gout, gains = grads
    gains = gains.reshape(2, D)
    return (output, grad_tokens, gains[0], gqkv, gout, gains[1], gup, gdown)


def solution(mesh):
    field = P(LAT, LON, None, None)
    mesh = jax.sharding.Mesh(mesh.devices.reshape(4, 2, 2, 4, 2), ("x", "zl", "zh", "y", "c"))
    return jax.shard_map(
        shards,
        mesh=mesh,
        in_specs=(field, field, P(), P(), P(), P(), P(), P()),
        out_specs=(field, field, P(), P(), P(), P(), P(), P()),
        check_vma=False,
    )
```

```python
import functools

import jax
import jax.numpy as jnp
from jax import lax
from jax.experimental import pallas as pl
from jax.experimental.pallas import tpu as pltpu
from jax.sharding import PartitionSpec as P

HD = 64
WLAT = 6
WLON = 12
LEV = 2
WIN = WLAT * WLON * LEV
D = 512
FF = 2048
HALF_LAT = WLAT // 2
HALF_LON = WLON // 2
EPS = 1e-05
F32 = jnp.float32
BF16 = jnp.bfloat16
PAIR = 2 * HD


def mm(a, b):
    return lax.dot_general(a, b, (((1,), (0,)), ((), ())), preferred_element_type=F32)


def mm_t(a, b):
    return lax.dot_general(a, b, (((1,), (1,)), ((), ())), preferred_element_type=F32)


def t_mm(a, b):
    return lax.dot_general(a, b, (((0,), (0,)), ((), ())), preferred_element_type=F32)


def normalised(values):
    mean = jnp.mean(values, axis=-1, keepdims=True)
    centred = values - mean
    var = jnp.mean(centred * centred, axis=-1, keepdims=True)
    scale = lax.rsqrt(var + EPS)
    return centred * scale, scale


def norm_pullback(xhat, scale, gain, grad):
    dxhat = grad * gain
    m1 = jnp.mean(dxhat, axis=-1, keepdims=True)
    m2 = jnp.mean(dxhat * xhat, axis=-1, keepdims=True)
    return scale * (dxhat - m1 - xhat * m2)


def gelu_parts(x):
    a = jnp.abs(x)
    t = 1.0 / (1.0 + (0.3275911 * 0.7071067811865476) * a)
    e = jnp.exp(-0.5 * x * x)
    poly = t * (0.127414796 + t * (-0.142248368 + t * (0.7107068705 + t * (-0.7265760135 + t * 0.5307027145))))
    tail = poly * e
    cdf = jnp.where(x >= 0.0, 1.0 - tail, tail)
    return cdf, 0.3989422804014327 * e


BANDS = 4
SIDES = 2


def strips():
    for band in range(BANDS):
        first = HALF_LAT + band * WLAT
        last = band == BANDS - 1
        across = [(0, WLAT, first, False)]
        if last:
            across = [(0, HALF_LAT, first, False), (HALF_LAT, HALF_LAT, 0, True)]
        for side in range(SIDES):
            left = HALF_LON + side * WLON
            along = [(0, WLON, left, False)]
            if side == SIDES - 1:
                along = [(0, HALF_LON, left, False), (HALF_LON, HALF_LON, 0, True)]
            for at_row, rows, row, far_row in across:
                for at_col, cols, col, far_col in along:
                    piece = 2 * far_row + far_col
                    if far_row and not far_col:
                        col -= HALF_LON
                    if far_col and not far_row:
                        row -= HALF_LAT
                    yield (
                        band, side, pl.ds(at_row, rows), pl.ds(at_col, cols),
                        piece, pl.ds(row, rows), pl.ds(col, cols),
                    )


SAVES = 6
STRIPS = len(list(strips()))


def gather_windows(which, field, rim_lon, rim_lat, corner, buffer, sems):
    copies = []
    for i, (band, side, to_rows, to_cols, piece, rows, cols) in enumerate(strips()):
        source = field if piece == 0 else (None, rim_lon, rim_lat, corner)[piece].at[which]
        copies.append(pltpu.make_async_copy(
            source.at[rows, cols], buffer.at[band, side, to_rows, to_cols], sems.at[i]))
    return copies


def scatter_windows(which, buffer, field, rim_lon, rim_lat, corner, sems):
    copies = []
    for i, (band, side, to_rows, to_cols, piece, rows, cols) in enumerate(strips()):
        target = field if piece == 0 else (None, rim_lon, rim_lat, corner)[piece].at[which]
        copies.append(pltpu.make_async_copy(
            buffer.at[band, side, to_rows, to_cols], target.at[rows, cols], sems.at[i]))
    return copies


def front_kernel(flag_ref, tok_ref, cot_ref, lon_ref, lat_ref, corner_ref, g1_ref, wqkv_hbm, wout_hbm, g2_ref,
                 x_out, n1_out, qkv_out, p_out, att_out, mid_out, cot_out, cotw_ref, n2_ref,
                 tok_buf, cot_buf, x_ref, n1_ref, qkv_ref, p_ref, att_ref, mid_ref, wqkv_ref, wout_ref,
                 sems, out_sems, w_sems):
    wqkv_copy = pltpu.make_async_copy(wqkv_hbm, wqkv_ref, w_sems.at[0])
    wout_copy = pltpu.make_async_copy(wout_hbm, wout_ref, w_sems.at[1])
    saves = []

    def save(source, target):
        copy = pltpu.make_async_copy(source, target, out_sems.at[len(saves)])
        copy.start()
        saves.append(copy)

    tok_copies = gather_windows(0, tok_ref, lon_ref, lat_ref, corner_ref, tok_buf, sems.at[0])
    cot_copies = gather_windows(1, cot_ref, lon_ref, lat_ref, corner_ref, cot_buf, sems.at[1])
    for copy in tok_copies + [wqkv_copy, wout_copy] + cot_copies:
        copy.start()
    for copy in tok_copies:
        copy.wait()
    for band in range(BANDS):
        for side in range(SIDES):
            w = band * SIDES + side
            x_ref[w * WIN:(w + 1) * WIN, :] = tok_buf[band, side].reshape(WIN, D)
    save(x_ref, x_out)
    tokens = x_ref.shape[0]
    count = tokens // WIN
    per_row = count // 4
    gain1 = g1_ref[...]
    gain2 = g2_ref[...]

    @pl.loop(0, count, unroll=2)
    def _(w):
        rows = pl.ds(pl.multiple_of(w * WIN, WIN), WIN)
        xhat, _ = normalised(x_ref[rows, :].astype(F32))
        n1_ref[rows, :] = (xhat * gain1).astype(BF16)

    wqkv_copy.wait()

    big = ROWS

    @pl.loop(0, tokens // big)
    def _(b):
        rows = pl.ds(pl.multiple_of(b * big, big), big)
        n1 = n1_ref[rows, :]
        qkv_ref[rows, 0:D] = (mm(n1, wqkv_ref[:, 0:D]).astype(BF16) * 0.125).astype(BF16)
        qkv_ref[rows, D:2 * D] = mm(n1, wqkv_ref[:, D:2 * D]).astype(BF16)
        qkv_ref[rows, 2 * D:3 * D] = mm(n1, wqkv_ref[:, 2 * D:3 * D]).astype(BF16)

    save(n1_ref, n1_out)
    save(qkv_ref, qkv_out)

    key_group = lax.broadcasted_iota(jnp.int32, (WIN, WIN), 0) >= WIN // 2
    query_group = lax.broadcasted_iota(jnp.int32, (WIN, WIN), 1) >= WIN // 2
    split = key_group != query_group
    low = lax.broadcasted_iota(jnp.int32, (WIN, PAIR), 1) < HD

    @pl.loop(0, count, unroll=8)
    def _(w):
        rows = pl.ds(pl.multiple_of(w * WIN, WIN), WIN)
        cut = jnp.logical_and(flag_ref[0] == 1, w >= count - per_row)
        masked = jnp.logical_and(split, cut)
        for pair in range(D // PAIR):
            lanes = slice(pair * PAIR, (pair + 1) * PAIR)
            q = qkv_ref[rows, pair * PAIR:(pair + 1) * PAIR]
            k = qkv_ref[rows, D + pair * PAIR:D + (pair + 1) * PAIR]
            v = qkv_ref[rows, 2 * D + pair * PAIR:2 * D + (pair + 1) * PAIR]
            outs = []
            for h in range(2):
                mine = low if h == 0 else jnp.logical_not(low)
                kh = jnp.where(mine, k, jnp.zeros_like(k))
                s = mm_t(kh, q)
                s = jnp.where(masked, -1000000000.0, s)
                e = jnp.exp(s - jnp.max(s, axis=0, keepdims=True))
                p = (e * (1.0 / jnp.sum(e, axis=0, keepdims=True))).astype(BF16)
                p_ref[w, 2 * pair + h] = p
                outs.append(t_mm(p, v))
            att_ref[rows, lanes] = jnp.where(low, outs[0], outs[1]).astype(BF16)
        pltpu.make_async_copy(p_ref.at[w], p_out.at[w], out_sems.at[SAVES + w]).start()

    save(att_ref, att_out)
    wout_copy.wait()

    @pl.loop(0, tokens // big)
    def _(b):
        rows = pl.ds(pl.multiple_of(b * big, big), big)
        mid = (x_ref[rows, :].astype(F32) + mm(att_ref[rows, :], wout_ref[...])).astype(BF16)
        mid_ref[rows, :] = mid
        xhat, _ = normalised(mid.astype(F32))
        n2_ref[rows, :] = (xhat * gain2).astype(BF16)

    save(mid_ref, mid_out)
    for copy in cot_copies:
        copy.wait()
    for band in range(BANDS):
        for side in range(SIDES):
            w = band * SIDES + side
            cotw_ref[w * WIN:(w + 1) * WIN, :] = cot_buf[band, side].reshape(WIN, D)
    save(cotw_ref, cot_out)
    for copy in saves:
        copy.wait()
    for w in range(count):
        pltpu.make_async_copy(p_ref.at[w], p_out.at[w], out_sems.at[SAVES + w]).wait()


CHUNK = 512
ROWS = 8 * WIN


def mlp_chunk(chunk, n2_ref, cot_ref, wup_ref, wdown_ref, down_in, dn2_in, down_out, dn2_out, hid_ref, du_ref):
    at = pl.ds(pl.multiple_of(chunk * CHUNK, CHUNK), CHUNK)

    @pl.loop(0, n2_ref.shape[0] // ROWS)
    def _(b):
        rows = pl.ds(pl.multiple_of(b * ROWS, ROWS), ROWS)
        up = mm(n2_ref[rows, :], wup_ref[:, at])
        cdf, pdf = gelu_parts(up)
        hid = (up * cdf).astype(BF16)
        hid_ref[rows, :] = hid
        dhid = mm_t(cot_ref[rows, :], wdown_ref[at, :]).astype(BF16).astype(F32)
        du = (dhid * (cdf + up * pdf)).astype(BF16)
        du_ref[rows, :] = du
        down = mm(hid, wdown_ref[at, :])
        dn2 = mm_t(du, wup_ref[:, at])
        if down_in is None:
            down_out[rows, :] = down
            dn2_out[rows, :] = dn2
        else:
            down_out[rows, :] = down_in[rows, :] + down
            dn2_out[rows, :] = dn2_in[rows, :] + dn2

    return t_mm(n2_ref[...], du_ref[...]).astype(BF16), t_mm(hid_ref[...], cot_ref[...]).astype(BF16)


def send_kernel(me_ref, n2_ref, cot_ref, wup_ref, wdown_ref, down_ref, dn2_ref, grads_ref, hid_ref, du_ref):
    for i in range(2):
        carried = (down_ref, dn2_ref) if i else (None, None)
        grads = mlp_chunk((1 - me_ref[0]) * 2 + i, n2_ref, cot_ref, wup_ref, wdown_ref,
                          *carried, down_ref, dn2_ref, hid_ref, du_ref)
        for part, grad in enumerate(grads):
            grads_ref[(2 * part + i) * CHUNK:(2 * part + i + 1) * CHUNK, :] = grad


def keep_first_kernel(me_ref, n2_ref, cot_ref, wup_ref, wdown_ref, down_in, dn2_in,
                      down_ref, dn2_ref, early_ref, hid_ref, du_ref):
    grads = mlp_chunk(me_ref[0] * 2, n2_ref, cot_ref, wup_ref, wdown_ref,
                      down_in, dn2_in, down_ref, dn2_ref, hid_ref, du_ref)
    for part, grad in enumerate(grads):
        early_ref[part * CHUNK:(part + 1) * CHUNK, :] = grad


def keep_second_kernel(me_ref, n2_ref, cot_ref, wup_ref, wdown_ref, down_in, dn2_in, early_ref, got_ref,
                       down_hbm, dn2_hbm, grads_ref, hid_ref, du_ref, down_ref, dn2_ref, sems):
    grads = mlp_chunk(me_ref[0] * 2 + 1, n2_ref, cot_ref, wup_ref, wdown_ref,
                      down_in, dn2_in, down_ref, dn2_ref, hid_ref, du_ref)
    copies = [
        pltpu.make_async_copy(down_ref, down_hbm, sems.at[0]),
        pltpu.make_async_copy(dn2_ref, dn2_hbm, sems.at[1]),
    ]
    for copy in copies:
        copy.start()
    for part, grad in enumerate(grads):
        for i in range(2):
            rows = slice((2 * part + i) * CHUNK, (2 * part + i + 1) * CHUNK)
            mine = grad if i else early_ref[part * CHUNK:(part + 1) * CHUNK, :]
            grads_ref[rows, :] = (mine.astype(F32) + got_ref[rows, :].astype(F32)).astype(BF16)
    for copy in copies:
        copy.wait()


HALF = D // 2
CHIPS_N = 64
GRADS = 64
GAINS = 8


def att_grads(half, n1_ref, dqkv_ref, att_ref, dmid_ref, out_ref):
    per = D // (CHIPS_N // 4)
    lanes = pl.ds(pl.multiple_of(half * HALF, HALF), HALF)
    for part in range(4):
        if part < 3:
            part_lanes = pl.ds(pl.multiple_of(part * D + half * HALF, HALF), HALF)
            grad = t_mm(n1_ref[...], dqkv_ref[:, part_lanes])
        else:
            grad = t_mm(att_ref[...], dmid_ref[:, lanes])
        grad = grad.astype(BF16)
        first = part * (CHIPS_N // 4)
        for block in range(2):
            piece = grad[:, block * 128:(block + 1) * 128].reshape(CHIPS_N // 4, per, 128)
            out_ref[first:first + CHIPS_N // 4, block * per:(block + 1) * per, :] = piece


def att_back(first, last, datt_ref, qkv_ref, p_ref, dqkv_ref):
    low = lax.broadcasted_iota(jnp.int32, (WIN, PAIR), 1) < HD

    @pl.loop(first, last, unroll=4)
    def _(w):
        rows = pl.ds(pl.multiple_of(w * WIN, WIN), WIN)
        for pair in range(D // PAIR):
            lanes = slice(pair * PAIR, (pair + 1) * PAIR)
            q = qkv_ref[rows, pair * PAIR:(pair + 1) * PAIR]
            k = qkv_ref[rows, D + pair * PAIR:D + (pair + 1) * PAIR]
            v = qkv_ref[rows, 2 * D + pair * PAIR:2 * D + (pair + 1) * PAIR]
            da = datt_ref[rows, lanes]
            dqs, dks, dvs = [], [], []
            for h in range(2):
                mine = low if h == 0 else jnp.logical_not(low)
                vh = jnp.where(mine, v, jnp.zeros_like(v))
                p = p_ref[w, 2 * pair + h]
                pf = p.astype(F32)
                dp = mm_t(vh, da).astype(BF16).astype(F32)
                ds = (pf * (dp - jnp.sum(dp * pf, axis=0, keepdims=True))).astype(BF16)
                dvs.append(mm(p, da))
                dks.append(mm(ds, q))
                dqs.append(t_mm(ds, k))
            dqkv_ref[rows, pair * PAIR:(pair + 1) * PAIR] = (jnp.where(low, dqs[0], dqs[1]) * 0.125).astype(BF16)
            dqkv_ref[rows, D + pair * PAIR:D + (pair + 1) * PAIR] = jnp.where(low, dks[0], dks[1]).astype(BF16)
            dqkv_ref[rows, 2 * D + pair * PAIR:2 * D + (pair + 1) * PAIR] = jnp.where(low, dvs[0], dvs[1]).astype(BF16)


def start_loads(pairs, sems):
    loads = []
    for i, (source, target) in enumerate(pairs):
        loads.append(pltpu.make_async_copy(source, target, sems.at[i]))
        loads[-1].start()
    return loads


def back_kernel(cot_hbm, mid_hbm, down_hbm, dn2_hbm, wout_hbm, qkv_hbm, p_hbm, att_hbm, n1_hbm, g2_ref,
                res_out, dmid_out, dqkv_out, dg2_ref, att_ref, n1_ref, dmid_ref, dqkv_ref,
                cot_ref, mid_ref, down_ref, dn2_ref, wout_ref, qkv_ref, p_ref, datt_ref, res_ref, in_sems, sems):
    loads = start_loads((
        (cot_hbm, cot_ref), (mid_hbm, mid_ref), (down_hbm, down_ref), (dn2_hbm, dn2_ref),
        (wout_hbm, wout_ref), (qkv_hbm, qkv_ref), (p_hbm, p_ref), (att_hbm, att_ref), (n1_hbm, n1_ref),
    ), in_sems)
    gain2 = g2_ref[...]
    dg2_ref[...] = jnp.zeros_like(dg2_ref)
    tokens = cot_ref.shape[0]
    for load in loads[:4]:
        load.wait()

    @pl.loop(0, tokens // WIN, unroll=2)
    def _(b):
        rows = pl.ds(pl.multiple_of(b * WIN, WIN), WIN)
        mid = mid_ref[rows, :].astype(F32)
        res_ref[rows, :] = (mid + down_ref[rows, :]).astype(BF16)
        xhat, scale = normalised(mid)
        dn2 = dn2_ref[rows, :].astype(BF16).astype(F32)
        dg2_ref[...] += jnp.sum(dn2 * xhat, axis=0, keepdims=True)
        dmid = cot_ref[rows, :].astype(F32) + norm_pullback(xhat, scale, gain2, dn2)
        dmid_ref[rows, :] = dmid.astype(BF16)

    saves = [
        pltpu.make_async_copy(res_ref, res_out, sems.at[0]),
        pltpu.make_async_copy(dmid_ref, dmid_out, sems.at[1]),
    ]
    for copy in saves:
        copy.start()
    loads[4].wait()

    @pl.loop(0, tokens // ROWS)
    def _(b):
        rows = pl.ds(pl.multiple_of(b * ROWS, ROWS), ROWS)
        datt_ref[rows, :] = mm_t(dmid_ref[rows, :], wout_ref[...]).astype(BF16)

    loads[5].wait()
    loads[6].wait()
    att_back(0, tokens // WIN, datt_ref, qkv_ref, p_ref, dqkv_ref)
    saves.append(pltpu.make_async_copy(dqkv_ref, dqkv_out, sems.at[2]))
    saves[-1].start()
    for copy in loads[7:] + saves:
        copy.wait()


def tokens_kernel(dqkv_hbm, wqkv_hbm, x_hbm, dmid_hbm, res_hbm, g1_ref, after_ref,
                  out_ref, grad_ref, lon_ref, lat_ref, corner_ref, dg1_ref,
                  dqkv_ref, wqkv_ref, x_ref, dmid_ref, res_ref, dx_ref, res_buf, dx_buf, in_sems, sems):
    loads = start_loads((
        (res_hbm, res_ref), (dqkv_hbm, dqkv_ref), (wqkv_hbm, wqkv_ref), (x_hbm, x_ref), (dmid_hbm, dmid_ref),
    ), in_sems)
    gain1 = g1_ref[...]
    tokens = x_ref.shape[0]
    dg1_ref[...] = jnp.zeros_like(dg1_ref)
    loads[0].wait()
    for band in range(BANDS):
        for side in range(SIDES):
            w = band * SIDES + side
            res_buf[band, side] = res_ref[w * WIN:(w + 1) * WIN, :].reshape(WLAT, WLON, LEV, D)
    res_copies = scatter_windows(0, res_buf, out_ref, lon_ref, lat_ref, corner_ref, sems.at[0])
    for copy in res_copies:
        copy.start()
    for load in loads[1:]:
        load.wait()

    @pl.loop(0, tokens // ROWS)
    def _(b):
        rows = pl.ds(pl.multiple_of(b * ROWS, ROWS), ROWS)
        dn1 = mm_t(dqkv_ref[rows, :], wqkv_ref[...]).astype(BF16).astype(F32)
        xhat, scale = normalised(x_ref[rows, :].astype(F32))
        dg1_ref[...] += jnp.sum(dn1 * xhat, axis=0, keepdims=True)
        dx = dmid_ref[rows, :].astype(F32) + norm_pullback(xhat, scale, gain1, dn1)
        dx_ref[rows, :] = dx.astype(BF16)

    for band in range(BANDS):
        for side in range(SIDES):
            w = band * SIDES + side
            dx_buf[band, side] = dx_ref[w * WIN:(w + 1) * WIN, :].reshape(WLAT, WLON, LEV, D)
    dx_copies = scatter_windows(1, dx_buf, grad_ref, lon_ref, lat_ref, corner_ref, sems.at[1])
    for copy in dx_copies:
        copy.start()
    for copy in res_copies + dx_copies:
        copy.wait()


SHARE = FF // CHIPS_N
MLP = SHARE * D // 128
ALL = GRADS + GAINS + MLP


def total_of(parts_ref, rows):
    total = parts_ref[0, rows, :].astype(F32)
    for chip in range(1, CHIPS_N):
        total += parts_ref[chip, rows, :].astype(F32)
    return total.astype(BF16)


def half_kernel(half_ref, n1_ref, dqkv_ref, att_ref, dmid_ref, out_ref):
    att_grads(half_ref[0], n1_ref, dqkv_ref, att_ref, dmid_ref, out_ref)


def add_kernel(keep_ref, got_ref, out_ref):
    for chip in range(CHIPS_N):
        out_ref[chip] = (keep_ref[chip].astype(F32) + got_ref[chip].astype(F32)).astype(BF16)


def share_mlp_kernel(sums_ref, after_ref, tile_ref):
    del after_ref
    total = total_of(sums_ref, slice(0, SHARE))
    for block in range(D // 128):
        tile_ref[block * SHARE:(block + 1) * SHARE, :] = total[:, block * 128:(block + 1) * 128]


def share_kernel(parts_ref, tile_ref, dg1_ref, dg2_ref, out_ref, share_ref, sems):
    share_ref[GRADS + GAINS:, :] = tile_ref[...]
    share_ref[GRADS:GRADS + GAINS, :] = jnp.concatenate(
        [ref[:, block * 128:(block + 1) * 128] for ref in (dg1_ref, dg2_ref) for block in range(D // 128)]).astype(BF16)
    share_ref[0:GRADS, :] = total_of(parts_ref, slice(0, GRADS))
    copies = [pltpu.make_async_copy(share_ref, out_ref.at[chip], sems.at[chip]) for chip in range(CHIPS_N)]
    for copy in copies:
        copy.start()
    for copy in copies:
        copy.wait()


def unpack_kernel(mine, half_ref, all_ref, gains_in, *refs):
    (gup_hbm, gdown_hbm, gqkv_hbm, gout_hbm, gains_ref, gup_ref, gdown_ref, att_ref, sems) = refs if mine else refs[4:]
    half = half_ref[0]
    wide = FF // 2
    copies = []

    def send(source, target):
        copies.append(pltpu.make_async_copy(source, target, sems.at[len(copies)]))
        copies[-1].start()

    blocks = [(slice(GRADS + GAINS + i * SHARE, GRADS + GAINS + (i + 1) * SHARE), i * 128) for i in range(D // 128)]
    quarter = CHIPS_N // 4
    for rows, lane in blocks:
        gdown_ref[:, lane:lane + 128] = all_ref[2 * quarter:, rows, :].reshape(wide, 128).astype(F32)
    send(gdown_ref, gdown_hbm.at[pl.ds(pl.multiple_of(half * wide, wide), wide), :])
    for j in range(2):
        for rows, lane in blocks:
            piece = all_ref[j * quarter:(j + 1) * quarter, rows, :].reshape(D, 128)
            gup_ref[:, j * D + lane:j * D + lane + 128] = piece.astype(F32)
    send(gup_ref, gup_hbm.at[:, pl.ds(pl.multiple_of(half * wide, wide), wide)])
    per = GRADS // 2
    for part in range(4):
        for block in range(2):
            piece = all_ref[part * quarter:(part + 1) * quarter, block * per:(block + 1) * per, :].reshape(D, 128)
            att_ref[part, :, block * 128:(block + 1) * 128] = piece.astype(F32)
        out, first = (gqkv_hbm, part * D) if part < 3 else (gout_hbm, 0)
        send(att_ref.at[part], out.at[:, pl.ds(pl.multiple_of(half * HALF + first, HALF), HALF)])
    gains = all_ref[0, GRADS:GRADS + GAINS, :].astype(F32)
    for chip in range(1, CHIPS_N):
        gains += all_ref[chip, GRADS:GRADS + GAINS, :].astype(F32)
    gains_ref[...] = gains if mine else gains_in[...] + gains
    for copy in copies:
        copy.wait()


def pack_kernel(tok_ref, cot_ref, lon_ref, lat_ref, corner_ref, sems):
    copies = []
    for which, ref in enumerate((tok_ref, cot_ref)):
        below, right = pl.ds(HALF_LAT, ref.shape[0] - HALF_LAT), pl.ds(HALF_LON, ref.shape[1] - HALF_LON)
        top, left = pl.ds(0, HALF_LAT), pl.ds(0, HALF_LON)
        for i, (rows, cols, out) in enumerate(((below, left, lon_ref), (top, right, lat_ref), (top, left, corner_ref))):
            copies.append(pltpu.make_async_copy(ref.at[rows, cols], out.at[which], sems.at[which, i]))
    for copy in copies:
        copy.start()
    for copy in copies:
        copy.wait()


def place_kernel(out_in, grad_in, lon_ref, lat_ref, corner_ref, after_ref, out_ref, grad_ref, sems):
    del out_in, grad_in, after_ref
    copies = []
    for which, ref in enumerate((out_ref, grad_ref)):
        below, right = pl.ds(HALF_LAT, ref.shape[0] - HALF_LAT), pl.ds(HALF_LON, ref.shape[1] - HALF_LON)
        top, left = pl.ds(0, HALF_LAT), pl.ds(0, HALF_LON)
        for i, (rows, cols, rim) in enumerate(((below, left, lon_ref), (top, right, lat_ref), (top, left, corner_ref))):
            copies.append(pltpu.make_async_copy(rim.at[which], ref.at[rows, cols], sems.at[which, i]))
    for copy in copies:
        copy.start()
    for copy in copies:
        copy.wait()


def params(mib=32):
    return pltpu.CompilerParams(vmem_limit_bytes=mib * 2**20)


def cost(flops, moved):
    return pl.CostEstimate(flops=flops, bytes_accessed=moved, transcendentals=0)


def shape(dims, dtype=BF16):
    return jax.ShapeDtypeStruct(dims, dtype)


SM = pl.BlockSpec(memory_space=pltpu.SMEM)
VM = pl.BlockSpec(memory_space=pltpu.VMEM)


ANY = pl.BlockSpec(memory_space=pl.ANY)
HB = pl.BlockSpec(memory_space=pltpu.HBM)


def rim_shapes(rows, cols, levels):
    return [
        shape((2, rows - HALF_LAT, HALF_LON, levels, D)),
        shape((2, HALF_LAT, cols - HALF_LON, levels, D)),
        shape((2, HALF_LAT, HALF_LON, levels, D)),
    ]


def pack(tokens, cotangent):
    return pl.pallas_call(
        pack_kernel,
        name="pack",
        in_specs=[ANY] * 2,
        out_specs=[VM] * 3,
        out_shape=[local(rim.shape) for rim in rim_shapes(*tokens.shape[:3])],
        scratch_shapes=[pltpu.SemaphoreType.DMA((2, 3))],
    )(tokens, cotangent)


def place(output, grad, lon, lat, corner, after):
    return pl.pallas_call(
        place_kernel,
        name="place",
        in_specs=[ANY] * 2 + [VM] * 3 + [ANY],
        out_specs=[ANY] * 2,
        out_shape=[shape(output.shape), shape(grad.shape)],
        input_output_aliases={0: 0, 1: 1},
        scratch_shapes=[pltpu.SemaphoreType.DMA((2, 3))],
        cost_estimate=cost(10**9, 2**21),
    )(output, grad, lon, lat, corner, after)


WINDOWED = (BANDS, SIDES, WLAT, WLON, LEV, D)


def local(dims, dtype=BF16):
    return pltpu.VMEM(dims, dtype)


def held(*arrays):
    return [pltpu.with_memory_space_constraint(array, pltpu.VMEM) for array in arrays]


def far(*arrays):
    return [pltpu.with_memory_space_constraint(array, pltpu.HBM) for array in arrays]


def front(flag, tok, cot, lon, lat, corner, g1, wqkv, wout, g2):
    tokens = tok.size // D
    count = tokens // WIN
    saved = [(tokens, D), (tokens, D), (tokens, 3 * D), (count, D // HD, WIN, WIN), (tokens, D), (tokens, D)]
    return pl.pallas_call(
        front_kernel,
        name="front",
        in_specs=[SM] + [ANY] * 5 + [VM, HB, HB, VM],
        out_specs=[HB] * 7 + [VM] * 2,
        out_shape=[pltpu.HBM(dims, BF16) for dims in saved + [(tokens, D)]] + [local((tokens, D)), local((tokens, D))],
        scratch_shapes=[
            pltpu.VMEM(WINDOWED, BF16),
            pltpu.VMEM(WINDOWED, BF16),
        ] + [pltpu.VMEM(dims, BF16) for dims in saved] + [
            pltpu.VMEM((D, 3 * D), BF16),
            pltpu.VMEM((D, D), BF16),
            pltpu.SemaphoreType.DMA((2, STRIPS)),
            pltpu.SemaphoreType.DMA((SAVES + count,)),
            pltpu.SemaphoreType.DMA((2,)),
        ],
        compiler_params=params(),
        cost_estimate=cost(15 * 10**9, 10 * 2**20),
    )(flag, tok, cot, lon, lat, corner, g1, *far(wqkv, wout), g2)


def mlp(kind, me, n2, cot, wup, wdown, *carried):
    tokens = n2.shape[0]
    sums = [local((tokens, D), F32)] * 2
    scratch = [pltpu.VMEM((tokens, CHUNK), BF16)] * 2
    out_specs, aliases = [VM] * 3, {}
    if kind == "send":
        kernel, out_shape = send_kernel, sums + [shape((FF, D))]
    elif kind == "first":
        kernel, out_shape = keep_first_kernel, sums + [local((2 * CHUNK, D))]
        aliases = {5: 0, 6: 1}
    else:
        kernel, out_shape = keep_second_kernel, [pltpu.HBM((tokens, D), F32)] * 2 + [pltpu.HBM((FF, D), BF16)]
        out_specs = [HB, HB, VM]
        scratch = scratch + [pltpu.VMEM((tokens, D), F32)] * 2 + [pltpu.SemaphoreType.DMA((2,))]
    return pl.pallas_call(
        kernel,
        name="mlp_" + kind,
        in_specs=[SM, VM, VM, VM, VM] + [VM] * len(carried),
        out_specs=out_specs,
        out_shape=out_shape,
        scratch_shapes=scratch,
        input_output_aliases=aliases,
        compiler_params=params(),
        cost_estimate=cost((16 if kind == "send" else 8) * 10**9, 10 * 2**20),
    )(me, *held(n2, cot, wup, wdown, *carried))


def back(cot, mid, down, dn2, wout, qkv, p, att, n1, g2):
    tokens = cot.shape[0]
    count = tokens // WIN
    halves = pltpu.VMEM((tokens, D), BF16)
    full = pltpu.VMEM((tokens, D), F32)
    return pl.pallas_call(
        back_kernel,
        name="back",
        in_specs=[HB] * 9 + [VM],
        out_specs=[HB] * 3 + [VM] * 5,
        out_shape=[
            pltpu.HBM((tokens, D), BF16),
            pltpu.HBM((tokens, D), BF16),
            pltpu.HBM((tokens, 3 * D), BF16),
            shape((1, D), F32),
            local((tokens, D)),
            local((tokens, D)),
            local((tokens, D)),
            local((tokens, 3 * D)),
        ],
        scratch_shapes=[
            halves,
            halves,
            full,
            full,
            pltpu.VMEM((D, D), BF16),
            pltpu.VMEM((tokens, 3 * D), BF16),
            pltpu.VMEM((count, D // HD, WIN, WIN), BF16),
            halves,
            halves,
            pltpu.SemaphoreType.DMA((9,)),
            pltpu.SemaphoreType.DMA((3,)),
        ],
        compiler_params=params(40),
        cost_estimate=cost(25 * 10**9, 10 * 2**20),
    )(*far(cot, mid, down, dn2, wout, qkv, p, att, n1), g2)


def token_grads(dqkv, wqkv, x, dmid, res, g1, after, field):
    tokens = x.shape[0]
    halves = pltpu.VMEM((tokens, D), BF16)
    return pl.pallas_call(
        tokens_kernel,
        name="tokens",
        in_specs=[HB] * 5 + [VM, ANY],
        out_specs=[ANY] * 5 + [VM],
        out_shape=[shape(field), shape(field)] + rim_shapes(*field[:3]) + [shape((1, D), F32)],
        scratch_shapes=[
            pltpu.VMEM((tokens, 3 * D), BF16),
            pltpu.VMEM((D, 3 * D), BF16),
            halves,
            halves,
            halves,
            halves,
            pltpu.VMEM(WINDOWED, BF16),
            pltpu.VMEM(WINDOWED, BF16),
            pltpu.SemaphoreType.DMA((5,)),
            pltpu.SemaphoreType.DMA((2, STRIPS)),
        ],
        compiler_params=params(),
        cost_estimate=cost(6 * 10**9, 10 * 2**20),
    )(*far(dqkv, wqkv, x, dmid, res), g1, after)


def half_grads(name, half, n1, dqkv, att, dmid):
    return pl.pallas_call(
        half_kernel,
        name=name,
        in_specs=[SM] + [VM] * 4,
        out_specs=VM,
        out_shape=local((CHIPS_N, GRADS, 128)),
        compiler_params=params(),
        cost_estimate=cost(4 * 10**9, 4 * 2**20),
    )(half, *held(n1, dqkv, att, dmid))


def simple(kernel, name, out_shape, *operands, specs=None, scratch=(), mib=56):
    return pl.pallas_call(
        kernel,
        name=name,
        in_specs=specs or [VM] * len(operands),
        out_specs=VM if not scratch else HB,
        out_shape=out_shape,
        scratch_shapes=scratch,
        compiler_params=params(mib),
        cost_estimate=cost(10**9, 4 * 2**20),
    )(*operands)


def unpack(half, gathered, carried=None):
    mine = carried is None
    outs = [pltpu.HBM((D, FF), F32), pltpu.HBM((FF, D), F32), pltpu.HBM((D, 3 * D), F32), pltpu.HBM((D, D), F32)]
    gains = jnp.zeros((GAINS, 128), F32) if mine else carried[4]
    return pl.pallas_call(
        functools.partial(unpack_kernel, mine),
        name="unpack_mine" if mine else "unpack_theirs",
        in_specs=[SM, VM, VM] + ([] if mine else [HB] * 4),
        out_specs=[HB] * 4 + [VM],
        out_shape=outs + [shape((GAINS, 128), F32)],
        scratch_shapes=[
            pltpu.VMEM((D, FF // 2), F32),
            pltpu.VMEM((FF // 2, D), F32),
            pltpu.VMEM((4, D, HALF), F32),
            pltpu.SemaphoreType.DMA((6,)),
        ],
        input_output_aliases={} if mine else {3: 0, 4: 1, 5: 2, 6: 3},
        compiler_params=params(40),
        cost_estimate=cost(10**9, 10 * 2**20),
    )(half, gathered, gains, *([] if mine else far(*carried[:4])))


LAT = ("x", "zl")
LON = ("zh", "y", "c")
CHIPS = ("y", "x", "zh", "zl")


def send_rims(lon, lat, corner, distance):
    lats, lons = lax.axis_size(LAT), lax.axis_size(LON)
    moved = []
    for block, down, across in ((lon, 0, distance), (lat, distance, 0), (corner, distance, distance)):
        route = [
            (i * lons + j, (i + down) % lats * lons + (j + across) % lons)
            for i in range(lats) for j in range(lons)
        ]
        moved.append(lax.ppermute(block, LAT + LON, route))
    return moved


def other_core(block):
    return lax.ppermute(block, "c", [(0, 1), (1, 0)])


def exchange(parts):
    return lax.all_to_all(parts, CHIPS, 0, 0, tiled=True)


def shards(tokens, cotangent, norm_gain, w_qkv, w_out, mlp_gain, w_up, w_down):
    g1 = norm_gain.reshape(1, D)
    g2 = mlp_gain.reshape(1, D)
    last_band = lax.axis_index(LAT) == lax.axis_size(LAT) - 1
    flag = last_band.astype(jnp.int32).reshape(1)
    me = lax.axis_index("c").astype(jnp.int32).reshape(1)

    rims = send_rims(*pack(tokens, cotangent), -1)
    x, n1, qkv, p, att, mid, cot_far, cot, n2 = front(flag, tokens, cotangent, *rims, g1, w_qkv, w_out, g2)
    fixed = (me, n2, cot, w_up, w_down)
    down, dn2, grads = mlp("send", *fixed)
    got = other_core(grads)
    down, dn2, early = mlp("first", *fixed, down, dn2)
    down, dn2, grads = mlp("second", *fixed, down, dn2, early, got)
    sums = exchange(grads.reshape(CHIPS_N, SHARE, D))
    res, dmid_far, dqkv_far, dg2, att, n1, dmid, dqkv = back(cot_far, mid, down, dn2, w_out, qkv, p, att, n1, g2)
    got = other_core(half_grads("send", 1 - me, n1, dqkv, att, dmid))
    keep = half_grads("keep", me, n1, dqkv, att, dmid)
    added = simple(add_kernel, "add", pltpu.HBM((CHIPS_N, GRADS, 128), BF16), *held(keep, got), mib=32)
    att_sums = exchange(added)
    tile = simple(share_mlp_kernel, "share_mlp", shape((MLP, 128)), sums, added, specs=[VM, ANY])
    output, grad_tokens, lon, lat, corner, dg1 = token_grads(
        dqkv_far, w_qkv, x, dmid_far, res, g1, added, tokens.shape)
    att_sums, tile, dg1 = lax.optimization_barrier((att_sums, tile, dg1))
    rims = send_rims(lon, lat, corner, 1)
    shares = simple(
        share_kernel, "share", pltpu.HBM((CHIPS_N, ALL, 128), BF16), *held(att_sums), tile, dg1, dg2, mib=32,
        scratch=[pltpu.VMEM((ALL, 128), BF16), pltpu.SemaphoreType.DMA((CHIPS_N,))])
    gathered = exchange(shares)
    theirs = other_core(gathered)
    grads = unpack(1 - me, theirs, unpack(me, gathered))
    output, grad_tokens = place(output, grad_tokens, *rims, grads[4])
    gup, gdown, gqkv, gout, gains = grads
    gains = gains.reshape(2, D)
    return (output, grad_tokens, gains[0], gqkv, gout, gains[1], gup, gdown)


def solution(mesh):
    field = P(LAT, LON, None, None)
    mesh = jax.sharding.Mesh(mesh.devices.reshape(4, 2, 2, 4, 2), ("x", "zl", "zh", "y", "c"))
    return jax.shard_map(
        shards,
        mesh=mesh,
        in_specs=(field, field, P(), P(), P(), P(), P(), P()),
        out_specs=(field, field, P(), P(), P(), P(), P(), P()),
        check_vma=False,
    )
```

```python
import functools

import jax
import jax.numpy as jnp
from jax import lax
from jax.experimental import pallas as pl
from jax.experimental.pallas import tpu as pltpu
from jax.sharding import PartitionSpec as P

HD = 64
WLAT = 6
WLON = 12
LEV = 2
WIN = WLAT * WLON * LEV
D = 512
FF = 2048
HALF_LAT = WLAT // 2
HALF_LON = WLON // 2
EPS = 1e-05
F32 = jnp.float32
BF16 = jnp.bfloat16
PAIR = 2 * HD


def mm(a, b):
    return lax.dot_general(a, b, (((1,), (0,)), ((), ())), preferred_element_type=F32)


def mm_t(a, b):
    return lax.dot_general(a, b, (((1,), (1,)), ((), ())), preferred_element_type=F32)


def t_mm(a, b):
    return lax.dot_general(a, b, (((0,), (0,)), ((), ())), preferred_element_type=F32)


def normalised(values):
    mean = jnp.mean(values, axis=-1, keepdims=True)
    centred = values - mean
    var = jnp.mean(centred * centred, axis=-1, keepdims=True)
    scale = lax.rsqrt(var + EPS)
    return centred * scale, scale


def norm_pullback(xhat, scale, gain, grad):
    dxhat = grad * gain
    m1 = jnp.mean(dxhat, axis=-1, keepdims=True)
    m2 = jnp.mean(dxhat * xhat, axis=-1, keepdims=True)
    return scale * (dxhat - m1 - xhat * m2)


def gelu_parts(x):
    a = jnp.abs(x)
    t = 1.0 / (1.0 + (0.3275911 * 0.7071067811865476) * a)
    e = jnp.exp(-0.5 * x * x)
    poly = t * (0.127414796 + t * (-0.142248368 + t * (0.7107068705 + t * (-0.7265760135 + t * 0.5307027145))))
    tail = poly * e
    cdf = jnp.where(x >= 0.0, 1.0 - tail, tail)
    return cdf, 0.3989422804014327 * e


BANDS = 4
SIDES = 2


def strips():
    for band in range(BANDS):
        first = HALF_LAT + band * WLAT
        last = band == BANDS - 1
        across = [(0, WLAT, first, False)]
        if last:
            across = [(0, HALF_LAT, first, False), (HALF_LAT, HALF_LAT, 0, True)]
        for side in range(SIDES):
            left = HALF_LON + side * WLON
            along = [(0, WLON, left, False)]
            if side == SIDES - 1:
                along = [(0, HALF_LON, left, False), (HALF_LON, HALF_LON, 0, True)]
            for at_row, rows, row, far_row in across:
                for at_col, cols, col, far_col in along:
                    piece = 2 * far_row + far_col
                    if far_row and not far_col:
                        col -= HALF_LON
                    if far_col and not far_row:
                        row -= HALF_LAT
                    yield (
                        band, side, pl.ds(at_row, rows), pl.ds(at_col, cols),
                        piece, pl.ds(row, rows), pl.ds(col, cols),
                    )


SAVES = 6
STRIPS = len(list(strips()))


def gather_windows(which, field, rim_lon, rim_lat, corner, buffer, sems):
    copies = []
    for i, (band, side, to_rows, to_cols, piece, rows, cols) in enumerate(strips()):
        source = field if piece == 0 else (None, rim_lon, rim_lat, corner)[piece].at[which]
        copies.append(pltpu.make_async_copy(
            source.at[rows, cols], buffer.at[band, side, to_rows, to_cols], sems.at[i]))
    return copies


def scatter_windows(which, buffer, field, rim_lon, rim_lat, corner, sems):
    copies = []
    for i, (band, side, to_rows, to_cols, piece, rows, cols) in enumerate(strips()):
        target = field if piece == 0 else (None, rim_lon, rim_lat, corner)[piece].at[which]
        copies.append(pltpu.make_async_copy(
            buffer.at[band, side, to_rows, to_cols], target.at[rows, cols], sems.at[i]))
    return copies


def front_kernel(flag_ref, tok_ref, cot_ref, lon_ref, lat_ref, corner_ref, g1_ref, wqkv_hbm, wout_hbm, g2_ref,
                 x_out, n1_out, qkv_out, p_out, att_out, mid_out, cot_out, cotw_ref, n2_ref,
                 tok_buf, cot_buf, x_ref, n1_ref, qkv_ref, p_ref, att_ref, mid_ref, wqkv_ref, wout_ref,
                 sems, out_sems, w_sems):
    wqkv_copy = pltpu.make_async_copy(wqkv_hbm, wqkv_ref, w_sems.at[0])
    wout_copy = pltpu.make_async_copy(wout_hbm, wout_ref, w_sems.at[1])
    saves = []

    def save(source, target):
        copy = pltpu.make_async_copy(source, target, out_sems.at[len(saves)])
        copy.start()
        saves.append(copy)

    tok_copies = gather_windows(0, tok_ref, lon_ref, lat_ref, corner_ref, tok_buf, sems.at[0])
    cot_copies = gather_windows(1, cot_ref, lon_ref, lat_ref, corner_ref, cot_buf, sems.at[1])
    for copy in tok_copies + [wqkv_copy, wout_copy] + cot_copies:
        copy.start()
    for copy in tok_copies:
        copy.wait()
    for band in range(BANDS):
        for side in range(SIDES):
            w = band * SIDES + side
            x_ref[w * WIN:(w + 1) * WIN, :] = tok_buf[band, side].reshape(WIN, D)
    save(x_ref, x_out)
    tokens = x_ref.shape[0]
    count = tokens // WIN
    per_row = count // 4
    gain1 = g1_ref[...]
    gain2 = g2_ref[...]

    @pl.loop(0, count, unroll=2)
    def _(w):
        rows = pl.ds(pl.multiple_of(w * WIN, WIN), WIN)
        xhat, _ = normalised(x_ref[rows, :].astype(F32))
        n1_ref[rows, :] = (xhat * gain1).astype(BF16)

    wqkv_copy.wait()

    big = ROWS

    @pl.loop(0, tokens // big)
    def _(b):
        rows = pl.ds(pl.multiple_of(b * big, big), big)
        n1 = n1_ref[rows, :]
        qkv_ref[rows, 0:D] = (mm(n1, wqkv_ref[:, 0:D]).astype(BF16) * 0.125).astype(BF16)
        qkv_ref[rows, D:2 * D] = mm(n1, wqkv_ref[:, D:2 * D]).astype(BF16)
        qkv_ref[rows, 2 * D:3 * D] = mm(n1, wqkv_ref[:, 2 * D:3 * D]).astype(BF16)

    save(n1_ref, n1_out)
    save(qkv_ref, qkv_out)

    key_group = lax.broadcasted_iota(jnp.int32, (WIN, WIN), 0) >= WIN // 2
    query_group = lax.broadcasted_iota(jnp.int32, (WIN, WIN), 1) >= WIN // 2
    split = key_group != query_group
    low = lax.broadcasted_iota(jnp.int32, (WIN, PAIR), 1) < HD

    @pl.loop(0, count, unroll=4)
    def _(w):
        rows = pl.ds(pl.multiple_of(w * WIN, WIN), WIN)
        cut = jnp.logical_and(flag_ref[0] == 1, w >= count - per_row)
        masked = jnp.logical_and(split, cut)
        for pair in range(D // PAIR):
            lanes = slice(pair * PAIR, (pair + 1) * PAIR)
            q = qkv_ref[rows, pair * PAIR:(pair + 1) * PAIR]
            k = qkv_ref[rows, D + pair * PAIR:D + (pair + 1) * PAIR]
            v = qkv_ref[rows, 2 * D + pair * PAIR:2 * D + (pair + 1) * PAIR]
            outs = []
            for h in range(2):
                mine = low if h == 0 else jnp.logical_not(low)
                kh = jnp.where(mine, k, jnp.zeros_like(k))
                s = mm_t(kh, q)
                s = jnp.where(masked, -1000000000.0, s)
                e = jnp.exp(s - jnp.max(s, axis=0, keepdims=True))
                p = (e * (1.0 / jnp.sum(e, axis=0, keepdims=True))).astype(BF16)
                p_ref[w, 2 * pair + h] = p
                outs.append(t_mm(p, v))
            att_ref[rows, lanes] = jnp.where(low, outs[0], outs[1]).astype(BF16)
        pltpu.make_async_copy(p_ref.at[w], p_out.at[w], out_sems.at[SAVES + w]).start()

    save(att_ref, att_out)
    wout_copy.wait()

    @pl.loop(0, tokens // big)
    def _(b):
        rows = pl.ds(pl.multiple_of(b * big, big), big)
        mid = (x_ref[rows, :].astype(F32) + mm(att_ref[rows, :], wout_ref[...])).astype(BF16)
        mid_ref[rows, :] = mid
        xhat, _ = normalised(mid.astype(F32))
        n2_ref[rows, :] = (xhat * gain2).astype(BF16)

    save(mid_ref, mid_out)
    for copy in cot_copies:
        copy.wait()
    for band in range(BANDS):
        for side in range(SIDES):
            w = band * SIDES + side
            cotw_ref[w * WIN:(w + 1) * WIN, :] = cot_buf[band, side].reshape(WIN, D)
    save(cotw_ref, cot_out)
    for copy in saves:
        copy.wait()
    for w in range(count):
        pltpu.make_async_copy(p_ref.at[w], p_out.at[w], out_sems.at[SAVES + w]).wait()


CHUNK = 512
ROWS = 4 * WIN


def mlp_chunk(chunk, n2_ref, cot_ref, wup_ref, wdown_ref, down_in, dn2_in, down_out, dn2_out, hid_ref, du_ref):
    at = pl.ds(pl.multiple_of(chunk * CHUNK, CHUNK), CHUNK)

    @pl.loop(0, n2_ref.shape[0] // ROWS)
    def _(b):
        rows = pl.ds(pl.multiple_of(b * ROWS, ROWS), ROWS)
        up = mm(n2_ref[rows, :], wup_ref[:, at])
        cdf, pdf = gelu_parts(up)
        hid = (up * cdf).astype(BF16)
        hid_ref[rows, :] = hid
        dhid = mm_t(cot_ref[rows, :], wdown_ref[at, :]).astype(BF16).astype(F32)
        du = (dhid * (cdf + up * pdf)).astype(BF16)
        du_ref[rows, :] = du
        down = mm(hid, wdown_ref[at, :])
        dn2 = mm_t(du, wup_ref[:, at])
        if down_in is None:
            down_out[rows, :] = down
            dn2_out[rows, :] = dn2
        else:
            down_out[rows, :] = down_in[rows, :] + down
            dn2_out[rows, :] = dn2_in[rows, :] + dn2

    return t_mm(n2_ref[...], du_ref[...]).astype(BF16), t_mm(hid_ref[...], cot_ref[...]).astype(BF16)


def send_kernel(me_ref, n2_ref, cot_ref, wup_ref, wdown_ref, down_ref, dn2_ref, grads_ref, hid_ref, du_ref):
    for i in range(2):
        carried = (down_ref, dn2_ref) if i else (None, None)
        grads = mlp_chunk((1 - me_ref[0]) * 2 + i, n2_ref, cot_ref, wup_ref, wdown_ref,
                          *carried, down_ref, dn2_ref, hid_ref, du_ref)
        for part, grad in enumerate(grads):
            grads_ref[(2 * part + i) * CHUNK:(2 * part + i + 1) * CHUNK, :] = grad


def keep_first_kernel(me_ref, n2_ref, cot_ref, wup_ref, wdown_ref, down_in, dn2_in,
                      down_ref, dn2_ref, early_ref, hid_ref, du_ref):
    grads = mlp_chunk(me_ref[0] * 2, n2_ref, cot_ref, wup_ref, wdown_ref,
                      down_in, dn2_in, down_ref, dn2_ref, hid_ref, du_ref)
    for part, grad in enumerate(grads):
        early_ref[part * CHUNK:(part + 1) * CHUNK, :] = grad


def keep_second_kernel(me_ref, n2_ref, cot_ref, wup_ref, wdown_ref, down_in, dn2_in, early_ref, got_ref,
                       down_hbm, dn2_hbm, grads_ref, hid_ref, du_ref, down_ref, dn2_ref, sems):
    grads = mlp_chunk(me_ref[0] * 2 + 1, n2_ref, cot_ref, wup_ref, wdown_ref,
                      down_in, dn2_in, down_ref, dn2_ref, hid_ref, du_ref)
    copies = [
        pltpu.make_async_copy(down_ref, down_hbm, sems.at[0]),
        pltpu.make_async_copy(dn2_ref, dn2_hbm, sems.at[1]),
    ]
    for copy in copies:
        copy.start()
    for part, grad in enumerate(grads):
        for i in range(2):
            rows = slice((2 * part + i) * CHUNK, (2 * part + i + 1) * CHUNK)
            mine = grad if i else early_ref[part * CHUNK:(part + 1) * CHUNK, :]
            grads_ref[rows, :] = (mine.astype(F32) + got_ref[rows, :].astype(F32)).astype(BF16)
    for copy in copies:
        copy.wait()


HALF = D // 2
CHIPS_N = 64
GRADS = 64
GAINS = 8


def att_grads(half, n1_ref, dqkv_ref, att_ref, dmid_ref, out_ref):
    per = D // (CHIPS_N // 4)
    lanes = pl.ds(pl.multiple_of(half * HALF, HALF), HALF)
    for part in range(4):
        if part < 3:
            part_lanes = pl.ds(pl.multiple_of(part * D + half * HALF, HALF), HALF)
            grad = t_mm(n1_ref[...], dqkv_ref[:, part_lanes])
        else:
            grad = t_mm(att_ref[...], dmid_ref[:, lanes])
        grad = grad.astype(BF16)
        first = part * (CHIPS_N // 4)
        for block in range(2):
            piece = grad[:, block * 128:(block + 1) * 128].reshape(CHIPS_N // 4, per, 128)
            out_ref[first:first + CHIPS_N // 4, block * per:(block + 1) * per, :] = piece


def att_back(first, last, datt_ref, qkv_ref, p_ref, dqkv_ref):
    low = lax.broadcasted_iota(jnp.int32, (WIN, PAIR), 1) < HD

    @pl.loop(first, last, unroll=4)
    def _(w):
        rows = pl.ds(pl.multiple_of(w * WIN, WIN), WIN)
        for pair in range(D // PAIR):
            lanes = slice(pair * PAIR, (pair + 1) * PAIR)
            q = qkv_ref[rows, pair * PAIR:(pair + 1) * PAIR]
            k = qkv_ref[rows, D + pair * PAIR:D + (pair + 1) * PAIR]
            v = qkv_ref[rows, 2 * D + pair * PAIR:2 * D + (pair + 1) * PAIR]
            da = datt_ref[rows, lanes]
            dqs, dks, dvs = [], [], []
            for h in range(2):
                mine = low if h == 0 else jnp.logical_not(low)
                vh = jnp.where(mine, v, jnp.zeros_like(v))
                p = p_ref[w, 2 * pair + h]
                pf = p.astype(F32)
                dp = mm_t(vh, da).astype(BF16).astype(F32)
                ds = (pf * (dp - jnp.sum(dp * pf, axis=0, keepdims=True))).astype(BF16)
                dvs.append(mm(p, da))
                dks.append(mm(ds, q))
                dqs.append(t_mm(ds, k))
            dqkv_ref[rows, pair * PAIR:(pair + 1) * PAIR] = (jnp.where(low, dqs[0], dqs[1]) * 0.125).astype(BF16)
            dqkv_ref[rows, D + pair * PAIR:D + (pair + 1) * PAIR] = jnp.where(low, dks[0], dks[1]).astype(BF16)
            dqkv_ref[rows, 2 * D + pair * PAIR:2 * D + (pair + 1) * PAIR] = jnp.where(low, dvs[0], dvs[1]).astype(BF16)


def start_loads(pairs, sems):
    loads = []
    for i, (source, target) in enumerate(pairs):
        loads.append(pltpu.make_async_copy(source, target, sems.at[i]))
        loads[-1].start()
    return loads


def back_kernel(cot_hbm, mid_hbm, down_hbm, dn2_hbm, wout_hbm, qkv_hbm, p_hbm, att_hbm, n1_hbm, g2_ref,
                res_out, dmid_out, dqkv_out, dg2_ref, att_ref, n1_ref, dmid_ref, dqkv_ref,
                cot_ref, mid_ref, down_ref, dn2_ref, wout_ref, qkv_ref, p_ref, datt_ref, res_ref, in_sems, sems):
    loads = start_loads((
        (cot_hbm, cot_ref), (mid_hbm, mid_ref), (down_hbm, down_ref), (dn2_hbm, dn2_ref),
        (wout_hbm, wout_ref), (qkv_hbm, qkv_ref), (p_hbm, p_ref), (att_hbm, att_ref), (n1_hbm, n1_ref),
    ), in_sems)
    gain2 = g2_ref[...]
    dg2_ref[...] = jnp.zeros_like(dg2_ref)
    tokens = cot_ref.shape[0]
    for load in loads[:4]:
        load.wait()

    @pl.loop(0, tokens // WIN, unroll=2)
    def _(b):
        rows = pl.ds(pl.multiple_of(b * WIN, WIN), WIN)
        mid = mid_ref[rows, :].astype(F32)
        res_ref[rows, :] = (mid + down_ref[rows, :]).astype(BF16)
        xhat, scale = normalised(mid)
        dn2 = dn2_ref[rows, :].astype(BF16).astype(F32)
        dg2_ref[...] += jnp.sum(dn2 * xhat, axis=0, keepdims=True)
        dmid = cot_ref[rows, :].astype(F32) + norm_pullback(xhat, scale, gain2, dn2)
        dmid_ref[rows, :] = dmid.astype(BF16)

    saves = [
        pltpu.make_async_copy(res_ref, res_out, sems.at[0]),
        pltpu.make_async_copy(dmid_ref, dmid_out, sems.at[1]),
    ]
    for copy in saves:
        copy.start()
    loads[4].wait()

    @pl.loop(0, tokens // ROWS)
    def _(b):
        rows = pl.ds(pl.multiple_of(b * ROWS, ROWS), ROWS)
        datt_ref[rows, :] = mm_t(dmid_ref[rows, :], wout_ref[...]).astype(BF16)

    loads[5].wait()
    loads[6].wait()
    att_back(0, tokens // WIN, datt_ref, qkv_ref, p_ref, dqkv_ref)
    saves.append(pltpu.make_async_copy(dqkv_ref, dqkv_out, sems.at[2]))
    saves[-1].start()
    for copy in loads[7:] + saves:
        copy.wait()


def tokens_kernel(dqkv_hbm, wqkv_hbm, x_hbm, dmid_hbm, res_hbm, g1_ref, after_ref,
                  out_ref, grad_ref, lon_ref, lat_ref, corner_ref, dg1_ref,
                  dqkv_ref, wqkv_ref, x_ref, dmid_ref, res_ref, dx_ref, res_buf, dx_buf, in_sems, sems):
    loads = start_loads((
        (res_hbm, res_ref), (dqkv_hbm, dqkv_ref), (wqkv_hbm, wqkv_ref), (x_hbm, x_ref), (dmid_hbm, dmid_ref),
    ), in_sems)
    gain1 = g1_ref[...]
    tokens = x_ref.shape[0]
    dg1_ref[...] = jnp.zeros_like(dg1_ref)
    loads[0].wait()
    for band in range(BANDS):
        for side in range(SIDES):
            w = band * SIDES + side
            res_buf[band, side] = res_ref[w * WIN:(w + 1) * WIN, :].reshape(WLAT, WLON, LEV, D)
    res_copies = scatter_windows(0, res_buf, out_ref, lon_ref, lat_ref, corner_ref, sems.at[0])
    for copy in res_copies:
        copy.start()
    for load in loads[1:]:
        load.wait()

    @pl.loop(0, tokens // ROWS)
    def _(b):
        rows = pl.ds(pl.multiple_of(b * ROWS, ROWS), ROWS)
        dn1 = mm_t(dqkv_ref[rows, :], wqkv_ref[...]).astype(BF16).astype(F32)
        xhat, scale = normalised(x_ref[rows, :].astype(F32))
        dg1_ref[...] += jnp.sum(dn1 * xhat, axis=0, keepdims=True)
        dx = dmid_ref[rows, :].astype(F32) + norm_pullback(xhat, scale, gain1, dn1)
        dx_ref[rows, :] = dx.astype(BF16)

    for band in range(BANDS):
        for side in range(SIDES):
            w = band * SIDES + side
            dx_buf[band, side] = dx_ref[w * WIN:(w + 1) * WIN, :].reshape(WLAT, WLON, LEV, D)
    dx_copies = scatter_windows(1, dx_buf, grad_ref, lon_ref, lat_ref, corner_ref, sems.at[1])
    for copy in dx_copies:
        copy.start()
    for copy in res_copies + dx_copies:
        copy.wait()


SHARE = FF // CHIPS_N
MLP = SHARE * D // 128
ALL = GRADS + GAINS + MLP


def total_of(parts_ref, rows):
    total = parts_ref[0, rows, :].astype(F32)
    for chip in range(1, CHIPS_N):
        total += parts_ref[chip, rows, :].astype(F32)
    return total.astype(BF16)


def half_kernel(half_ref, n1_ref, dqkv_ref, att_ref, dmid_ref, out_ref):
    att_grads(half_ref[0], n1_ref, dqkv_ref, att_ref, dmid_ref, out_ref)


def add_kernel(keep_ref, got_ref, out_ref):
    for chip in range(CHIPS_N):
        out_ref[chip] = (keep_ref[chip].astype(F32) + got_ref[chip].astype(F32)).astype(BF16)


def share_mlp_kernel(sums_ref, after_ref, tile_ref):
    del after_ref
    total = total_of(sums_ref, slice(0, SHARE))
    for block in range(D // 128):
        tile_ref[block * SHARE:(block + 1) * SHARE, :] = total[:, block * 128:(block + 1) * 128]


def share_kernel(parts_ref, tile_ref, dg1_ref, dg2_ref, out_ref, share_ref, sems):
    share_ref[GRADS + GAINS:, :] = tile_ref[...]
    share_ref[GRADS:GRADS + GAINS, :] = jnp.concatenate(
        [ref[:, block * 128:(block + 1) * 128] for ref in (dg1_ref, dg2_ref) for block in range(D // 128)]).astype(BF16)
    share_ref[0:GRADS, :] = total_of(parts_ref, slice(0, GRADS))
    copies = [pltpu.make_async_copy(share_ref, out_ref.at[chip], sems.at[chip]) for chip in range(CHIPS_N)]
    for copy in copies:
        copy.start()
    for copy in copies:
        copy.wait()


def unpack_kernel(mine, half_ref, all_ref, gains_in, *refs):
    (gup_hbm, gdown_hbm, gqkv_hbm, gout_hbm, gains_ref, gup_ref, gdown_ref, att_ref, sems) = refs if mine else refs[4:]
    half = half_ref[0]
    wide = FF // 2
    copies = []

    def send(source, target):
        copies.append(pltpu.make_async_copy(source, target, sems.at[len(copies)]))
        copies[-1].start()

    blocks = [(slice(GRADS + GAINS + i * SHARE, GRADS + GAINS + (i + 1) * SHARE), i * 128) for i in range(D // 128)]
    quarter = CHIPS_N // 4
    for rows, lane in blocks:
        gdown_ref[:, lane:lane + 128] = all_ref[2 * quarter:, rows, :].reshape(wide, 128).astype(F32)
    send(gdown_ref, gdown_hbm.at[pl.ds(pl.multiple_of(half * wide, wide), wide), :])
    for j in range(2):
        for rows, lane in blocks:
            piece = all_ref[j * quarter:(j + 1) * quarter, rows, :].reshape(D, 128)
            gup_ref[:, j * D + lane:j * D + lane + 128] = piece.astype(F32)
    send(gup_ref, gup_hbm.at[:, pl.ds(pl.multiple_of(half * wide, wide), wide)])
    per = GRADS // 2
    for part in range(4):
        for block in range(2):
            piece = all_ref[part * quarter:(part + 1) * quarter, block * per:(block + 1) * per, :].reshape(D, 128)
            att_ref[part, :, block * 128:(block + 1) * 128] = piece.astype(F32)
        out, first = (gqkv_hbm, part * D) if part < 3 else (gout_hbm, 0)
        send(att_ref.at[part], out.at[:, pl.ds(pl.multiple_of(half * HALF + first, HALF), HALF)])
    gains = all_ref[0, GRADS:GRADS + GAINS, :].astype(F32)
    for chip in range(1, CHIPS_N):
        gains += all_ref[chip, GRADS:GRADS + GAINS, :].astype(F32)
    gains_ref[...] = gains if mine else gains_in[...] + gains
    for copy in copies:
        copy.wait()


def pack_kernel(tok_ref, cot_ref, lon_ref, lat_ref, corner_ref, sems):
    copies = []
    for which, ref in enumerate((tok_ref, cot_ref)):
        below, right = pl.ds(HALF_LAT, ref.shape[0] - HALF_LAT), pl.ds(HALF_LON, ref.shape[1] - HALF_LON)
        top, left = pl.ds(0, HALF_LAT), pl.ds(0, HALF_LON)
        for i, (rows, cols, out) in enumerate(((below, left, lon_ref), (top, right, lat_ref), (top, left, corner_ref))):
            copies.append(pltpu.make_async_copy(ref.at[rows, cols], out.at[which], sems.at[which, i]))
    for copy in copies:
        copy.start()
    for copy in copies:
        copy.wait()


def place_kernel(out_in, grad_in, lon_ref, lat_ref, corner_ref, after_ref, out_ref, grad_ref, sems):
    del out_in, grad_in, after_ref
    copies = []
    for which, ref in enumerate((out_ref, grad_ref)):
        below, right = pl.ds(HALF_LAT, ref.shape[0] - HALF_LAT), pl.ds(HALF_LON, ref.shape[1] - HALF_LON)
        top, left = pl.ds(0, HALF_LAT), pl.ds(0, HALF_LON)
        for i, (rows, cols, rim) in enumerate(((below, left, lon_ref), (top, right, lat_ref), (top, left, corner_ref))):
            copies.append(pltpu.make_async_copy(rim.at[which], ref.at[rows, cols], sems.at[which, i]))
    for copy in copies:
        copy.start()
    for copy in copies:
        copy.wait()


def params(mib=32):
    return pltpu.CompilerParams(vmem_limit_bytes=mib * 2**20)


def cost(flops, moved):
    return pl.CostEstimate(flops=flops, bytes_accessed=moved, transcendentals=0)


def shape(dims, dtype=BF16):
    return jax.ShapeDtypeStruct(dims, dtype)


SM = pl.BlockSpec(memory_space=pltpu.SMEM)
VM = pl.BlockSpec(memory_space=pltpu.VMEM)


ANY = pl.BlockSpec(memory_space=pl.ANY)
HB = pl.BlockSpec(memory_space=pltpu.HBM)


def rim_shapes(rows, cols, levels):
    return [
        shape((2, rows - HALF_LAT, HALF_LON, levels, D)),
        shape((2, HALF_LAT, cols - HALF_LON, levels, D)),
        shape((2, HALF_LAT, HALF_LON, levels, D)),
    ]


def pack(tokens, cotangent):
    return pl.pallas_call(
        pack_kernel,
        name="pack",
        in_specs=[ANY] * 2,
        out_specs=[VM] * 3,
        out_shape=[local(rim.shape) for rim in rim_shapes(*tokens.shape[:3])],
        scratch_shapes=[pltpu.SemaphoreType.DMA((2, 3))],
    )(tokens, cotangent)


def place(output, grad, lon, lat, corner, after):
    return pl.pallas_call(
        place_kernel,
        name="place",
        in_specs=[ANY] * 2 + [VM] * 3 + [ANY],
        out_specs=[ANY] * 2,
        out_shape=[shape(output.shape), shape(grad.shape)],
        input_output_aliases={0: 0, 1: 1},
        scratch_shapes=[pltpu.SemaphoreType.DMA((2, 3))],
        cost_estimate=cost(10**9, 2**21),
    )(output, grad, lon, lat, corner, after)


WINDOWED = (BANDS, SIDES, WLAT, WLON, LEV, D)


def local(dims, dtype=BF16):
    return pltpu.VMEM(dims, dtype)


def held(*arrays):
    return [pltpu.with_memory_space_constraint(array, pltpu.VMEM) for array in arrays]


def far(*arrays):
    return [pltpu.with_memory_space_constraint(array, pltpu.HBM) for array in arrays]


def front(flag, tok, cot, lon, lat, corner, g1, wqkv, wout, g2):
    tokens = tok.size // D
    count = tokens // WIN
    saved = [(tokens, D), (tokens, D), (tokens, 3 * D), (count, D // HD, WIN, WIN), (tokens, D), (tokens, D)]
    return pl.pallas_call(
        front_kernel,
        name="front",
        in_specs=[SM] + [ANY] * 5 + [VM, HB, HB, VM],
        out_specs=[HB] * 7 + [VM] * 2,
        out_shape=[pltpu.HBM(dims, BF16) for dims in saved + [(tokens, D)]] + [local((tokens, D)), local((tokens, D))],
        scratch_shapes=[
            pltpu.VMEM(WINDOWED, BF16),
            pltpu.VMEM(WINDOWED, BF16),
        ] + [pltpu.VMEM(dims, BF16) for dims in saved] + [
            pltpu.VMEM((D, 3 * D), BF16),
            pltpu.VMEM((D, D), BF16),
            pltpu.SemaphoreType.DMA((2, STRIPS)),
            pltpu.SemaphoreType.DMA((SAVES + count,)),
            pltpu.SemaphoreType.DMA((2,)),
        ],
        compiler_params=params(),
        cost_estimate=cost(15 * 10**9, 10 * 2**20),
    )(flag, tok, cot, lon, lat, corner, g1, *far(wqkv, wout), g2)


def mlp(kind, me, n2, cot, wup, wdown, *carried):
    tokens = n2.shape[0]
    sums = [local((tokens, D), F32)] * 2
    scratch = [pltpu.VMEM((tokens, CHUNK), BF16)] * 2
    out_specs, aliases = [VM] * 3, {}
    if kind == "send":
        kernel, out_shape = send_kernel, sums + [shape((FF, D))]
    elif kind == "first":
        kernel, out_shape = keep_first_kernel, sums + [local((2 * CHUNK, D))]
        aliases = {5: 0, 6: 1}
    else:
        kernel, out_shape = keep_second_kernel, [pltpu.HBM((tokens, D), F32)] * 2 + [pltpu.HBM((FF, D), BF16)]
        out_specs = [HB, HB, VM]
        scratch = scratch + [pltpu.VMEM((tokens, D), F32)] * 2 + [pltpu.SemaphoreType.DMA((2,))]
    return pl.pallas_call(
        kernel,
        name="mlp_" + kind,
        in_specs=[SM, VM, VM, VM, VM] + [VM] * len(carried),
        out_specs=out_specs,
        out_shape=out_shape,
        scratch_shapes=scratch,
        input_output_aliases=aliases,
        compiler_params=params(),
        cost_estimate=cost((16 if kind == "send" else 8) * 10**9, 10 * 2**20),
    )(me, *held(n2, cot, wup, wdown, *carried))


def back(cot, mid, down, dn2, wout, qkv, p, att, n1, g2):
    tokens = cot.shape[0]
    count = tokens // WIN
    halves = pltpu.VMEM((tokens, D), BF16)
    full = pltpu.VMEM((tokens, D), F32)
    return pl.pallas_call(
        back_kernel,
        name="back",
        in_specs=[HB] * 9 + [VM],
        out_specs=[HB] * 3 + [VM] * 5,
        out_shape=[
            pltpu.HBM((tokens, D), BF16),
            pltpu.HBM((tokens, D), BF16),
            pltpu.HBM((tokens, 3 * D), BF16),
            shape((1, D), F32),
            local((tokens, D)),
            local((tokens, D)),
            local((tokens, D)),
            local((tokens, 3 * D)),
        ],
        scratch_shapes=[
            halves,
            halves,
            full,
            full,
            pltpu.VMEM((D, D), BF16),
            pltpu.VMEM((tokens, 3 * D), BF16),
            pltpu.VMEM((count, D // HD, WIN, WIN), BF16),
            halves,
            halves,
            pltpu.SemaphoreType.DMA((9,)),
            pltpu.SemaphoreType.DMA((3,)),
        ],
        compiler_params=params(40),
        cost_estimate=cost(25 * 10**9, 10 * 2**20),
    )(*far(cot, mid, down, dn2, wout, qkv, p, att, n1), g2)


def token_grads(dqkv, wqkv, x, dmid, res, g1, after, field):
    tokens = x.shape[0]
    halves = pltpu.VMEM((tokens, D), BF16)
    return pl.pallas_call(
        tokens_kernel,
        name="tokens",
        in_specs=[HB] * 5 + [VM, ANY],
        out_specs=[ANY] * 5 + [VM],
        out_shape=[shape(field), shape(field)] + rim_shapes(*field[:3]) + [shape((1, D), F32)],
        scratch_shapes=[
            pltpu.VMEM((tokens, 3 * D), BF16),
            pltpu.VMEM((D, 3 * D), BF16),
            halves,
            halves,
            halves,
            halves,
            pltpu.VMEM(WINDOWED, BF16),
            pltpu.VMEM(WINDOWED, BF16),
            pltpu.SemaphoreType.DMA((5,)),
            pltpu.SemaphoreType.DMA((2, STRIPS)),
        ],
        compiler_params=params(),
        cost_estimate=cost(6 * 10**9, 10 * 2**20),
    )(*far(dqkv, wqkv, x, dmid, res), g1, after)


def half_grads(name, half, n1, dqkv, att, dmid):
    return pl.pallas_call(
        half_kernel,
        name=name,
        in_specs=[SM] + [VM] * 4,
        out_specs=VM,
        out_shape=local((CHIPS_N, GRADS, 128)),
        compiler_params=params(),
        cost_estimate=cost(4 * 10**9, 4 * 2**20),
    )(half, *held(n1, dqkv, att, dmid))


def simple(kernel, name, out_shape, *operands, specs=None, scratch=(), mib=56):
    return pl.pallas_call(
        kernel,
        name=name,
        in_specs=specs or [VM] * len(operands),
        out_specs=VM if not scratch else HB,
        out_shape=out_shape,
        scratch_shapes=scratch,
        compiler_params=params(mib),
        cost_estimate=cost(10**9, 4 * 2**20),
    )(*operands)


def unpack(half, gathered, carried=None):
    mine = carried is None
    outs = [pltpu.HBM((D, FF), F32), pltpu.HBM((FF, D), F32), pltpu.HBM((D, 3 * D), F32), pltpu.HBM((D, D), F32)]
    gains = jnp.zeros((GAINS, 128), F32) if mine else carried[4]
    return pl.pallas_call(
        functools.partial(unpack_kernel, mine),
        name="unpack_mine" if mine else "unpack_theirs",
        in_specs=[SM, VM, VM] + ([] if mine else [HB] * 4),
        out_specs=[HB] * 4 + [VM],
        out_shape=outs + [shape((GAINS, 128), F32)],
        scratch_shapes=[
            pltpu.VMEM((D, FF // 2), F32),
            pltpu.VMEM((FF // 2, D), F32),
            pltpu.VMEM((4, D, HALF), F32),
            pltpu.SemaphoreType.DMA((6,)),
        ],
        input_output_aliases={} if mine else {3: 0, 4: 1, 5: 2, 6: 3},
        compiler_params=params(40),
        cost_estimate=cost(10**9, 10 * 2**20),
    )(half, gathered, gains, *([] if mine else far(*carried[:4])))


LAT = ("x", "zl")
LON = ("zh", "y", "c")
CHIPS = ("y", "x", "zh", "zl")


def send_rims(lon, lat, corner, distance):
    lats, lons = lax.axis_size(LAT), lax.axis_size(LON)
    moved = []
    for block, down, across in ((lon, 0, distance), (lat, distance, 0), (corner, distance, distance)):
        route = [
            (i * lons + j, (i + down) % lats * lons + (j + across) % lons)
            for i in range(lats) for j in range(lons)
        ]
        moved.append(lax.ppermute(block, LAT + LON, route))
    return moved


def other_core(block):
    return lax.ppermute(block, "c", [(0, 1), (1, 0)])


def exchange(parts):
    return lax.all_to_all(parts, CHIPS, 0, 0, tiled=True)


def shards(tokens, cotangent, norm_gain, w_qkv, w_out, mlp_gain, w_up, w_down):
    g1 = norm_gain.reshape(1, D)
    g2 = mlp_gain.reshape(1, D)
    last_band = lax.axis_index(LAT) == lax.axis_size(LAT) - 1
    flag = last_band.astype(jnp.int32).reshape(1)
    me = lax.axis_index("c").astype(jnp.int32).reshape(1)

    rims = send_rims(*pack(tokens, cotangent), -1)
    x, n1, qkv, p, att, mid, cot_far, cot, n2 = front(flag, tokens, cotangent, *rims, g1, w_qkv, w_out, g2)
    fixed = (me, n2, cot, w_up, w_down)
    down, dn2, grads = mlp("send", *fixed)
    got = other_core(grads)
    down, dn2, early = mlp("first", *fixed, down, dn2)
    down, dn2, grads = mlp("second", *fixed, down, dn2, early, got)
    sums = exchange(grads.reshape(CHIPS_N, SHARE, D))
    res, dmid_far, dqkv_far, dg2, att, n1, dmid, dqkv = back(cot_far, mid, down, dn2, w_out, qkv, p, att, n1, g2)
    got = other_core(half_grads("send", 1 - me, n1, dqkv, att, dmid))
    keep = half_grads("keep", me, n1, dqkv, att, dmid)
    added = simple(add_kernel, "add", pltpu.HBM((CHIPS_N, GRADS, 128), BF16), *held(keep, got), mib=32)
    att_sums = exchange(added)
    tile = simple(share_mlp_kernel, "share_mlp", shape((MLP, 128)), sums, added, specs=[VM, ANY])
    output, grad_tokens, lon, lat, corner, dg1 = token_grads(
        dqkv_far, w_qkv, x, dmid_far, res, g1, added, tokens.shape)
    att_sums, tile, dg1 = lax.optimization_barrier((att_sums, tile, dg1))
    rims = send_rims(lon, lat, corner, 1)
    shares = simple(
        share_kernel, "share", pltpu.HBM((CHIPS_N, ALL, 128), BF16), *held(att_sums), tile, dg1, dg2, mib=32,
        scratch=[pltpu.VMEM((ALL, 128), BF16), pltpu.SemaphoreType.DMA((CHIPS_N,))])
    gathered = exchange(shares)
    theirs = other_core(gathered)
    grads = unpack(1 - me, theirs, unpack(me, gathered))
    output, grad_tokens = place(output, grad_tokens, *rims, grads[4])
    gup, gdown, gqkv, gout, gains = grads
    gains = gains.reshape(2, D)
    return (output, grad_tokens, gains[0], gqkv, gout, gains[1], gup, gdown)


def solution(mesh):
    field = P(LAT, LON, None, None)
    mesh = jax.sharding.Mesh(mesh.devices.reshape(4, 2, 2, 4, 2), ("x", "zl", "zh", "y", "c"))
    return jax.shard_map(
        shards,
        mesh=mesh,
        in_specs=(field, field, P(), P(), P(), P(), P(), P()),
        out_specs=(field, field, P(), P(), P(), P(), P(), P()),
        check_vma=False,
    )
```

```python
import functools

import jax
import jax.numpy as jnp
from jax import lax
from jax.experimental import pallas as pl
from jax.experimental.pallas import tpu as pltpu
from jax.sharding import PartitionSpec as P

HD = 64
WLAT = 6
WLON = 12
LEV = 2
WIN = WLAT * WLON * LEV
D = 512
FF = 2048
HALF_LAT = WLAT // 2
HALF_LON = WLON // 2
EPS = 1e-05
F32 = jnp.float32
BF16 = jnp.bfloat16
PAIR = 2 * HD


def mm(a, b):
    return lax.dot_general(a, b, (((1,), (0,)), ((), ())), preferred_element_type=F32)


def mm_t(a, b):
    return lax.dot_general(a, b, (((1,), (1,)), ((), ())), preferred_element_type=F32)


def t_mm(a, b):
    return lax.dot_general(a, b, (((0,), (0,)), ((), ())), preferred_element_type=F32)


def normalised(values):
    mean = jnp.mean(values, axis=-1, keepdims=True)
    centred = values - mean
    var = jnp.mean(centred * centred, axis=-1, keepdims=True)
    scale = lax.rsqrt(var + EPS)
    return centred * scale, scale


def norm_pullback(xhat, scale, gain, grad):
    dxhat = grad * gain
    m1 = jnp.mean(dxhat, axis=-1, keepdims=True)
    m2 = jnp.mean(dxhat * xhat, axis=-1, keepdims=True)
    return scale * (dxhat - m1 - xhat * m2)


def gelu_parts(x):
    a = jnp.abs(x)
    t = 1.0 / (1.0 + (0.3275911 * 0.7071067811865476) * a)
    e = jnp.exp(-0.5 * x * x)
    poly = t * (0.127414796 + t * (-0.142248368 + t * (0.7107068705 + t * (-0.7265760135 + t * 0.5307027145))))
    tail = poly * e
    cdf = jnp.where(x >= 0.0, 1.0 - tail, tail)
    return cdf, 0.3989422804014327 * e


BANDS = 4
SIDES = 2


def strips():
    for band in range(BANDS):
        first = HALF_LAT + band * WLAT
        last = band == BANDS - 1
        across = [(0, WLAT, first, False)]
        if last:
            across = [(0, HALF_LAT, first, False), (HALF_LAT, HALF_LAT, 0, True)]
        for side in range(SIDES):
            left = HALF_LON + side * WLON
            along = [(0, WLON, left, False)]
            if side == SIDES - 1:
                along = [(0, HALF_LON, left, False), (HALF_LON, HALF_LON, 0, True)]
            for at_row, rows, row, far_row in across:
                for at_col, cols, col, far_col in along:
                    piece = 2 * far_row + far_col
                    if far_row and not far_col:
                        col -= HALF_LON
                    if far_col and not far_row:
                        row -= HALF_LAT
                    yield (
                        band, side, pl.ds(at_row, rows), pl.ds(at_col, cols),
                        piece, pl.ds(row, rows), pl.ds(col, cols),
                    )


SAVES = 6
STRIPS = len(list(strips()))


def gather_windows(which, field, rim_lon, rim_lat, corner, buffer, sems):
    copies = []
    for i, (band, side, to_rows, to_cols, piece, rows, cols) in enumerate(strips()):
        source = field if piece == 0 else (None, rim_lon, rim_lat, corner)[piece].at[which]
        copies.append(pltpu.make_async_copy(
            source.at[rows, cols], buffer.at[band, side, to_rows, to_cols], sems.at[i]))
    return copies


def scatter_windows(which, buffer, field, rim_lon, rim_lat, corner, sems):
    copies = []
    for i, (band, side, to_rows, to_cols, piece, rows, cols) in enumerate(strips()):
        target = field if piece == 0 else (None, rim_lon, rim_lat, corner)[piece].at[which]
        copies.append(pltpu.make_async_copy(
            buffer.at[band, side, to_rows, to_cols], target.at[rows, cols], sems.at[i]))
    return copies


def front_kernel(flag_ref, tok_ref, cot_ref, lon_ref, lat_ref, corner_ref, g1_ref, wqkv_hbm, wout_hbm, g2_ref,
                 x_out, n1_out, qkv_out, p_out, att_out, mid_out, cot_out, cotw_ref, n2_ref,
                 tok_buf, cot_buf, x_ref, n1_ref, qkv_ref, p_ref, att_ref, mid_ref, wqkv_ref, wout_ref,
                 sems, out_sems, w_sems):
    wqkv_copy = pltpu.make_async_copy(wqkv_hbm, wqkv_ref, w_sems.at[0])
    wout_copy = pltpu.make_async_copy(wout_hbm, wout_ref, w_sems.at[1])
    saves = []

    def save(source, target):
        copy = pltpu.make_async_copy(source, target, out_sems.at[len(saves)])
        copy.start()
        saves.append(copy)

    tok_copies = gather_windows(0, tok_ref, lon_ref, lat_ref, corner_ref, tok_buf, sems.at[0])
    cot_copies = gather_windows(1, cot_ref, lon_ref, lat_ref, corner_ref, cot_buf, sems.at[1])
    for copy in tok_copies + [wqkv_copy, wout_copy] + cot_copies:
        copy.start()
    for copy in tok_copies:
        copy.wait()
    for band in range(BANDS):
        for side in range(SIDES):
            w = band * SIDES + side
            x_ref[w * WIN:(w + 1) * WIN, :] = tok_buf[band, side].reshape(WIN, D)
    save(x_ref, x_out)
    tokens = x_ref.shape[0]
    count = tokens // WIN
    per_row = count // 4
    gain1 = g1_ref[...]
    gain2 = g2_ref[...]

    @pl.loop(0, count, unroll=2)
    def _(w):
        rows = pl.ds(pl.multiple_of(w * WIN, WIN), WIN)
        xhat, _ = normalised(x_ref[rows, :].astype(F32))
        n1_ref[rows, :] = (xhat * gain1).astype(BF16)

    wqkv_copy.wait()

    big = tokens

    @pl.loop(0, tokens // big)
    def _(b):
        rows = pl.ds(pl.multiple_of(b * big, big), big)
        n1 = n1_ref[rows, :]
        qkv_ref[rows, 0:D] = (mm(n1, wqkv_ref[:, 0:D]).astype(BF16) * 0.125).astype(BF16)
        qkv_ref[rows, D:2 * D] = mm(n1, wqkv_ref[:, D:2 * D]).astype(BF16)
        qkv_ref[rows, 2 * D:3 * D] = mm(n1, wqkv_ref[:, 2 * D:3 * D]).astype(BF16)

    save(n1_ref, n1_out)
    save(qkv_ref, qkv_out)

    key_group = lax.broadcasted_iota(jnp.int32, (WIN, WIN), 0) >= WIN // 2
    query_group = lax.broadcasted_iota(jnp.int32, (WIN, WIN), 1) >= WIN // 2
    split = key_group != query_group
    low = lax.broadcasted_iota(jnp.int32, (WIN, PAIR), 1) < HD

    @pl.loop(0, count, unroll=4)
    def _(w):
        rows = pl.ds(pl.multiple_of(w * WIN, WIN), WIN)
        cut = jnp.logical_and(flag_ref[0] == 1, w >= count - per_row)
        masked = jnp.logical_and(split, cut)
        for pair in range(D // PAIR):
            lanes = slice(pair * PAIR, (pair + 1) * PAIR)
            q = qkv_ref[rows, pair * PAIR:(pair + 1) * PAIR]
            k = qkv_ref[rows, D + pair * PAIR:D + (pair + 1) * PAIR]
            v = qkv_ref[rows, 2 * D + pair * PAIR:2 * D + (pair + 1) * PAIR]
            outs = []
            for h in range(2):
                mine = low if h == 0 else jnp.logical_not(low)
                kh = jnp.where(mine, k, jnp.zeros_like(k))
                s = mm_t(kh, q)
                s = jnp.where(masked, -1000000000.0, s)
                e = jnp.exp(s - jnp.max(s, axis=0, keepdims=True))
                p = (e * (1.0 / jnp.sum(e, axis=0, keepdims=True))).astype(BF16)
                p_ref[w, 2 * pair + h] = p
                outs.append(t_mm(p, v))
            att_ref[rows, lanes] = jnp.where(low, outs[0], outs[1]).astype(BF16)
        pltpu.make_async_copy(p_ref.at[w], p_out.at[w], out_sems.at[SAVES + w]).start()

    save(att_ref, att_out)
    wout_copy.wait()

    @pl.loop(0, tokens // big)
    def _(b):
        rows = pl.ds(pl.multiple_of(b * big, big), big)
        mid = (x_ref[rows, :].astype(F32) + mm(att_ref[rows, :], wout_ref[...])).astype(BF16)
        mid_ref[rows, :] = mid
        xhat, _ = normalised(mid.astype(F32))
        n2_ref[rows, :] = (xhat * gain2).astype(BF16)

    save(mid_ref, mid_out)
    for copy in cot_copies:
        copy.wait()
    for band in range(BANDS):
        for side in range(SIDES):
            w = band * SIDES + side
            cotw_ref[w * WIN:(w + 1) * WIN, :] = cot_buf[band, side].reshape(WIN, D)
    save(cotw_ref, cot_out)
    for copy in saves:
        copy.wait()
    for w in range(count):
        pltpu.make_async_copy(p_ref.at[w], p_out.at[w], out_sems.at[SAVES + w]).wait()


CHUNK = 512
ROWS = 4 * WIN


def mlp_chunk(chunk, n2_ref, cot_ref, wup_ref, wdown_ref, down_in, dn2_in, down_out, dn2_out, hid_ref, du_ref):
    at = pl.ds(pl.multiple_of(chunk * CHUNK, CHUNK), CHUNK)

    @pl.loop(0, n2_ref.shape[0] // ROWS)
    def _(b):
        rows = pl.ds(pl.multiple_of(b * ROWS, ROWS), ROWS)
        up = mm(n2_ref[rows, :], wup_ref[:, at])
        cdf, pdf = gelu_parts(up)
        hid = (up * cdf).astype(BF16)
        hid_ref[rows, :] = hid
        dhid = mm_t(cot_ref[rows, :], wdown_ref[at, :]).astype(BF16).astype(F32)
        du = (dhid * (cdf + up * pdf)).astype(BF16)
        du_ref[rows, :] = du
        down = mm(hid, wdown_ref[at, :])
        dn2 = mm_t(du, wup_ref[:, at])
        if down_in is None:
            down_out[rows, :] = down
            dn2_out[rows, :] = dn2
        else:
            down_out[rows, :] = down_in[rows, :] + down
            dn2_out[rows, :] = dn2_in[rows, :] + dn2

    return t_mm(n2_ref[...], du_ref[...]).astype(BF16), t_mm(hid_ref[...], cot_ref[...]).astype(BF16)


def send_kernel(me_ref, n2_ref, cot_ref, wup_ref, wdown_ref, down_ref, dn2_ref, grads_ref, hid_ref, du_ref):
    for i in range(2):
        carried = (down_ref, dn2_ref) if i else (None, None)
        grads = mlp_chunk((1 - me_ref[0]) * 2 + i, n2_ref, cot_ref, wup_ref, wdown_ref,
                          *carried, down_ref, dn2_ref, hid_ref, du_ref)
        for part, grad in enumerate(grads):
            grads_ref[(2 * part + i) * CHUNK:(2 * part + i + 1) * CHUNK, :] = grad


def keep_first_kernel(me_ref, n2_ref, cot_ref, wup_ref, wdown_ref, down_in, dn2_in,
                      down_ref, dn2_ref, early_ref, hid_ref, du_ref):
    grads = mlp_chunk(me_ref[0] * 2, n2_ref, cot_ref, wup_ref, wdown_ref,
                      down_in, dn2_in, down_ref, dn2_ref, hid_ref, du_ref)
    for part, grad in enumerate(grads):
        early_ref[part * CHUNK:(part + 1) * CHUNK, :] = grad


def keep_second_kernel(me_ref, n2_ref, cot_ref, wup_ref, wdown_ref, down_in, dn2_in, early_ref, got_ref,
                       down_hbm, dn2_hbm, grads_ref, hid_ref, du_ref, down_ref, dn2_ref, sems):
    grads = mlp_chunk(me_ref[0] * 2 + 1, n2_ref, cot_ref, wup_ref, wdown_ref,
                      down_in, dn2_in, down_ref, dn2_ref, hid_ref, du_ref)
    copies = [
        pltpu.make_async_copy(down_ref, down_hbm, sems.at[0]),
        pltpu.make_async_copy(dn2_ref, dn2_hbm, sems.at[1]),
    ]
    for copy in copies:
        copy.start()
    for part, grad in enumerate(grads):
        for i in range(2):
            rows = slice((2 * part + i) * CHUNK, (2 * part + i + 1) * CHUNK)
            mine = grad if i else early_ref[part * CHUNK:(part + 1) * CHUNK, :]
            grads_ref[rows, :] = (mine.astype(F32) + got_ref[rows, :].astype(F32)).astype(BF16)
    for copy in copies:
        copy.wait()


HALF = D // 2
CHIPS_N = 64
GRADS = 64
GAINS = 8


def att_grads(half, n1_ref, dqkv_ref, att_ref, dmid_ref, out_ref):
    per = D // (CHIPS_N // 4)
    lanes = pl.ds(pl.multiple_of(half * HALF, HALF), HALF)
    for part in range(4):
        if part < 3:
            part_lanes = pl.ds(pl.multiple_of(part * D + half * HALF, HALF), HALF)
            grad = t_mm(n1_ref[...], dqkv_ref[:, part_lanes])
        else:
            grad = t_mm(att_ref[...], dmid_ref[:, lanes])
        grad = grad.astype(BF16)
        first = part * (CHIPS_N // 4)
        for block in range(2):
            piece = grad[:, block * 128:(block + 1) * 128].reshape(CHIPS_N // 4, per, 128)
            out_ref[first:first + CHIPS_N // 4, block * per:(block + 1) * per, :] = piece


def att_back(first, last, datt_ref, qkv_ref, p_ref, dqkv_ref):
    low = lax.broadcasted_iota(jnp.int32, (WIN, PAIR), 1) < HD

    @pl.loop(first, last, unroll=4)
    def _(w):
        rows = pl.ds(pl.multiple_of(w * WIN, WIN), WIN)
        for pair in range(D // PAIR):
            lanes = slice(pair * PAIR, (pair + 1) * PAIR)
            q = qkv_ref[rows, pair * PAIR:(pair + 1) * PAIR]
            k = qkv_ref[rows, D + pair * PAIR:D + (pair + 1) * PAIR]
            v = qkv_ref[rows, 2 * D + pair * PAIR:2 * D + (pair + 1) * PAIR]
            da = datt_ref[rows, lanes]
            dqs, dks, dvs = [], [], []
            for h in range(2):
                mine = low if h == 0 else jnp.logical_not(low)
                vh = jnp.where(mine, v, jnp.zeros_like(v))
                p = p_ref[w, 2 * pair + h]
                pf = p.astype(F32)
                dp = mm_t(vh, da).astype(BF16).astype(F32)
                ds = (pf * (dp - jnp.sum(dp * pf, axis=0, keepdims=True))).astype(BF16)
                dvs.append(mm(p, da))
                dks.append(mm(ds, q))
                dqs.append(t_mm(ds, k))
            dqkv_ref[rows, pair * PAIR:(pair + 1) * PAIR] = (jnp.where(low, dqs[0], dqs[1]) * 0.125).astype(BF16)
            dqkv_ref[rows, D + pair * PAIR:D + (pair + 1) * PAIR] = jnp.where(low, dks[0], dks[1]).astype(BF16)
            dqkv_ref[rows, 2 * D + pair * PAIR:2 * D + (pair + 1) * PAIR] = jnp.where(low, dvs[0], dvs[1]).astype(BF16)


def start_loads(pairs, sems):
    loads = []
    for i, (source, target) in enumerate(pairs):
        loads.append(pltpu.make_async_copy(source, target, sems.at[i]))
        loads[-1].start()
    return loads


def back_kernel(cot_hbm, mid_hbm, down_hbm, dn2_hbm, wout_hbm, qkv_hbm, p_hbm, att_hbm, n1_hbm, g2_ref,
                res_out, dmid_out, dqkv_out, dg2_ref, att_ref, n1_ref, dmid_ref, dqkv_ref,
                cot_ref, mid_ref, down_ref, dn2_ref, wout_ref, qkv_ref, p_ref, datt_ref, res_ref, in_sems, sems):
    loads = start_loads((
        (cot_hbm, cot_ref), (mid_hbm, mid_ref), (down_hbm, down_ref), (dn2_hbm, dn2_ref),
        (wout_hbm, wout_ref), (qkv_hbm, qkv_ref), (p_hbm, p_ref), (att_hbm, att_ref), (n1_hbm, n1_ref),
    ), in_sems)
    gain2 = g2_ref[...]
    dg2_ref[...] = jnp.zeros_like(dg2_ref)
    tokens = cot_ref.shape[0]
    for load in loads[:4]:
        load.wait()

    @pl.loop(0, tokens // WIN, unroll=2)
    def _(b):
        rows = pl.ds(pl.multiple_of(b * WIN, WIN), WIN)
        mid = mid_ref[rows, :].astype(F32)
        res_ref[rows, :] = (mid + down_ref[rows, :]).astype(BF16)
        xhat, scale = normalised(mid)
        dn2 = dn2_ref[rows, :].astype(BF16).astype(F32)
        dg2_ref[...] += jnp.sum(dn2 * xhat, axis=0, keepdims=True)
        dmid = cot_ref[rows, :].astype(F32) + norm_pullback(xhat, scale, gain2, dn2)
        dmid_ref[rows, :] = dmid.astype(BF16)

    saves = [
        pltpu.make_async_copy(res_ref, res_out, sems.at[0]),
        pltpu.make_async_copy(dmid_ref, dmid_out, sems.at[1]),
    ]
    for copy in saves:
        copy.start()
    loads[4].wait()

    @pl.loop(0, tokens // ROWS)
    def _(b):
        rows = pl.ds(pl.multiple_of(b * ROWS, ROWS), ROWS)
        datt_ref[rows, :] = mm_t(dmid_ref[rows, :], wout_ref[...]).astype(BF16)

    loads[5].wait()
    loads[6].wait()
    att_back(0, tokens // WIN, datt_ref, qkv_ref, p_ref, dqkv_ref)
    saves.append(pltpu.make_async_copy(dqkv_ref, dqkv_out, sems.at[2]))
    saves[-1].start()
    for copy in loads[7:] + saves:
        copy.wait()


def tokens_kernel(dqkv_hbm, wqkv_hbm, x_hbm, dmid_hbm, res_hbm, g1_ref, after_ref,
                  out_ref, grad_ref, lon_ref, lat_ref, corner_ref, dg1_ref,
                  dqkv_ref, wqkv_ref, x_ref, dmid_ref, res_ref, dx_ref, res_buf, dx_buf, in_sems, sems):
    loads = start_loads((
        (res_hbm, res_ref), (dqkv_hbm, dqkv_ref), (wqkv_hbm, wqkv_ref), (x_hbm, x_ref), (dmid_hbm, dmid_ref),
    ), in_sems)
    gain1 = g1_ref[...]
    tokens = x_ref.shape[0]
    dg1_ref[...] = jnp.zeros_like(dg1_ref)
    loads[0].wait()
    for band in range(BANDS):
        for side in range(SIDES):
            w = band * SIDES + side
            res_buf[band, side] = res_ref[w * WIN:(w + 1) * WIN, :].reshape(WLAT, WLON, LEV, D)
    res_copies = scatter_windows(0, res_buf, out_ref, lon_ref, lat_ref, corner_ref, sems.at[0])
    for copy in res_copies:
        copy.start()
    for load in loads[1:]:
        load.wait()

    @pl.loop(0, tokens // ROWS)
    def _(b):
        rows = pl.ds(pl.multiple_of(b * ROWS, ROWS), ROWS)
        dn1 = mm_t(dqkv_ref[rows, :], wqkv_ref[...]).astype(BF16).astype(F32)
        xhat, scale = normalised(x_ref[rows, :].astype(F32))
        dg1_ref[...] += jnp.sum(dn1 * xhat, axis=0, keepdims=True)
        dx = dmid_ref[rows, :].astype(F32) + norm_pullback(xhat, scale, gain1, dn1)
        dx_ref[rows, :] = dx.astype(BF16)

    for band in range(BANDS):
        for side in range(SIDES):
            w = band * SIDES + side
            dx_buf[band, side] = dx_ref[w * WIN:(w + 1) * WIN, :].reshape(WLAT, WLON, LEV, D)
    dx_copies = scatter_windows(1, dx_buf, grad_ref, lon_ref, lat_ref, corner_ref, sems.at[1])
    for copy in dx_copies:
        copy.start()
    for copy in res_copies + dx_copies:
        copy.wait()


SHARE = FF // CHIPS_N
MLP = SHARE * D // 128
ALL = GRADS + GAINS + MLP


def total_of(parts_ref, rows):
    total = parts_ref[0, rows, :].astype(F32)
    for chip in range(1, CHIPS_N):
        total += parts_ref[chip, rows, :].astype(F32)
    return total.astype(BF16)


def half_kernel(half_ref, n1_ref, dqkv_ref, att_ref, dmid_ref, out_ref):
    att_grads(half_ref[0], n1_ref, dqkv_ref, att_ref, dmid_ref, out_ref)


def add_kernel(keep_ref, got_ref, out_ref):
    for chip in range(CHIPS_N):
        out_ref[chip] = (keep_ref[chip].astype(F32) + got_ref[chip].astype(F32)).astype(BF16)


def share_mlp_kernel(sums_ref, after_ref, tile_ref):
    del after_ref
    total = total_of(sums_ref, slice(0, SHARE))
    for block in range(D // 128):
        tile_ref[block * SHARE:(block + 1) * SHARE, :] = total[:, block * 128:(block + 1) * 128]


def share_kernel(parts_ref, tile_ref, dg1_ref, dg2_ref, out_ref, share_ref, sems):
    share_ref[GRADS + GAINS:, :] = tile_ref[...]
    share_ref[GRADS:GRADS + GAINS, :] = jnp.concatenate(
        [ref[:, block * 128:(block + 1) * 128] for ref in (dg1_ref, dg2_ref) for block in range(D // 128)]).astype(BF16)
    share_ref[0:GRADS, :] = total_of(parts_ref, slice(0, GRADS))
    copies = [pltpu.make_async_copy(share_ref, out_ref.at[chip], sems.at[chip]) for chip in range(CHIPS_N)]
    for copy in copies:
        copy.start()
    for copy in copies:
        copy.wait()


def unpack_kernel(mine, half_ref, all_ref, gains_in, *refs):
    (gup_hbm, gdown_hbm, gqkv_hbm, gout_hbm, gains_ref, gup_ref, gdown_ref, att_ref, sems) = refs if mine else refs[4:]
    half = half_ref[0]
    wide = FF // 2
    copies = []

    def send(source, target):
        copies.append(pltpu.make_async_copy(source, target, sems.at[len(copies)]))
        copies[-1].start()

    blocks = [(slice(GRADS + GAINS + i * SHARE, GRADS + GAINS + (i + 1) * SHARE), i * 128) for i in range(D // 128)]
    quarter = CHIPS_N // 4
    for rows, lane in blocks:
        gdown_ref[:, lane:lane + 128] = all_ref[2 * quarter:, rows, :].reshape(wide, 128).astype(F32)
    send(gdown_ref, gdown_hbm.at[pl.ds(pl.multiple_of(half * wide, wide), wide), :])
    for j in range(2):
        for rows, lane in blocks:
            piece = all_ref[j * quarter:(j + 1) * quarter, rows, :].reshape(D, 128)
            gup_ref[:, j * D + lane:j * D + lane + 128] = piece.astype(F32)
    send(gup_ref, gup_hbm.at[:, pl.ds(pl.multiple_of(half * wide, wide), wide)])
    per = GRADS // 2
    for part in range(4):
        for block in range(2):
            piece = all_ref[part * quarter:(part + 1) * quarter, block * per:(block + 1) * per, :].reshape(D, 128)
            att_ref[part, :, block * 128:(block + 1) * 128] = piece.astype(F32)
        out, first = (gqkv_hbm, part * D) if part < 3 else (gout_hbm, 0)
        send(att_ref.at[part], out.at[:, pl.ds(pl.multiple_of(half * HALF + first, HALF), HALF)])
    gains = all_ref[0, GRADS:GRADS + GAINS, :].astype(F32)
    for chip in range(1, CHIPS_N):
        gains += all_ref[chip, GRADS:GRADS + GAINS, :].astype(F32)
    gains_ref[...] = gains if mine else gains_in[...] + gains
    for copy in copies:
        copy.wait()


def pack_kernel(tok_ref, cot_ref, lon_ref, lat_ref, corner_ref, sems):
    copies = []
    for which, ref in enumerate((tok_ref, cot_ref)):
        below, right = pl.ds(HALF_LAT, ref.shape[0] - HALF_LAT), pl.ds(HALF_LON, ref.shape[1] - HALF_LON)
        top, left = pl.ds(0, HALF_LAT), pl.ds(0, HALF_LON)
        for i, (rows, cols, out) in enumerate(((below, left, lon_ref), (top, right, lat_ref), (top, left, corner_ref))):
            copies.append(pltpu.make_async_copy(ref.at[rows, cols], out.at[which], sems.at[which, i]))
    for copy in copies:
        copy.start()
    for copy in copies:
        copy.wait()


def place_kernel(out_in, grad_in, lon_ref, lat_ref, corner_ref, after_ref, out_ref, grad_ref, sems):
    del out_in, grad_in, after_ref
    copies = []
    for which, ref in enumerate((out_ref, grad_ref)):
        below, right = pl.ds(HALF_LAT, ref.shape[0] - HALF_LAT), pl.ds(HALF_LON, ref.shape[1] - HALF_LON)
        top, left = pl.ds(0, HALF_LAT), pl.ds(0, HALF_LON)
        for i, (rows, cols, rim) in enumerate(((below, left, lon_ref), (top, right, lat_ref), (top, left, corner_ref))):
            copies.append(pltpu.make_async_copy(rim.at[which], ref.at[rows, cols], sems.at[which, i]))
    for copy in copies:
        copy.start()
    for copy in copies:
        copy.wait()


def params(mib=32):
    return pltpu.CompilerParams(vmem_limit_bytes=mib * 2**20)


def cost(flops, moved):
    return pl.CostEstimate(flops=flops, bytes_accessed=moved, transcendentals=0)


def shape(dims, dtype=BF16):
    return jax.ShapeDtypeStruct(dims, dtype)


SM = pl.BlockSpec(memory_space=pltpu.SMEM)
VM = pl.BlockSpec(memory_space=pltpu.VMEM)


ANY = pl.BlockSpec(memory_space=pl.ANY)
HB = pl.BlockSpec(memory_space=pltpu.HBM)


def rim_shapes(rows, cols, levels):
    return [
        shape((2, rows - HALF_LAT, HALF_LON, levels, D)),
        shape((2, HALF_LAT, cols - HALF_LON, levels, D)),
        shape((2, HALF_LAT, HALF_LON, levels, D)),
    ]


def pack(tokens, cotangent):
    return pl.pallas_call(
        pack_kernel,
        name="pack",
        in_specs=[ANY] * 2,
        out_specs=[VM] * 3,
        out_shape=[local(rim.shape) for rim in rim_shapes(*tokens.shape[:3])],
        scratch_shapes=[pltpu.SemaphoreType.DMA((2, 3))],
    )(tokens, cotangent)


def place(output, grad, lon, lat, corner, after):
    return pl.pallas_call(
        place_kernel,
        name="place",
        in_specs=[ANY] * 2 + [VM] * 3 + [ANY],
        out_specs=[ANY] * 2,
        out_shape=[shape(output.shape), shape(grad.shape)],
        input_output_aliases={0: 0, 1: 1},
        scratch_shapes=[pltpu.SemaphoreType.DMA((2, 3))],
        cost_estimate=cost(10**9, 2**21),
    )(output, grad, lon, lat, corner, after)


WINDOWED = (BANDS, SIDES, WLAT, WLON, LEV, D)


def local(dims, dtype=BF16):
    return pltpu.VMEM(dims, dtype)


def held(*arrays):
    return [pltpu.with_memory_space_constraint(array, pltpu.VMEM) for array in arrays]


def far(*arrays):
    return [pltpu.with_memory_space_constraint(array, pltpu.HBM) for array in arrays]


def front(flag, tok, cot, lon, lat, corner, g1, wqkv, wout, g2):
    tokens = tok.size // D
    count = tokens // WIN
    saved = [(tokens, D), (tokens, D), (tokens, 3 * D), (count, D // HD, WIN, WIN), (tokens, D), (tokens, D)]
    return pl.pallas_call(
        front_kernel,
        name="front",
        in_specs=[SM] + [ANY] * 5 + [VM, HB, HB, VM],
        out_specs=[HB] * 7 + [VM] * 2,
        out_shape=[pltpu.HBM(dims, BF16) for dims in saved + [(tokens, D)]] + [local((tokens, D)), local((tokens, D))],
        scratch_shapes=[
            pltpu.VMEM(WINDOWED, BF16),
            pltpu.VMEM(WINDOWED, BF16),
        ] + [pltpu.VMEM(dims, BF16) for dims in saved] + [
            pltpu.VMEM((D, 3 * D), BF16),
            pltpu.VMEM((D, D), BF16),
            pltpu.SemaphoreType.DMA((2, STRIPS)),
            pltpu.SemaphoreType.DMA((SAVES + count,)),
            pltpu.SemaphoreType.DMA((2,)),
        ],
        compiler_params=params(),
        cost_estimate=cost(15 * 10**9, 10 * 2**20),
    )(flag, tok, cot, lon, lat, corner, g1, *far(wqkv, wout), g2)


def mlp(kind, me, n2, cot, wup, wdown, *carried):
    tokens = n2.shape[0]
    sums = [local((tokens, D), F32)] * 2
    scratch = [pltpu.VMEM((tokens, CHUNK), BF16)] * 2
    out_specs, aliases = [VM] * 3, {}
    if kind == "send":
        kernel, out_shape = send_kernel, sums + [shape((FF, D))]
    elif kind == "first":
        kernel, out_shape = keep_first_kernel, sums + [local((2 * CHUNK, D))]
        aliases = {5: 0, 6: 1}
    else:
        kernel, out_shape = keep_second_kernel, [pltpu.HBM((tokens, D), F32)] * 2 + [pltpu.HBM((FF, D), BF16)]
        out_specs = [HB, HB, VM]
        scratch = scratch + [pltpu.VMEM((tokens, D), F32)] * 2 + [pltpu.SemaphoreType.DMA((2,))]
    return pl.pallas_call(
        kernel,
        name="mlp_" + kind,
        in_specs=[SM, VM, VM, VM, VM] + [VM] * len(carried),
        out_specs=out_specs,
        out_shape=out_shape,
        scratch_shapes=scratch,
        input_output_aliases=aliases,
        compiler_params=params(),
        cost_estimate=cost((16 if kind == "send" else 8) * 10**9, 10 * 2**20),
    )(me, *held(n2, cot, wup, wdown, *carried))


def back(cot, mid, down, dn2, wout, qkv, p, att, n1, g2):
    tokens = cot.shape[0]
    count = tokens // WIN
    halves = pltpu.VMEM((tokens, D), BF16)
    full = pltpu.VMEM((tokens, D), F32)
    return pl.pallas_call(
        back_kernel,
        name="back",
        in_specs=[HB] * 9 + [VM],
        out_specs=[HB] * 3 + [VM] * 5,
        out_shape=[
            pltpu.HBM((tokens, D), BF16),
            pltpu.HBM((tokens, D), BF16),
            pltpu.HBM((tokens, 3 * D), BF16),
            shape((1, D), F32),
            local((tokens, D)),
            local((tokens, D)),
            local((tokens, D)),
            local((tokens, 3 * D)),
        ],
        scratch_shapes=[
            halves,
            halves,
            full,
            full,
            pltpu.VMEM((D, D), BF16),
            pltpu.VMEM((tokens, 3 * D), BF16),
            pltpu.VMEM((count, D // HD, WIN, WIN), BF16),
            halves,
            halves,
            pltpu.SemaphoreType.DMA((9,)),
            pltpu.SemaphoreType.DMA((3,)),
        ],
        compiler_params=params(40),
        cost_estimate=cost(25 * 10**9, 10 * 2**20),
    )(*far(cot, mid, down, dn2, wout, qkv, p, att, n1), g2)


def token_grads(dqkv, wqkv, x, dmid, res, g1, after, field):
    tokens = x.shape[0]
    halves = pltpu.VMEM((tokens, D), BF16)
    return pl.pallas_call(
        tokens_kernel,
        name="tokens",
        in_specs=[HB] * 5 + [VM, ANY],
        out_specs=[ANY] * 5 + [VM],
        out_shape=[shape(field), shape(field)] + rim_shapes(*field[:3]) + [shape((1, D), F32)],
        scratch_shapes=[
            pltpu.VMEM((tokens, 3 * D), BF16),
            pltpu.VMEM((D, 3 * D), BF16),
            halves,
            halves,
            halves,
            halves,
            pltpu.VMEM(WINDOWED, BF16),
            pltpu.VMEM(WINDOWED, BF16),
            pltpu.SemaphoreType.DMA((5,)),
            pltpu.SemaphoreType.DMA((2, STRIPS)),
        ],
        compiler_params=params(),
        cost_estimate=cost(6 * 10**9, 10 * 2**20),
    )(*far(dqkv, wqkv, x, dmid, res), g1, after)


def half_grads(name, half, n1, dqkv, att, dmid):
    return pl.pallas_call(
        half_kernel,
        name=name,
        in_specs=[SM] + [VM] * 4,
        out_specs=VM,
        out_shape=local((CHIPS_N, GRADS, 128)),
        compiler_params=params(),
        cost_estimate=cost(4 * 10**9, 4 * 2**20),
    )(half, *held(n1, dqkv, att, dmid))


def simple(kernel, name, out_shape, *operands, specs=None, scratch=(), mib=56):
    return pl.pallas_call(
        kernel,
        name=name,
        in_specs=specs or [VM] * len(operands),
        out_specs=VM if not scratch else HB,
        out_shape=out_shape,
        scratch_shapes=scratch,
        compiler_params=params(mib),
        cost_estimate=cost(10**9, 4 * 2**20),
    )(*operands)


def unpack(half, gathered, carried=None):
    mine = carried is None
    outs = [pltpu.HBM((D, FF), F32), pltpu.HBM((FF, D), F32), pltpu.HBM((D, 3 * D), F32), pltpu.HBM((D, D), F32)]
    gains = jnp.zeros((GAINS, 128), F32) if mine else carried[4]
    return pl.pallas_call(
        functools.partial(unpack_kernel, mine),
        name="unpack_mine" if mine else "unpack_theirs",
        in_specs=[SM, VM, VM] + ([] if mine else [HB] * 4),
        out_specs=[HB] * 4 + [VM],
        out_shape=outs + [shape((GAINS, 128), F32)],
        scratch_shapes=[
            pltpu.VMEM((D, FF // 2), F32),
            pltpu.VMEM((FF // 2, D), F32),
            pltpu.VMEM((4, D, HALF), F32),
            pltpu.SemaphoreType.DMA((6,)),
        ],
        input_output_aliases={} if mine else {3: 0, 4: 1, 5: 2, 6: 3},
        compiler_params=params(40),
        cost_estimate=cost(10**9, 10 * 2**20),
    )(half, gathered, gains, *([] if mine else far(*carried[:4])))


LAT = ("x", "zl")
LON = ("zh", "y", "c")
CHIPS = ("y", "x", "zh", "zl")


def send_rims(lon, lat, corner, distance):
    lats, lons = lax.axis_size(LAT), lax.axis_size(LON)
    moved = []
    for block, down, across in ((lon, 0, distance), (lat, distance, 0), (corner, distance, distance)):
        route = [
            (i * lons + j, (i + down) % lats * lons + (j + across) % lons)
            for i in range(lats) for j in range(lons)
        ]
        moved.append(lax.ppermute(block, LAT + LON, route))
    return moved


def other_core(block):
    return lax.ppermute(block, "c", [(0, 1), (1, 0)])


def exchange(parts):
    return lax.all_to_all(parts, CHIPS, 0, 0, tiled=True)


def shards(tokens, cotangent, norm_gain, w_qkv, w_out, mlp_gain, w_up, w_down):
    g1 = norm_gain.reshape(1, D)
    g2 = mlp_gain.reshape(1, D)
    last_band = lax.axis_index(LAT) == lax.axis_size(LAT) - 1
    flag = last_band.astype(jnp.int32).reshape(1)
    me = lax.axis_index("c").astype(jnp.int32).reshape(1)

    rims = send_rims(*pack(tokens, cotangent), -1)
    x, n1, qkv, p, att, mid, cot_far, cot, n2 = front(flag, tokens, cotangent, *rims, g1, w_qkv, w_out, g2)
    fixed = (me, n2, cot, w_up, w_down)
    down, dn2, grads = mlp("send", *fixed)
    got = other_core(grads)
    down, dn2, early = mlp("first", *fixed, down, dn2)
    down, dn2, grads = mlp("second", *fixed, down, dn2, early, got)
    sums = exchange(grads.reshape(CHIPS_N, SHARE, D))
    res, dmid_far, dqkv_far, dg2, att, n1, dmid, dqkv = back(cot_far, mid, down, dn2, w_out, qkv, p, att, n1, g2)
    got = other_core(half_grads("send", 1 - me, n1, dqkv, att, dmid))
    keep = half_grads("keep", me, n1, dqkv, att, dmid)
    added = simple(add_kernel, "add", pltpu.HBM((CHIPS_N, GRADS, 128), BF16), *held(keep, got), mib=32)
    att_sums = exchange(added)
    tile = simple(share_mlp_kernel, "share_mlp", shape((MLP, 128)), sums, added, specs=[VM, ANY])
    output, grad_tokens, lon, lat, corner, dg1 = token_grads(
        dqkv_far, w_qkv, x, dmid_far, res, g1, added, tokens.shape)
    att_sums, tile, dg1 = lax.optimization_barrier((att_sums, tile, dg1))
    rims = send_rims(lon, lat, corner, 1)
    shares = simple(
        share_kernel, "share", pltpu.HBM((CHIPS_N, ALL, 128), BF16), *held(att_sums), tile, dg1, dg2, mib=32,
        scratch=[pltpu.VMEM((ALL, 128), BF16), pltpu.SemaphoreType.DMA((CHIPS_N,))])
    gathered = exchange(shares)
    theirs = other_core(gathered)
    grads = unpack(1 - me, theirs, unpack(me, gathered))
    output, grad_tokens = place(output, grad_tokens, *rims, grads[4])
    gup, gdown, gqkv, gout, gains = grads
    gains = gains.reshape(2, D)
    return (output, grad_tokens, gains[0], gqkv, gout, gains[1], gup, gdown)


def solution(mesh):
    field = P(LAT, LON, None, None)
    mesh = jax.sharding.Mesh(mesh.devices.reshape(4, 2, 2, 4, 2), ("x", "zl", "zh", "y", "c"))
    return jax.shard_map(
        shards,
        mesh=mesh,
        in_specs=(field, field, P(), P(), P(), P(), P(), P()),
        out_specs=(field, field, P(), P(), P(), P(), P(), P()),
        check_vma=False,
    )
```
